128 devices in a mesh: vol: 32 (over x, z, core), mem: 4 (over y).
Axes of the slice: x: 4, y: 4, z: 4, core: 2. Of those that a mesh axis runs over, the one named last changes fastest.
Arguments:
- potential: float32 [128, 256, 1024], P('vol', 'mem'), may hold values from -6 to 6
- conductivity: float32 [128, 256, 1024], P('vol', 'mem'), may hold values from 0.1 to 4
- ion_states: float32 [40, 2097152], P(None, ('vol', 'mem')), may hold values from 0 to 1
- rate_scale: float32 [2, 40], replicated, may hold values from 0.05 to 2
- rate_slope: float32 [2, 40], replicated, may hold values from -1 to 1
- type_cond: float32 [3, 40], replicated, may hold values from 0.005 to 0.05
- reversal: float32 [40], replicated, may hold values from -2 to 2
- facet_counts: int32 [8192], P(('vol', 'mem')), may hold values from 0 to 256, as said below
- intra_voxel: int32 [2097152], P(('vol', 'mem')), may hold values from 0 to 262143, as said below
- extra_voxel: int32 [2097152], P(('vol', 'mem')), may hold values from 0 to 262143, as said below
- cell_type: int32 [8192], P(('vol', 'mem')), may hold values from 0 to 2
- gap_partner: int32 [8192, 8], P(('vol', 'mem')), may hold values from 0 to 8191, as said below
- gap_cond: float32 [8192, 8], P(('vol', 'mem')), may hold values from 0.2 to 2
Outputs:
- potential_next: float32 [128, 256, 1024], P('vol', 'mem')
- states_next: float32 [40, 2097152], P(None, ('vol', 'mem'))
- membrane_current: float32 [2097152], P(('vol', 'mem'))
The draws below stay inside these ranges and needn't reach their ends.
Inputs may be any that keep to these rules, and one draw needn't show every extreme that they name: `facet_counts`: within each brick's 64 cell slots, the cells with a positive count come first; a used cell has 64 to 256 facets; some brick has all its cells used and some cell uses all 256 slots. `intra_voxel`: local index x * 64 * 1024 + y * 1024 + z within the brick that holds the facet; the facets of the cell in slot s of its brick lie in local indices s * R to s * R + R - 1, with R = 4096. `extra_voxel`: local index x * 64 * 1024 + y * 1024 + z within the brick that holds the facet; the facets of the cell in slot s of its brick lie in local indices s * R to s * R + R - 1, with R = 4096. `gap_partner`: each partner is a cell with a positive count, in a brick whose first brick index differs from its own cell's by at most one.
All inputs are finite; a program needn't handle non-finite values.
Results may differ from the reference program's by a relative error of at most 0.0003.
Values sent between devices are 32-bit elements; how exact they have to be, the bound alone decides.
No kernel may reach another device: no remote copies, remote signals or barrier semaphores. Data moves between devices by JAX's collectives and lax.ppermute only.
A program may use at most 64 MiB of HBM per device.

```python
import math
import jax
import jax.numpy as jnp
from jax import lax

CX = 4
CY = 64
CZ = 1024
CELL_DEV = 64
FPC = 256
NSTATES = 40
NTYPES = 3
JPC = 8
ITERS = 4
BRICKS_X = 32
BRICKS_Y = 4
NX = 128
NY = 256
NZ = 1024
CELLS = 8192
FACETS = 2097152


def used_cells(key):
    first, second = jax.random.split(jax.random.fold_in(key, 11))
    bricks = BRICKS_X * BRICKS_Y
    occupied = jax.random.randint(first, (bricks,), max(1, CELL_DEV // 4), CELL_DEV + 1)
    fullest = jax.random.randint(second, (), 0, bricks)
    occupied = occupied.at[fullest].set(CELL_DEV)
    return (occupied.astype(jnp.int32), fullest)


def draw_facet_counts(key, part):
    occupied, fullest = used_cells(key)
    counts = jax.random.randint(jax.random.fold_in(key, 23), (CELLS,), max(1, FPC // 4), FPC + 1)
    cells = jnp.arange(CELLS, dtype=jnp.int32)
    counts = jnp.where(cells % CELL_DEV < occupied[cells // CELL_DEV], counts, 0)
    counts = counts.at[fullest * CELL_DEV].set(FPC)
    return counts.astype(jnp.int32)


def facet_voxels(key, salt):
    region = CX * CY * CZ // CELL_DEV
    facets = jnp.arange(FACETS, dtype=jnp.int32)
    slot = facets // FPC % CELL_DEV
    inner = jax.random.randint(jax.random.fold_in(key, salt), (FACETS,), 0, region)
    local = slot * region + inner
    local = local.at[0].set(0)
    local = local.at[FACETS - 1].set(CX * CY * CZ - 1)
    return local.astype(jnp.int32)


def draw_intra_voxel(key, part):
    return facet_voxels(key, 51)


def draw_extra_voxel(key, part):
    return facet_voxels(key, 53)


def draw_gap_partner(key, part):
    occupied, fullest = used_cells(key)
    keys = jax.random.split(jax.random.fold_in(key, 37), 3)
    cells = jnp.arange(CELLS, dtype=jnp.int32)
    brick_x = cells // CELL_DEV // BRICKS_Y
    offset = jax.random.randint(keys[0], (CELLS, JPC), -1, 2)
    other_x = jnp.clip(brick_x[:, None] + offset, 0, BRICKS_X - 1)
    other_y = jax.random.randint(keys[1], (CELLS, JPC), 0, BRICKS_Y)
    other_brick = other_x * BRICKS_Y + other_y
    other_slot = jax.random.randint(keys[2], (CELLS, JPC), 0, 1 << 20) % occupied[other_brick]
    return (other_brick * CELL_DEV + other_slot).astype(jnp.int32)


def plant(drawn, stream_key, smallest, high):
    longest = drawn.shape.index(max(drawn.shape))
    spots = []
    for shift in (0, 1):
        where = [jax.random.randint(jax.random.fold_in(stream_key, axis), (), 0, length) for axis, length in enumerate(drawn.shape)]
        where[longest] = (where[longest] + shift) % drawn.shape[longest]
        spots.append(tuple(where))
    return drawn.at[spots[0]].set(smallest).at[spots[1]].set(high)


def steps_of(stream_key, shape, cuts, low, high):
    def one(dim, shards_of):
        heights = jax.random.uniform(jax.random.fold_in(jax.random.fold_in(stream_key, 6), dim), (shards_of,), jnp.float32, low / len(cuts), high / len(cuts))
        return jnp.repeat(jnp.exp(heights), shape[dim] // shards_of).reshape((-1,) + (1,) * (len(shape) - dim - 1))

    factor_of = one(*cuts[0])
    for cut in cuts[1:]:
        factor_of = factor_of * one(*cut)
    return factor_of


def bell_draw(own_key, extent, scale, limit, cuts=(), kind=jnp.bfloat16):
    loudness = steps_of(own_key, extent, cuts, -0.22, 0.18) if cuts else 1.0
    entries = jax.random.normal(own_key, extent, jnp.float32) * scale * loudness
    return jnp.minimum(jnp.maximum(entries, -limit), limit).astype(kind)


def setup_inputs(seed: int = 0) -> dict:
    key_list = jax.random.split(jax.random.key(seed), 14)
    return {
        "potential": bell_draw(key_list[0], (NX, NY, NZ), 1.0, 6.0, ((0, 32), (1, 4)), jnp.float32),
        "conductivity": jnp.clip(jnp.exp(math.log(4.0) - 3.6888794 * jax.random.uniform(key_list[1], (NX, NY, NZ), jnp.float32) ** steps_of(key_list[1], (NX, NY, NZ), ((0, 32), (1, 4)), -0.2, 0.2)), 0.1, 4.0),
        "ion_states": jnp.clip(1.0 * jax.random.uniform(key_list[2], (NSTATES, FACETS), jnp.float32) ** steps_of(key_list[2], (NSTATES, FACETS), ((1, 128),), -0.2, 0.2), 0.0, 1.0),
        "rate_scale": jnp.clip(jnp.exp(jax.random.uniform(key_list[3], (2, NSTATES), jnp.float32, math.log(0.05), math.log(2.0))), 0.05, 2.0),
        "rate_slope": jnp.clip(jax.random.uniform(key_list[4], (2, NSTATES), jnp.float32, -1.0, 1.0), -1.0, 1.0),
        "type_cond": jnp.clip(jnp.exp(jax.random.uniform(key_list[5], (NTYPES, NSTATES), jnp.float32, math.log(0.005), math.log(0.05))), 0.005, 0.05),
        "reversal": jnp.clip(jax.random.uniform(key_list[6], (NSTATES,), jnp.float32, -2.0, 2.0), -2.0, 2.0),
        "facet_counts": draw_facet_counts(jax.random.fold_in(key_list[13], 71), 0),
        "intra_voxel": draw_intra_voxel(jax.random.fold_in(key_list[13], 71), 0),
        "extra_voxel": draw_extra_voxel(jax.random.fold_in(key_list[13], 71), 0),
        "cell_type": plant(jax.random.randint(key_list[10], (CELLS,), 0, NTYPES), jax.random.fold_in(key_list[10], 1), 0, NTYPES - 1).astype(jnp.int32),
        "gap_partner": draw_gap_partner(jax.random.fold_in(key_list[13], 71), 0),
        "gap_cond": jnp.clip(jnp.exp(math.log(2.0) - 2.3025851 * jax.random.uniform(key_list[12], (CELLS, JPC), jnp.float32) ** steps_of(key_list[12], (CELLS, JPC), ((0, 128),), -0.2, 0.2)), 0.2, 2.0),
    }


mass_coef = 1.0
time_step = 0.5
low_eig = 0.2
high_eig = 1.8


def neighbour_views(extended):
    padded = jnp.pad(extended, ((0, 0), (0, 0), (1, 1)))
    centre = padded[1:-1, 1:-1, 1:-1]
    views = (padded[:-2, 1:-1, 1:-1], padded[2:, 1:-1, 1:-1], padded[1:-1, :-2, 1:-1],
             padded[1:-1, 2:, 1:-1], padded[1:-1, 1:-1, :-2], padded[1:-1, 1:-1, 2:])
    return centre, views


def face_coeffs(cond_ext):
    centre, views = neighbour_views(cond_ext)
    coeffs = tuple(0.5 * (centre + other) for other in views)
    diagonal = mass_coef + time_step * (coeffs[0] + coeffs[1] + coeffs[2] + coeffs[3] + coeffs[4] + coeffs[5])
    return coeffs, diagonal


def operator_apply(field_ext, coeffs, diagonal):
    centre, views = neighbour_views(field_ext)
    total = coeffs[0] * views[0]
    for number in range(1, 6):
        total = total + coeffs[number] * views[number]
    return diagonal * centre - time_step * total


def chebyshev(apply_fn, rhs_field, start, diagonal, inside):
    theta = 0.5 * (high_eig + low_eig)
    delta = 0.5 * (high_eig - low_eig)
    sigma_one = theta / delta
    cheb_rho = 1.0 / sigma_one
    iterate = start
    resid = inside * (rhs_field - apply_fn(iterate)) / diagonal
    update = resid / theta
    for sweep in range(ITERS):
        iterate = iterate + update
        if sweep + 1 < ITERS:
            resid = inside * (rhs_field - apply_fn(iterate)) / diagonal
            rho_next = 1.0 / (2.0 * sigma_one - cheb_rho)
            update = rho_next * cheb_rho * update + (2.0 * rho_next / delta) * resid
            cheb_rho = rho_next
    return iterate


def ionic_update(states, voltage, type_flat, rate_scale, rate_slope, type_cond, reversal):
    opening = rate_scale[0][:, None] * jnp.exp(rate_slope[0][:, None] * voltage[None, :])
    closing = rate_scale[1][:, None] * jnp.exp(-rate_slope[1][:, None] * voltage[None, :])
    total = opening + closing
    steady = opening / total
    fresh = steady + (states - steady) * jnp.exp(-time_step * total)
    weighted = jnp.dot(type_cond, fresh, precision=lax.Precision.HIGHEST)
    offsets = jnp.dot(type_cond * reversal[None, :], fresh, precision=lax.Precision.HIGHEST)
    kinds = jnp.arange(type_cond.shape[0], dtype=jnp.int32)
    onehot = (type_flat[None, :] == kinds[:, None]).astype(fresh.dtype)
    ion_current = jnp.sum(onehot * (weighted * voltage[None, :] - offsets), axis=0)
    return fresh, ion_current


def reference(potential, conductivity, ion_states, rate_scale, rate_slope, type_cond, reversal, facet_counts, intra_voxel, extra_voxel, cell_type, gap_partner, gap_cond):
    bricks = BRICKS_X * BRICKS_Y
    facets_dev = CELL_DEV * FPC
    positions = jnp.arange(FACETS, dtype=jnp.int32)
    owner = positions // facets_dev
    brick_x = owner // BRICKS_Y
    brick_y = owner % BRICKS_Y

    def to_global(local):
        loc_x = local // (CY * CZ)
        loc_y = (local // CZ) % CY
        loc_z = local % CZ
        return (((brick_x * CX + loc_x) * NY + brick_y * CY + loc_y) * NZ + loc_z).astype(jnp.int32)

    global_in = to_global(intra_voxel)
    global_ex = to_global(extra_voxel)
    flat_field = potential.reshape(-1)
    voltage = flat_field[global_in] - flat_field[global_ex]
    active = (jnp.arange(FPC, dtype=jnp.int32)[None, :] < facet_counts[:, None]).reshape(-1)
    divisor = jnp.maximum(facet_counts, 1).astype(potential.dtype)
    cell_volt = jnp.sum(jnp.where(active, voltage, 0.0).reshape(CELLS, FPC), axis=1) / divisor
    partner_volt = cell_volt[gap_partner]
    gap_current = jnp.sum(gap_cond * (cell_volt[:, None] - partner_volt), axis=1)
    gap_facet = jnp.repeat(gap_current / divisor, FPC)
    type_flat = jnp.repeat(cell_type, FPC)

    states_blocks = jnp.transpose(ion_states.reshape(NSTATES, bricks, facets_dev), (1, 0, 2))

    def per_block(items):
        return ionic_update(items[0], items[1], items[2], rate_scale, rate_slope, type_cond, reversal)

    fresh_blocks, current_blocks = lax.map(per_block, (states_blocks, voltage.reshape(bricks, facets_dev), type_flat.reshape(bricks, facets_dev)))
    fresh = jnp.transpose(fresh_blocks, (1, 0, 2)).reshape(NSTATES, FACETS)
    ion_current = current_blocks.reshape(FACETS)
    states_next = jnp.where(active[None, :], fresh, ion_states)
    membrane_current = jnp.where(active, ion_current + gap_facet, 0.0)

    source = jnp.zeros_like(flat_field).at[global_in].add(membrane_current).at[global_ex].add(-membrane_current)
    rhs_field = mass_coef * potential - time_step * source.reshape(potential.shape)

    def border(field):
        return jnp.pad(field, ((1, 1), (1, 1), (0, 0)))

    coeffs, diagonal = face_coeffs(border(conductivity))

    def apply_operator(field):
        return operator_apply(border(field), coeffs, diagonal)

    potential_next = chebyshev(apply_operator, rhs_field, potential, diagonal, 1.0)
    return potential_next, states_next, membrane_current
```

```python
import functools
import math

import jax
import jax.numpy as jnp
from jax import lax
from jax.experimental import pallas as pl
from jax.experimental.pallas import tpu as pltpu
from jax.sharding import PartitionSpec as P

LOG2E = math.log2(math.e)
SWEEPS = 4
F32 = jnp.float32
BF16 = jnp.bfloat16
ANY = pl.BlockSpec(memory_space=pl.ANY)
VM = pl.BlockSpec(memory_space=pltpu.VMEM)
SM = pl.BlockSpec(memory_space=pltpu.SMEM)
BIG = pltpu.CompilerParams(vmem_limit_bytes=48 * 1024 * 1024)


def sweep_factors():
    theta, delta = 1.0, 0.8
    sigma = theta / delta
    rho = 1.0 / sigma
    factors = []
    for _ in range(SWEEPS - 1):
        rho_next = 1.0 / (2.0 * sigma - rho)
        factors.append((rho_next * rho, 2.0 * rho_next / delta))
        rho = rho_next
    return factors


def iota(shape, dim):
    return lax.broadcasted_iota(jnp.int32, shape, dim)


def plane_of(parity, j):
    return j + parity * (3 - 2 * j)


def gather_kernel(p_ref, in_ref, ex_ref, cnt_ref, volt_ref, cell_ref):
    sub = iota((8, 128), 0)
    low = sub < 4

    def body(kk, carry):
        x = kk // 4
        blocks = [r[pl.ds(pl.multiple_of(8 * kk, 8), 8), :] & 4095 for r in (in_ref, ex_ref)]
        for q in range(2):
            row = pl.multiple_of((2 * (kk % 4) + q) * 8, 8)
            tiles = [p_ref[x, pl.ds(row, 8), 128 * z : 128 * z + 128] for z in range(8)]
            for h in range(2):
                picked = []
                for block in blocks:
                    a = jnp.broadcast_to(block[4 * q + h : 4 * q + h + 1], (8, 128))
                    b = jnp.broadcast_to(block[4 * q + 2 + h : 4 * q + 3 + h], (8, 128))
                    o = jnp.where(low, a, b)
                    lane = o & 127
                    z_of = (o >> 7) & 7
                    got = jnp.take_along_axis(tiles[0], lane, axis=1, mode="promise_in_bounds")
                    for z in range(1, 8):
                        new = jnp.take_along_axis(tiles[z], lane, axis=1, mode="promise_in_bounds")
                        got = jnp.where(z_of == z, new, got)
                    picked.append(jnp.where((o >> 10) == (sub & 3), got, 0.0))
                d = picked[0] - picked[1]
                d = d + pltpu.roll(d, 7, 0)
                d = d + pltpu.roll(d, 6, 0)
                volt_ref[pl.ds(8 * kk + 4 * q + h, 1), :] = d[0:1]
                volt_ref[pl.ds(8 * kk + 4 * q + 2 + h, 1), :] = d[4:5]
        return carry

    lax.fori_loop(0, 16, body, 0)
    turned = jnp.transpose(volt_ref[...])
    cnt = cnt_ref[...]
    lanes = iota((128, 128), 1)
    used = iota((128, 128), 0) + 128 * (lanes & 1) < cnt
    total = jnp.sum(jnp.where(used, turned, 0.0), axis=0, keepdims=True)
    even = (iota((1, 128), 1) & 1) == 0
    other = jnp.where(even, pltpu.roll(total, 127, 1), pltpu.roll(total, 1, 1))
    cell_ref[...] = (total + other) / jnp.maximum(cnt, 1).astype(F32)


def pack_kernel(meta, p_ref, c_ref, a_ref, b_ref, up_ref, down_ref, sem):
    par = meta[0]
    copies = []
    for i in range(3):
        copies.append((c_ref.at[plane_of(par, 3 - i)], a_ref.at[i]))
        copies.append((c_ref.at[plane_of(par, i)], b_ref.at[i]))
    copies.append((p_ref.at[plane_of(par, 3)], a_ref.at[3]))
    copies.append((p_ref.at[plane_of(par, 0)], b_ref.at[3]))
    for k, ref in enumerate((c_ref, p_ref)):
        copies.append((ref.at[:, 56:64], up_ref.at[4 * k : 4 * k + 4]))
        copies.append((ref.at[:, 0:8], down_ref.at[4 * k : 4 * k + 4]))
    run_copies(copies, sem)


def run_copies(copies, sem, start=0):
    made = [pltpu.make_async_copy(s, d, sem.at[start + n]) for n, (s, d) in enumerate(copies)]
    for m in made:
        m.start()
    for m in made:
        m.wait()


def ionic_kernel(cnt, typ, volt_ref, st_ref, rate_ref, g_ref, gr_ref, out_ref, ion_ref, act_ref):
    step = pl.program_id(0)
    cells = volt_ref.shape[0] // 2
    lane = iota((8, 128), 1)

    def body(cc, carry):
        n = cnt[step * cells + cc]
        ty = typ[step * cells + cc]
        for h in range(2):
            r = cc * 2 + h
            cols = pl.ds(pl.multiple_of(r * 128, 128), 128)
            v = jnp.broadcast_to(volt_ref[pl.ds(r, 1), :], (8, 128))
            active = lane + h * 128 < n
            w1 = w2 = None
            for k in range(5):
                rows = slice(8 * k, 8 * k + 8)
                st = st_ref[rows, cols]
                opening = jnp.exp2(rate_ref[0, rows] * v + rate_ref[1, rows])
                closing = jnp.exp2(rate_ref[2, rows] * v + rate_ref[3, rows])
                total = opening + closing
                rec = pl.reciprocal(total, approx=True)
                rec = rec * (2.0 - total * rec)
                steady = opening * rec
                fresh = steady + (st - steady) * jnp.exp2(total * (-0.5 * LOG2E))
                out_ref[rows, cols] = jnp.where(active, fresh, st)
                a = g_ref[ty, rows] * fresh
                b = gr_ref[ty, rows] * fresh
                w1 = a if w1 is None else w1 + a
                w2 = b if w2 is None else w2 + b
            ion = jnp.sum(w1 * v - w2, axis=0, keepdims=True)
            ion_ref[pl.ds(r, 1), :] = jnp.where(active[0:1], ion, 0.0)
            act_ref[pl.ds(r, 1), :] = jnp.where(active[0:1], 1.0, 0.0)
        return carry

    lax.fori_loop(0, cells, body, 0)


def scatter_kernel(ion_ref, act_ref, in_ref, ex_ref, s_ref, n_ref):
    row_iota = iota((32, 512), 0)
    lane_iota = iota((128, 512), 0)
    low = iota((8, 128), 0) < 4
    odd_row = (iota((8, 128), 0) & 2) // 2

    def body(kk, carry):
        rows8 = pl.ds(pl.multiple_of(8 * kk, 8), 8)
        x = kk // 4
        val = ion_ref[rows8, :]
        act = act_ref[rows8, :]
        hi = val.astype(BF16).astype(F32)
        lo = val - hi
        mids, lanes = [], []
        for ref in (in_ref, ex_ref):
            o = ref[rows8, :] & 4095
            mids.append((((o >> 7) & 7) ^ odd_row) * 4 + (o >> 10))
            lanes.append(o & 127)

        def line(a, b, s):
            r = 2 * s
            return jnp.concatenate([a[r : r + 1], a[r + 1 : r + 2], b[r : r + 1], b[r + 1 : r + 2]], axis=1)

        for q in range(2):
            results = []
            for s in (2 * q, 2 * q + 1):
                hit = line(mids[0], mids[1], s) == row_iota
                left = jnp.concatenate(
                    [jnp.where(hit, line(piece, -piece, s), 0.0).astype(BF16) for piece in (hi, lo, act)], axis=0
                )
                right = jnp.where(line(lanes[0], lanes[1], s) == lane_iota, 1.0, 0.0).astype(BF16)
                out = lax.dot_general(left, right, (((1,), (1,)), ((), ())), preferred_element_type=F32)
                results.append((out[0:32] + out[32:64], out[64:96]))
            row = pl.ds(pl.multiple_of((2 * (kk % 4) + q) * 8, 8), 8)
            for dst, e, o in ((s_ref, results[0][0], results[1][0]), (n_ref, results[0][1], results[1][1])):
                for j in range(4):
                    ej, oj = e[8 * j : 8 * j + 8], o[8 * j : 8 * j + 8]
                    dst[x, row, 256 * j : 256 * j + 128] = jnp.where(low, ej, oj)
                    dst[x, row, 256 * j + 128 : 256 * j + 256] = pltpu.roll(jnp.where(low, oj, ej), 4, 0)
        return carry

    lax.fori_loop(0, 16, body, 0)


def tile(ref, e, t):
    return ref[e, 8 * t : 8 * t + 8, :]


class Around:
    def __init__(self, ref, e):
        self.ref, self.e = ref, e
        self.sub = iota((8, 1024), 0)

    def at(self, t):
        ref, e = self.ref, self.e
        c = tile(ref, e, t)
        before, after = tile(ref, e, (t + 8) % 9), tile(ref, e, (t + 1) % 9)
        ym = jnp.where(self.sub == 0, pltpu.roll(before, 1, 0), pltpu.roll(c, 1, 0))
        yp = jnp.where(self.sub == 7, pltpu.roll(after, 7, 0), pltpu.roll(c, 7, 0))
        zm, zp = pltpu.roll(c, 1, 1), pltpu.roll(c, 1023, 1)
        return c, tile(ref, e - 1, t), tile(ref, e + 1, t), ym, yp, zm, zp


def couplings(around, t):
    lane = iota((8, 1024), 1)
    c, xm, xp, ym, yp, zm, zp = around.at(t)
    first, last = lane == 0, lane == 1023
    zm = jnp.where(first, 0.0, zm)
    zp = jnp.where(last, 0.0, zp)
    fs = [0.25 * (c + other) for other in (xm, xp, ym, yp, zm, zp)]
    diagonal = 1.0 + (((fs[0] + fs[1]) + (fs[2] + fs[3])) + (fs[4] + fs[5]))
    fs[4] = jnp.where(first, 0.0, fs[4])
    fs[5] = jnp.where(last, 0.0, fs[5])
    return fs, diagonal


def weighted(fs, views):
    t = [f * v for f, v in zip(fs, views)]
    return ((t[0] + t[1]) + (t[2] + t[3])) + (t[4] + t[5])


def start_kernel(meta, p_hbm, c_hbm, a_hbm, b_hbm, y_hbm, s_ref, n_ref, w_ref, k_ref, pe, ce, sem):
    par = meta[0]
    copies = []
    for e, hbm, yk in ((ce, c_hbm, 0), (pe, p_hbm, 4)):
        for j in range(4):
            copies.append((hbm.at[plane_of(par, j)], e.at[1 + j, 0:64]))
            copies.append((y_hbm.at[yk + plane_of(par, j)], e.at[1 + j, 64:72]))
    copies.append((a_hbm.at[0], ce.at[5, 0:64]))
    copies.append((b_hbm.at[0], ce.at[0, 0:64]))
    copies.append((a_hbm.at[3], pe.at[5, 0:64]))
    copies.append((b_hbm.at[3], pe.at[0, 0:64]))
    run_copies(copies, sem)

    def body(j, carry):
        x = plane_of(par, j)
        ca, pa = Around(ce, 1 + j), Around(pe, 1 + j)
        for t in range(8):
            rows = slice(8 * t, 8 * t + 8)
            fs, diagonal = couplings(ca, t)
            inv = 1.0 / diagonal
            views = pa.at(t)
            p = views[0]
            w_ref[x, rows, :] = (p + weighted(fs, views[1:]) - 0.5 * s_ref[x, rows, :]) * inv - p
            k_ref[x, rows, :] = (-0.5 * inv) * n_ref[x, rows, :]
        return carry

    lax.fori_loop(0, 4, body, 0)


def gap_kernel(meta, table_ref, part_ref, cond_ref, cnt_ref, ion_ref, act_ref, w_ref, k_ref,
               u_ref, a_ref, b_ref, up_ref, down_ref, mem_ref, spread):
    par, mine, v = meta[0], meta[2], meta[3]
    part = part_ref[...]
    brick = part >> 6
    bx, by = brick >> 2, brick & 3
    side = jnp.where(bx == v, 0, jnp.where(bx == (v ^ 1), 1, 2))
    row = side * 4 + ((mine - by) & 3)
    lane = (part & 63) * 2
    other = jnp.zeros((8, 128), F32)
    for r in range(12):
        line = jnp.broadcast_to(table_ref[r : r + 1, :], (8, 128))
        other = jnp.where(row == r, jnp.take_along_axis(line, lane, axis=1, mode="promise_in_bounds"), other)
    own = table_ref[0:1, :]
    current = jnp.sum(cond_ref[...] * (own - other), axis=0, keepdims=True)
    g = current / jnp.maximum(cnt_ref[...], 1).astype(F32)
    g8 = jnp.broadcast_to(g, (8, 128))
    mem_ref[...] = ion_ref[...] + act_ref[...] * jnp.transpose(jnp.broadcast_to(g, (128, 128)))
    for half in range(2):
        at = 64 * half + 2 * (iota((8, 128), 1) // 4)
        wide = jnp.take_along_axis(g8, at, axis=1, mode="promise_in_bounds")[0:1]
        spread[128 * half : 128 * half + 128, :] = jnp.transpose(jnp.broadcast_to(wide, (128, 128)))

    def body(j, carry):
        x = plane_of(par, j)
        for t in range(8):
            rows = slice(8 * t, 8 * t + 8)
            gt = spread[pl.ds(pl.multiple_of(x * 64 + 8 * t, 8), 8), :]
            u = w_ref[x, rows, :] + k_ref[x, rows, :] * jnp.tile(gt, (1, 8))
            u_ref[x, rows, :] = u
            if t == 0:
                down_ref[x] = u
            if t == 7:
                up_ref[x] = u

            @pl.when(j < 3)
            def _():
                b_ref[j, rows, :] = u

            @pl.when(j > 0)
            def _():
                a_ref[3 - j, rows, :] = u

        return carry

    lax.fori_loop(0, 4, body, 0)


def sweep_kernel(meta, p_ref, c_hbm, ca_hbm, cb_hbm, cy_hbm, cca_hbm, ccb_hbm,
                 u_hbm, ua_hbm, ub_hbm, uy_hbm, uca_hbm, ucb_hbm, out_ref,
                 c, u0, u1, u2, r, fx, fym, fyp, fzm, fzp, inv, sem):
    par, has_b, mine = meta[0], meta[1], meta[2]

    def loads(dst, own, a, b, y, ca, cb, start):
        copies = []
        for j in range(4):
            copies.append((own.at[plane_of(par, j)], dst.at[3 + j, 0:64]))
            copies.append((y.at[plane_of(par, j)], dst.at[3 + j, 64:72]))
        for i in range(3):
            copies.append((a.at[i], dst.at[7 + i, 0:64]))
            copies.append((b.at[i], dst.at[2 - i, 0:64]))
        for i in range(2):
            copies.append((ca.at[i], dst.at[7 + i, 64:72]))
            copies.append((cb.at[i], dst.at[2 - i, 64:72]))
        made = [pltpu.make_async_copy(s, d, sem.at[start + n]) for n, (s, d) in enumerate(copies)]
        for m in made:
            m.start()
        return made

    c_copies = loads(c, c_hbm, ca_hbm, cb_hbm, cy_hbm, cca_hbm, ccb_hbm, 0)
    u_copies = loads(u0, u_hbm, ua_hbm, ub_hbm, uy_hbm, uca_hbm, ucb_hbm, len(c_copies))
    zero8 = jnp.zeros((8, 1024), F32)
    for dst in (c, u0):
        dst[0, 64:72, :] = zero8
        dst[9, 64:72, :] = zero8
    sub = iota((8, 1024), 0)
    bottom = (sub < 3) & (mine != 3)
    top = (sub >= 5) & (mine != 0)
    keep = jnp.where(bottom | top, 1.0, 0.0)
    for m in c_copies:
        m.wait()

    def build(e, carry):
        around = Around(c, e)
        inside = jnp.where((e >= 3) | (has_b == 1), 1.0, 0.0)
        for t in range(9):
            rows = slice(8 * t, 8 * t + 8)
            fs, diagonal = couplings(around, t)
            part = inside / diagonal
            inv[e, rows, :] = part * keep if t == 8 else part
            fx[e - 1, rows, :] = fs[0]
            fx[e, rows, :] = fs[1]
            fym[e, rows, :] = fs[2]
            fyp[e, rows, :] = fs[3]
            fzm[e, rows, :] = fs[4]
            fzp[e, rows, :] = fs[5]
        return carry

    lax.fori_loop(1, 9, build, 0)
    for m in u_copies:
        m.wait()
    (a1, b1), (a2, b2), (a3, b3) = sweep_factors()

    def coupled(around, e, t):
        fs = [tile(fx, e - 1, t), tile(fx, e, t)] + [tile(f, e, t) for f in (fym, fyp, fzm, fzp)]
        views = around.at(t)
        return views[0], tile(inv, e, t) * weighted(fs, views[1:])

    def first(e, carry):
        around = Around(u0, e)
        for t in range(9):
            rows = slice(8 * t, 8 * t + 8)
            u, res = coupled(around, e, t)
            r[e, rows, :] = res
            u1[e, rows, :] = a1 * u + b1 * res
        return carry

    lax.fori_loop(1, 9, first, 0)

    def second(e, carry):
        around = Around(u1, e)
        for t in range(9):
            rows = slice(8 * t, 8 * t + 8)
            u, more = coupled(around, e, t)
            res = (tile(r, e, t) - u) + more
            r[e, rows, :] = res
            u2[e, rows, :] = a2 * u + b2 * res
        return carry

    lax.fori_loop(2, 8, second, 0)

    def third(j, carry):
        e = 3 + j
        x = plane_of(par, j)
        around = Around(u2, e)
        for t in range(8):
            rows = slice(8 * t, 8 * t + 8)
            u, more = coupled(around, e, t)
            res = (tile(r, e, t) - u) + more
            before = (p_ref[x, rows, :] + tile(u0, e, t)) + (tile(u1, e, t) + u)
            out_ref[x, rows, :] = before + (a3 * u + b3 * res)
        return carry

    lax.fori_loop(0, 4, third, 0)


def shape(*dims, kind=F32):
    return jax.ShapeDtypeStruct(dims, kind)


def per_device(potential, conductivity, ion_states, rate_scale, rate_slope, type_cond, reversal,
               facet_counts, intra_voxel, extra_voxel, cell_type, gap_partner, gap_cond):
    v, m = lax.axis_index("vol"), lax.axis_index("mem")
    par = v & 1
    nv = lax.axis_size("vol")
    has_b = jnp.where((v == 0) | (v == nv - 1), 0, 1)
    meta = jnp.stack([par, has_b, m, v]).astype(jnp.int32)
    swap_a = [pair for i in range(0, nv, 2) for pair in ((i, i + 1), (i + 1, i))]
    swap_b = [pair for i in range(1, nv - 1, 2) for pair in ((i, i + 1), (i + 1, i))]
    up = [(i, i + 1) for i in range(3)]
    down = [(i + 1, i) for i in range(3)]
    to_a = functools.partial(lax.ppermute, axis_name="vol", perm=swap_a)
    to_b = functools.partial(lax.ppermute, axis_name="vol", perm=swap_b)
    to_up = functools.partial(lax.ppermute, axis_name="mem", perm=up)
    to_down = functools.partial(lax.ppermute, axis_name="mem", perm=down)

    intra = intra_voxel.reshape(128, 128)
    extra = extra_voxel.reshape(128, 128)
    cnt_lane = jnp.repeat(facet_counts, 2).reshape(1, 128)

    volt, cells = pl.pallas_call(
        gather_kernel,
        out_shape=(shape(128, 128), shape(1, 128)),
        in_specs=[VM] * 4,
        out_specs=(VM, VM),
        cost_estimate=pl.CostEstimate(flops=4000000, bytes_accessed=1300000, transcendentals=0),
        name="voltages",
    )(potential, intra, extra, cnt_lane)

    column = [cells] + [
        lax.ppermute(cells, "mem", [(i, (i + d) % 4) for i in range(4)]) for d in (1, 2, 3)
    ]
    own_table = jnp.concatenate(column, axis=0)

    send_a, send_b, send_up, send_down = pl.pallas_call(
        pack_kernel,
        out_shape=(shape(4, 64, 1024), shape(4, 64, 1024), shape(8, 8, 1024), shape(8, 8, 1024)),
        in_specs=[SM, ANY, ANY],
        out_specs=(ANY,) * 4,
        scratch_shapes=[pltpu.SemaphoreType.DMA((12,))],
        cost_estimate=pl.CostEstimate(flops=0, bytes_accessed=5000000, transcendentals=0),
        name="pack",
    )(meta, potential, conductivity)

    def edge_rows(from_below, from_above):
        sub = lax.broadcasted_iota(jnp.int32, from_below.shape, 1)
        return jnp.where(sub < 3, from_above, jnp.where(sub >= 5, from_below, 0.0))

    def corners(rows4):
        toward_b = jnp.where(par == 0, rows4[0:2], jnp.stack([rows4[3], rows4[2]]))
        toward_a = jnp.where(par == 0, jnp.stack([rows4[3], rows4[2]]), rows4[0:2])
        return to_a(toward_a), to_b(toward_b)

    early_a, early_b = to_a(send_a), to_b(send_b)
    y_early = edge_rows(to_up(send_up), to_down(send_down))
    corner_a, corner_b = corners(y_early[0:4])

    rates = jnp.stack([
        rate_slope[0] * LOG2E, jnp.log2(rate_scale[0]), rate_slope[1] * (-LOG2E), jnp.log2(rate_scale[1]),
    ])
    rates = jnp.broadcast_to(rates[:, :, None], (4, 40, 128))
    g_wide = jnp.broadcast_to(type_cond[:, :, None], (3, 40, 128))
    gr_wide = jnp.broadcast_to((type_cond * reversal[None, :])[:, :, None], (3, 40, 128))
    steps = 4
    width = 16384 // steps
    facet_rows = pl.BlockSpec((128 // steps, 128), lambda i, *_: (i, 0))
    state_block = pl.BlockSpec((40, width), lambda i, *_: (0, i))
    whole = lambda n: pl.BlockSpec((n, 40, 128), lambda i, *_: (0, 0, 0))
    states_next, ion, act = pl.pallas_call(
        ionic_kernel,
        out_shape=(shape(40, 16384), shape(128, 128), shape(128, 128)),
        grid_spec=pltpu.PrefetchScalarGridSpec(
            num_scalar_prefetch=2,
            grid=(steps,),
            in_specs=[facet_rows, state_block, whole(4), whole(3), whole(3)],
            out_specs=(state_block, facet_rows, facet_rows),
        ),
        cost_estimate=pl.CostEstimate(flops=16000000, bytes_accessed=5300000, transcendentals=2600000),
        name="ionic",
    )(facet_counts, cell_type, volt, ion_states, rates, g_wide, gr_wide)

    source, count = pl.pallas_call(
        scatter_kernel,
        out_shape=(shape(4, 64, 1024), shape(4, 64, 1024)),
        in_specs=[VM] * 4,
        out_specs=(VM, VM),
        cost_estimate=pl.CostEstimate(flops=800000000, bytes_accessed=2300000, transcendentals=0),
        name="scatter",
    )(ion, act, intra, extra)

    w, k = pl.pallas_call(
        start_kernel,
        out_shape=(shape(4, 64, 1024), shape(4, 64, 1024)),
        in_specs=[SM, ANY, ANY, ANY, ANY, ANY, VM, VM],
        out_specs=(VM, VM),
        scratch_shapes=[pltpu.VMEM((6, 72, 1024), F32), pltpu.VMEM((6, 72, 1024), F32),
                        pltpu.SemaphoreType.DMA((20,))],
        compiler_params=BIG,
        cost_estimate=pl.CostEstimate(flops=16000000, bytes_accessed=6000000, transcendentals=0),
        name="start",
    )(meta, potential, conductivity, early_a, early_b, y_early, source, count)

    table = jnp.concatenate([own_table, to_a(own_table), to_b(own_table)], axis=0)
    part_lane = jnp.repeat(gap_partner.T, 2, axis=1)
    cond_lane = jnp.repeat(gap_cond.T, 2, axis=1)
    u, u_a, u_b, u_up, u_down, membrane = pl.pallas_call(
        gap_kernel,
        out_shape=(shape(4, 64, 1024), shape(3, 64, 1024), shape(3, 64, 1024), shape(4, 8, 1024),
                   shape(4, 8, 1024), shape(128, 128)),
        in_specs=[SM] + [VM] * 8,
        out_specs=(VM,) * 6,
        scratch_shapes=[pltpu.VMEM((256, 128), F32)],
        cost_estimate=pl.CostEstimate(flops=1000000, bytes_accessed=5000000, transcendentals=0),
        compiler_params=BIG,
        name="gap",
    )(meta, table, part_lane, cond_lane, cnt_lane, ion, act, w, k)

    late_b, late_a = to_b(u_b), to_a(u_a)
    y_late = edge_rows(to_up(u_up), to_down(u_down))
    late_corner_a, late_corner_b = corners(y_late)

    big = lambda n: pltpu.VMEM((n, 72, 1024), F32)
    potential_next = pl.pallas_call(
        sweep_kernel,
        out_shape=shape(4, 64, 1024),
        in_specs=[SM, VM] + [ANY] * 12,
        out_specs=VM,
        scratch_shapes=[big(10), big(10), big(9), big(8), big(9), big(9), big(9), big(9), big(9), big(9), big(9),
                        pltpu.SemaphoreType.DMA((36,))],
        compiler_params=BIG,
        cost_estimate=pl.CostEstimate(flops=50000000, bytes_accessed=10000000, transcendentals=0),
        name="sweeps",
    )(meta, potential, conductivity, early_a, early_b, y_early[0:4], corner_a, corner_b,
      u, late_a, late_b, y_late, late_corner_a, late_corner_b)
    return potential_next, states_next, membrane.reshape(16384)


def solution(mesh):
    in_specs = (
        P("vol", "mem", None), P("vol", "mem", None), P(None, ("vol", "mem")),
        P(), P(), P(), P(),
        P(("vol", "mem")), P(("vol", "mem")), P(("vol", "mem")), P(("vol", "mem")),
        P(("vol", "mem"), None), P(("vol", "mem"), None),
    )
    out_specs = (P("vol", "mem", None), P(None, ("vol", "mem")), P(("vol", "mem")))
    return jax.shard_map(per_device, mesh=mesh, in_specs=in_specs, out_specs=out_specs, check_vma=False)
```

```python
import functools
import math

import jax
import jax.numpy as jnp
from jax import lax
from jax.experimental import pallas as pl
from jax.experimental.pallas import tpu as pltpu
from jax.sharding import PartitionSpec as P

LOG2E = math.log2(math.e)
SWEEPS = 4
F32 = jnp.float32
BF16 = jnp.bfloat16
ANY = pl.BlockSpec(memory_space=pl.ANY)
VM = pl.BlockSpec(memory_space=pltpu.VMEM)
SM = pl.BlockSpec(memory_space=pltpu.SMEM)


def grant(mib):
    return pltpu.CompilerParams(vmem_limit_bytes=mib * 1024 * 1024)


def sweep_factors():
    theta, delta = 1.0, 0.8
    sigma = theta / delta
    rho = 1.0 / sigma
    factors = []
    for _ in range(SWEEPS - 1):
        rho_next = 1.0 / (2.0 * sigma - rho)
        factors.append((rho_next * rho, 2.0 * rho_next / delta))
        rho = rho_next
    return factors


def iota(shape, dim):
    return lax.broadcasted_iota(jnp.int32, shape, dim)


def plane_of(parity, j):
    return j + parity * (3 - 2 * j)


def gather_kernel(p_ref, in_ref, ex_ref, cnt_ref, volt_ref, cell_ref):
    sub = iota((8, 128), 0)
    low = sub < 4

    def body(kk, carry):
        x = kk // 4
        blocks = [r[pl.ds(pl.multiple_of(8 * kk, 8), 8), :] & 4095 for r in (in_ref, ex_ref)]
        for q in range(2):
            row = pl.multiple_of((2 * (kk % 4) + q) * 8, 8)
            tiles = [p_ref[x, pl.ds(row, 8), 128 * z : 128 * z + 128] for z in range(8)]
            for h in range(2):
                picked = []
                for block in blocks:
                    a = jnp.broadcast_to(block[4 * q + h : 4 * q + h + 1], (8, 128))
                    b = jnp.broadcast_to(block[4 * q + 2 + h : 4 * q + 3 + h], (8, 128))
                    o = jnp.where(low, a, b)
                    lane = o & 127
                    z_of = (o >> 7) & 7
                    got = jnp.take_along_axis(tiles[0], lane, axis=1, mode="promise_in_bounds")
                    for z in range(1, 8):
                        new = jnp.take_along_axis(tiles[z], lane, axis=1, mode="promise_in_bounds")
                        got = jnp.where(z_of == z, new, got)
                    picked.append(jnp.where((o >> 10) == (sub & 3), got, 0.0))
                d = picked[0] - picked[1]
                d = d + pltpu.roll(d, 7, 0)
                d = d + pltpu.roll(d, 6, 0)
                volt_ref[pl.ds(8 * kk + 4 * q + h, 1), :] = d[0:1]
                volt_ref[pl.ds(8 * kk + 4 * q + 2 + h, 1), :] = d[4:5]
        return carry

    lax.fori_loop(0, 16, body, 0, unroll=4)
    turned = jnp.transpose(volt_ref[...])
    cnt = cnt_ref[...]
    lanes = iota((128, 128), 1)
    used = iota((128, 128), 0) + 128 * (lanes & 1) < cnt
    total = jnp.sum(jnp.where(used, turned, 0.0), axis=0, keepdims=True)
    even = (iota((1, 128), 1) & 1) == 0
    other = jnp.where(even, pltpu.roll(total, 127, 1), pltpu.roll(total, 1, 1))
    cell_ref[...] = (total + other) / jnp.maximum(cnt, 1).astype(F32)


def pack_kernel(meta, p_ref, c_ref, a_ref, b_ref, up_ref, down_ref):
    par = meta[0]
    for i in range(3):
        a_ref[i] = c_ref[plane_of(par, 3 - i)]
        b_ref[i] = c_ref[plane_of(par, i)]
    a_ref[3] = p_ref[plane_of(par, 3)]
    b_ref[3] = p_ref[plane_of(par, 0)]
    for k, ref in enumerate((c_ref, p_ref)):
        for x in range(4):
            up_ref[4 * k + x] = ref[x, 56:64]
            down_ref[4 * k + x] = ref[x, 0:8]


def ionic_kernel(cnt, typ, volt_ref, st_ref, rate_ref, g_ref, gr_ref, out_ref, ion_ref, act_ref):
    step = pl.program_id(0)
    cells = volt_ref.shape[0] // 2
    lane = iota((8, 128), 1)

    def body(group, carry):
        rows8 = pl.ds(pl.multiple_of(8 * group, 8), 8)
        volts = volt_ref[rows8, :]
        counts, types, v, active, cols = [], [], [], [], []
        for q in range(4):
            counts.append(cnt[step * cells + 4 * group + q])
            types.append(typ[step * cells + 4 * group + q])
        for r in range(8):
            v.append(jnp.broadcast_to(volts[r : r + 1], (8, 128)))
            active.append(lane + (r % 2) * 128 < counts[r // 2])
            cols.append(pl.ds(pl.multiple_of(1024 * group + 128 * r, 128), 128))
        w1, w2 = [None] * 8, [None] * 8
        for k in range(5):
            rows = slice(8 * k, 8 * k + 8)
            rate = [rate_ref[i, rows] for i in range(4)]
            for q in range(4):
                g, gr = g_ref[types[q], rows], gr_ref[types[q], rows]
                for r in (2 * q, 2 * q + 1):
                    st = st_ref[rows, cols[r]]
                    opening = jnp.exp2(rate[0] * v[r] + rate[1])
                    closing = jnp.exp2(rate[2] * v[r] + rate[3])
                    total = opening + closing
                    rec = pl.reciprocal(total, approx=True)
                    rec = rec * (2.0 - total * rec)
                    steady = opening * rec
                    fresh = steady + (st - steady) * jnp.exp2(total * (-0.5 * LOG2E))
                    out_ref[rows, cols[r]] = jnp.where(active[r], fresh, st)
                    w1[r] = g * fresh if k == 0 else w1[r] + g * fresh
                    w2[r] = gr * fresh if k == 0 else w2[r] + gr * fresh
        used = jnp.concatenate([jnp.where(a, 1.0, 0.0)[0:1] for a in active], axis=0)
        ion = [jnp.sum(w1[r] * v[r] - w2[r], axis=0, keepdims=True) for r in range(8)]
        ion_ref[rows8, :] = jnp.concatenate(ion, axis=0) * used
        act_ref[rows8, :] = used
        return carry

    lax.fori_loop(0, cells // 4, body, 0)


def scatter_kernel(ion_ref, act_ref, in_ref, ex_ref, s_ref, n_ref):
    row_iota = iota((32, 512), 0)
    lane_iota = iota((128, 512), 0)
    low = iota((8, 128), 0) < 4
    odd_row = (iota((8, 128), 0) & 2) // 2

    def body(kk, carry):
        rows8 = pl.ds(pl.multiple_of(8 * kk, 8), 8)
        x = kk // 4
        val = ion_ref[rows8, :]
        act = act_ref[rows8, :]
        hi = val.astype(BF16).astype(F32)
        lo = val - hi
        mids, lanes = [], []
        for ref in (in_ref, ex_ref):
            o = ref[rows8, :] & 4095
            mids.append((((o >> 7) & 7) ^ odd_row) * 4 + (o >> 10))
            lanes.append(o & 127)

        def line(a, b, s):
            r = 2 * s
            return jnp.concatenate([a[r : r + 1], a[r + 1 : r + 2], b[r : r + 1], b[r + 1 : r + 2]], axis=1)

        for q in range(2):
            results = []
            for s in (2 * q, 2 * q + 1):
                hit = line(mids[0], mids[1], s) == row_iota
                left = jnp.concatenate(
                    [jnp.where(hit, line(piece, -piece, s), 0.0).astype(BF16) for piece in (hi, lo, act)], axis=0
                )
                right = jnp.where(line(lanes[0], lanes[1], s) == lane_iota, 1.0, 0.0).astype(BF16)
                out = lax.dot_general(left, right, (((1,), (1,)), ((), ())), preferred_element_type=F32)
                results.append((out[0:32] + out[32:64], out[64:96]))
            row = pl.ds(pl.multiple_of((2 * (kk % 4) + q) * 8, 8), 8)
            for dst, e, o in ((s_ref, results[0][0], results[1][0]), (n_ref, results[0][1], results[1][1])):
                for j in range(4):
                    ej, oj = e[8 * j : 8 * j + 8], o[8 * j : 8 * j + 8]
                    dst[x, row, 256 * j : 256 * j + 128] = jnp.where(low, ej, oj)
                    dst[x, row, 256 * j + 128 : 256 * j + 256] = pltpu.roll(jnp.where(low, oj, ej), 4, 0)
        return carry

    lax.fori_loop(0, 16, body, 0, unroll=4)


def tile(ref, e, t):
    return ref[e, 8 * t : 8 * t + 8, :]


class Around:
    def __init__(self, ref, e):
        self.ref, self.e = ref, e
        self.sub = iota((8, 1024), 0)

    def at(self, t):
        ref, e = self.ref, self.e
        c = tile(ref, e, t)
        before, after = tile(ref, e, (t + 8) % 9), tile(ref, e, (t + 1) % 9)
        ym = jnp.where(self.sub == 0, pltpu.roll(before, 1, 0), pltpu.roll(c, 1, 0))
        yp = jnp.where(self.sub == 7, pltpu.roll(after, 7, 0), pltpu.roll(c, 7, 0))
        zm, zp = pltpu.roll(c, 1, 1), pltpu.roll(c, 1023, 1)
        return c, tile(ref, e - 1, t), tile(ref, e + 1, t), ym, yp, zm, zp


def couplings(around, t):
    lane = iota((8, 1024), 1)
    c, xm, xp, ym, yp, zm, zp = around.at(t)
    first, last = lane == 0, lane == 1023
    zm = jnp.where(first, 0.0, zm)
    zp = jnp.where(last, 0.0, zp)
    fs = [0.25 * (c + other) for other in (xm, xp, ym, yp, zm, zp)]
    diagonal = 1.0 + (((fs[0] + fs[1]) + (fs[2] + fs[3])) + (fs[4] + fs[5]))
    fs[4] = jnp.where(first, 0.0, fs[4])
    fs[5] = jnp.where(last, 0.0, fs[5])
    return fs, diagonal


def weighted(fs, views):
    t = [f * v for f, v in zip(fs, views)]
    return ((t[0] + t[1]) + (t[2] + t[3])) + (t[4] + t[5])


def halo_copies(par, dst, own, a, b, y, ca, cb, sem, start, own_y=0):
    copies = []
    for j in range(4):
        copies.append((own.at[plane_of(par, j)], dst.at[3 + j, 0:64]))
        copies.append((y.at[own_y + plane_of(par, j)], dst.at[3 + j, 64:72]))
    for i in range(3):
        copies.append((a.at[i], dst.at[7 + i, 0:64]))
        copies.append((b.at[i], dst.at[2 - i, 0:64]))
    for i in range(2):
        copies.append((ca.at[i], dst.at[7 + i, 64:72]))
        copies.append((cb.at[i], dst.at[2 - i, 64:72]))
    return begin(copies, sem, start)


def begin(copies, sem, start):
    made = [pltpu.make_async_copy(s, d, sem.at[start + n]) for n, (s, d) in enumerate(copies)]
    for m in made:
        m.start()
    return made


def operator_kernel(meta, p_hbm, c_hbm, a_hbm, b_hbm, y_hbm, ca_hbm, cb_hbm, s_ref, n_ref,
                    fx, fym, fyp, fzm, fzp, inv, w_ref, k_ref, c, pe, sem):
    par, has_b, mine = meta[0], meta[1], meta[2]
    made = halo_copies(par, c, c_hbm, a_hbm, b_hbm, y_hbm, ca_hbm, cb_hbm, sem, 0)
    copies = [(a_hbm.at[3], pe.at[5, 0:64]), (b_hbm.at[3], pe.at[0, 0:64])]
    for j in range(4):
        copies.append((p_hbm.at[plane_of(par, j)], pe.at[1 + j, 0:64]))
        copies.append((y_hbm.at[4 + plane_of(par, j)], pe.at[1 + j, 64:72]))
    made += begin(copies, sem, len(made))
    zero8 = jnp.zeros((8, 1024), F32)
    c[0, 64:72, :] = zero8
    c[9, 64:72, :] = zero8
    sub = iota((8, 1024), 0)
    bottom = (sub < 3) & (mine != 3)
    top = (sub >= 5) & (mine != 0)
    keep = jnp.where(bottom | top, 1.0, 0.0)
    for m in made:
        m.wait()

    def build(e, carry):
        around = Around(c, e)
        inside = jnp.where((e >= 3) | (has_b == 1), 1.0, 0.0)
        for t in range(9):
            rows = slice(8 * t, 8 * t + 8)
            fs, diagonal = couplings(around, t)
            part = inside / diagonal
            inv[e - 1, rows, :] = part * keep if t == 8 else part
            fx[e - 1, rows, :] = fs[0]
            fx[e, rows, :] = fs[1]
            fym[e - 1, rows, :] = fs[2]
            fyp[e - 1, rows, :] = fs[3]
            fzm[e - 1, rows, :] = fs[4]
            fzp[e - 1, rows, :] = fs[5]
        return carry

    lax.fori_loop(1, 9, build, 0)

    def body(j, carry):
        x = plane_of(par, j)
        pa = Around(pe, 1 + j)
        for t in range(8):
            rows = slice(8 * t, 8 * t + 8)
            fs = [tile(fx, j + 2, t), tile(fx, j + 3, t)] + [tile(f, j + 2, t) for f in (fym, fyp, fzm, fzp)]
            part = tile(inv, j + 2, t)
            views = pa.at(t)
            p = views[0]
            w_ref[x, rows, :] = (p + weighted(fs, views[1:]) - 0.5 * s_ref[x, rows, :]) * part - p
            k_ref[x, rows, :] = (-0.5 * part) * n_ref[x, rows, :]
        return carry

    lax.fori_loop(0, 4, body, 0)


def gap_kernel(meta, table_ref, part_ref, cond_ref, cnt_ref, ion_ref, act_ref, w_ref, k_ref,
               u_ref, a_ref, b_ref, up_ref, down_ref, mem_ref, spread):
    par, mine, v = meta[0], meta[2], meta[3]
    part = part_ref[...]
    brick = part >> 6
    bx, by = brick >> 2, brick & 3
    side = jnp.where(bx == v, 0, jnp.where(bx == (v ^ 1), 1, 2))
    row = side * 4 + ((mine - by) & 3)
    lane = (part & 63) * 2
    other = jnp.zeros((8, 128), F32)
    for r in range(12):
        line = jnp.broadcast_to(table_ref[r : r + 1, :], (8, 128))
        other = jnp.where(row == r, jnp.take_along_axis(line, lane, axis=1, mode="promise_in_bounds"), other)
    own = table_ref[0:1, :]
    current = jnp.sum(cond_ref[...] * (own - other), axis=0, keepdims=True)
    g = current / jnp.maximum(cnt_ref[...], 1).astype(F32)
    g8 = jnp.broadcast_to(g, (8, 128))
    mem_ref[...] = ion_ref[...] + act_ref[...] * jnp.transpose(jnp.broadcast_to(g, (128, 128)))
    for half in range(2):
        at = 64 * half + 2 * (iota((8, 128), 1) // 4)
        wide = jnp.take_along_axis(g8, at, axis=1, mode="promise_in_bounds")[0:1]
        spread[128 * half : 128 * half + 128, :] = jnp.transpose(jnp.broadcast_to(wide, (128, 128)))

    def body(j, carry):
        x = plane_of(par, j)
        for t in range(8):
            rows = slice(8 * t, 8 * t + 8)
            gt = spread[pl.ds(pl.multiple_of(x * 64 + 8 * t, 8), 8), :]
            u = w_ref[x, rows, :] + k_ref[x, rows, :] * jnp.tile(gt, (1, 8))
            u_ref[x, rows, :] = u
            if t == 0:
                down_ref[x] = u
            if t == 7:
                up_ref[x] = u

            @pl.when(j < 3)
            def _():
                b_ref[j, rows, :] = u

            @pl.when(j > 0)
            def _():
                a_ref[3 - j, rows, :] = u

        return carry

    lax.fori_loop(0, 4, body, 0)


def sweep_kernel(meta, p_ref, fx, fym, fyp, fzm, fzp, inv, u_hbm, ua_hbm, ub_hbm, uy_hbm, uca_hbm, ucb_hbm,
                 out_ref, u0, u1, u2, r, sem):
    par = meta[0]
    made = halo_copies(par, u0, u_hbm, ua_hbm, ub_hbm, uy_hbm, uca_hbm, ucb_hbm, sem, 0)
    zero8 = jnp.zeros((8, 1024), F32)
    u0[0, 64:72, :] = zero8
    u0[9, 64:72, :] = zero8
    for m in made:
        m.wait()
    (a1, b1), (a2, b2), (a3, b3) = sweep_factors()

    def coupled(around, e, t):
        fs = [tile(fx, e - 1, t), tile(fx, e, t)] + [tile(f, e - 1, t) for f in (fym, fyp, fzm, fzp)]
        views = around.at(t)
        return views[0], tile(inv, e - 1, t) * weighted(fs, views[1:])

    def first(e, carry):
        around = Around(u0, e)
        for t in range(9):
            rows = slice(8 * t, 8 * t + 8)
            u, res = coupled(around, e, t)
            r[e, rows, :] = res
            u1[e, rows, :] = a1 * u + b1 * res
        return carry

    lax.fori_loop(1, 9, first, 0)

    def second(e, carry):
        around = Around(u1, e)
        for t in range(9):
            rows = slice(8 * t, 8 * t + 8)
            u, more = coupled(around, e, t)
            res = (tile(r, e, t) - u) + more
            r[e, rows, :] = res
            u2[e, rows, :] = a2 * u + b2 * res
        return carry

    lax.fori_loop(2, 8, second, 0)

    def third(j, carry):
        e = 3 + j
        x = plane_of(par, j)
        around = Around(u2, e)
        for t in range(8):
            rows = slice(8 * t, 8 * t + 8)
            u, more = coupled(around, e, t)
            res = (tile(r, e, t) - u) + more
            before = (p_ref[x, rows, :] + tile(u0, e, t)) + (tile(u1, e, t) + u)
            out_ref[x, rows, :] = before + (a3 * u + b3 * res)
        return carry

    lax.fori_loop(0, 4, third, 0)


def shape(*dims, kind=F32):
    return jax.ShapeDtypeStruct(dims, kind)


def per_device(potential, conductivity, ion_states, rate_scale, rate_slope, type_cond, reversal,
               facet_counts, intra_voxel, extra_voxel, cell_type, gap_partner, gap_cond):
    v, m = lax.axis_index("vol"), lax.axis_index("mem")
    par = v & 1
    nv = lax.axis_size("vol")
    has_b = jnp.where((v == 0) | (v == nv - 1), 0, 1)
    meta = jnp.stack([par, has_b, m, v]).astype(jnp.int32)
    swap_a = [pair for i in range(0, nv, 2) for pair in ((i, i + 1), (i + 1, i))]
    swap_b = [pair for i in range(1, nv - 1, 2) for pair in ((i, i + 1), (i + 1, i))]
    up = [(i, i + 1) for i in range(3)]
    down = [(i + 1, i) for i in range(3)]
    to_a = functools.partial(lax.ppermute, axis_name="vol", perm=swap_a)
    to_b = functools.partial(lax.ppermute, axis_name="vol", perm=swap_b)
    to_up = functools.partial(lax.ppermute, axis_name="mem", perm=up)
    to_down = functools.partial(lax.ppermute, axis_name="mem", perm=down)

    intra = intra_voxel.reshape(128, 128)
    extra = extra_voxel.reshape(128, 128)
    cnt_lane = jnp.repeat(facet_counts, 2).reshape(1, 128)

    volt, cells = pl.pallas_call(
        gather_kernel,
        out_shape=(shape(128, 128), shape(1, 128)),
        in_specs=[VM] * 4,
        out_specs=(VM, VM),
        compiler_params=grant(8),
        cost_estimate=pl.CostEstimate(flops=4000000, bytes_accessed=1300000, transcendentals=0),
        name="voltages",
    )(potential, intra, extra, cnt_lane)

    column = [cells] + [
        lax.ppermute(cells, "mem", [(i, (i + d) % 4) for i in range(4)]) for d in (1, 2, 3)
    ]
    own_table = jnp.concatenate(column, axis=0)

    send_a, send_b, send_up, send_down = pl.pallas_call(
        pack_kernel,
        out_shape=(shape(4, 64, 1024), shape(4, 64, 1024), shape(8, 8, 1024), shape(8, 8, 1024)),
        in_specs=[SM, VM, VM],
        out_specs=(VM,) * 4,
        compiler_params=grant(12),
        cost_estimate=pl.CostEstimate(flops=0, bytes_accessed=5000000, transcendentals=0),
        name="pack",
    )(meta, potential, conductivity)

    def edge_rows(from_below, from_above):
        sub = lax.broadcasted_iota(jnp.int32, from_below.shape, 1)
        return jnp.where(sub < 3, from_above, jnp.where(sub >= 5, from_below, 0.0))

    def corners(rows4):
        toward_b = jnp.where(par == 0, rows4[0:2], jnp.stack([rows4[3], rows4[2]]))
        toward_a = jnp.where(par == 0, jnp.stack([rows4[3], rows4[2]]), rows4[0:2])
        return to_a(toward_a), to_b(toward_b)

    early_a, early_b = to_a(send_a), to_b(send_b)
    y_early = edge_rows(to_up(send_up), to_down(send_down))
    corner_a, corner_b = corners(y_early[0:4])

    rates = jnp.stack([
        rate_slope[0] * LOG2E, jnp.log2(rate_scale[0]), rate_slope[1] * (-LOG2E), jnp.log2(rate_scale[1]),
    ])
    rates = jnp.broadcast_to(rates[:, :, None], (4, 40, 128))
    g_wide = jnp.broadcast_to(type_cond[:, :, None], (3, 40, 128))
    gr_wide = jnp.broadcast_to((type_cond * reversal[None, :])[:, :, None], (3, 40, 128))
    steps = 4
    width = 16384 // steps
    facet_rows = pl.BlockSpec((128 // steps, 128), lambda i, *_: (i, 0))
    state_block = pl.BlockSpec((40, width), lambda i, *_: (0, i))
    whole = lambda n: pl.BlockSpec((n, 40, 128), lambda i, *_: (0, 0, 0))
    states_next, ion, act = pl.pallas_call(
        ionic_kernel,
        out_shape=(shape(40, 16384), shape(128, 128), shape(128, 128)),
        grid_spec=pltpu.PrefetchScalarGridSpec(
            num_scalar_prefetch=2,
            grid=(steps,),
            in_specs=[facet_rows, state_block, whole(4), whole(3), whole(3)],
            out_specs=(state_block, facet_rows, facet_rows),
        ),
        compiler_params=grant(16),
        cost_estimate=pl.CostEstimate(flops=16000000, bytes_accessed=5300000, transcendentals=2600000),
        name="ionic",
    )(facet_counts, cell_type, volt, ion_states, rates, g_wide, gr_wide)

    source, count = pl.pallas_call(
        scatter_kernel,
        out_shape=(shape(4, 64, 1024), shape(4, 64, 1024)),
        in_specs=[VM] * 4,
        out_specs=(VM, VM),
        compiler_params=grant(12),
        cost_estimate=pl.CostEstimate(flops=800000000, bytes_accessed=2300000, transcendentals=0),
        name="scatter",
    )(ion, act, intra, extra)

    coefficients = (shape(9, 72, 1024),) + (shape(8, 72, 1024),) * 5
    *operator, w, k = pl.pallas_call(
        operator_kernel,
        out_shape=coefficients + (shape(4, 64, 1024), shape(4, 64, 1024)),
        in_specs=[SM] + [ANY] * 7 + [VM, VM],
        out_specs=(VM,) * 8,
        scratch_shapes=[pltpu.VMEM((10, 72, 1024), F32), pltpu.VMEM((6, 72, 1024), F32),
                        pltpu.SemaphoreType.DMA((28,))],
        compiler_params=grant(28),
        cost_estimate=pl.CostEstimate(flops=16000000, bytes_accessed=6000000, transcendentals=0),
        name="operator",
    )(meta, potential, conductivity, early_a, early_b, y_early, corner_a, corner_b, source, count)

    table = jnp.concatenate([own_table, to_a(own_table), to_b(own_table)], axis=0)
    part_lane = jnp.repeat(gap_partner.T, 2, axis=1)
    cond_lane = jnp.repeat(gap_cond.T, 2, axis=1)
    u, u_a, u_b, u_up, u_down, membrane = pl.pallas_call(
        gap_kernel,
        out_shape=(shape(4, 64, 1024), shape(3, 64, 1024), shape(3, 64, 1024), shape(4, 8, 1024),
                   shape(4, 8, 1024), shape(128, 128)),
        in_specs=[SM] + [VM] * 8,
        out_specs=(VM,) * 6,
        scratch_shapes=[pltpu.VMEM((256, 128), F32)],
        cost_estimate=pl.CostEstimate(flops=1000000, bytes_accessed=5000000, transcendentals=0),
        compiler_params=grant(20),
        name="gap",
    )(meta, table, part_lane, cond_lane, cnt_lane, ion, act, w, k)

    late_b, late_a = to_b(u_b), to_a(u_a)
    y_late = edge_rows(to_up(u_up), to_down(u_down))
    late_corner_a, late_corner_b = corners(y_late)

    big = lambda n: pltpu.VMEM((n, 72, 1024), F32)
    potential_next = pl.pallas_call(
        sweep_kernel,
        out_shape=shape(4, 64, 1024),
        in_specs=[SM] + [VM] * 7 + [ANY] * 6,
        out_specs=VM,
        scratch_shapes=[big(10), big(9), big(8), big(9), pltpu.SemaphoreType.DMA((18,))],
        compiler_params=grant(30),
        cost_estimate=pl.CostEstimate(flops=50000000, bytes_accessed=10000000, transcendentals=0),
        name="sweeps",
    )(meta, potential, *operator, u, late_a, late_b, y_late, late_corner_a, late_corner_b)
    return potential_next, states_next, membrane.reshape(16384)


def solution(mesh):
    in_specs = (
        P("vol", "mem", None), P("vol", "mem", None), P(None, ("vol", "mem")),
        P(), P(), P(), P(),
        P(("vol", "mem")), P(("vol", "mem")), P(("vol", "mem")), P(("vol", "mem")),
        P(("vol", "mem"), None), P(("vol", "mem"), None),
    )
    out_specs = (P("vol", "mem", None), P(None, ("vol", "mem")), P(("vol", "mem")))
    return jax.shard_map(per_device, mesh=mesh, in_specs=in_specs, out_specs=out_specs, check_vma=False)
```

```python
import functools
import math

import jax
import jax.numpy as jnp
from jax import lax
from jax.experimental import pallas as pl
from jax.experimental.pallas import tpu as pltpu
from jax.sharding import PartitionSpec as P

LOG2E = math.log2(math.e)
SWEEPS = 4
F32 = jnp.float32
BF16 = jnp.bfloat16
ANY = pl.BlockSpec(memory_space=pl.ANY)
HBM = pl.BlockSpec(memory_space=pltpu.HBM)
VM = pl.BlockSpec(memory_space=pltpu.VMEM)
SM = pl.BlockSpec(memory_space=pltpu.SMEM)


def grant(mib):
    return pltpu.CompilerParams(vmem_limit_bytes=mib * 1024 * 1024)


def sweep_factors():
    theta, delta = 1.0, 0.8
    sigma = theta / delta
    rho = 1.0 / sigma
    factors = []
    for _ in range(SWEEPS - 1):
        rho_next = 1.0 / (2.0 * sigma - rho)
        factors.append((rho_next * rho, 2.0 * rho_next / delta))
        rho = rho_next
    return factors


def iota(shape, dim):
    return lax.broadcasted_iota(jnp.int32, shape, dim)


def plane_of(parity, j):
    return j + parity * (3 - 2 * j)


def pair_sum(row):
    even = (iota((1, 128), 1) & 1) == 0
    return row + jnp.where(even, pltpu.roll(row, 127, 1), pltpu.roll(row, 1, 1))


def gather_kernel(meta, cnt, p_hbm, c_hbm, in_ref, ex_ref, part_ref, cond_ref,
                  volt_ref, cell_ref, act_ref, part_out, cond_out, a_hbm, b_hbm, up_hbm, down_hbm,
                  p_ref, c_ref, note, sem):
    par = meta[0]
    loads = begin([(p_hbm.at[x], p_ref.at[x]) for x in range(4)] + [(c_hbm.at[x], c_ref.at[x]) for x in range(4)], sem, 0)
    twice = iota((8, 128), 1) // 2
    for src, dst in ((part_ref, part_out), (cond_ref, cond_out)):
        wide = jnp.concatenate([src[...].astype(F32), jnp.zeros((64, 120), F32)], axis=1)
        turned = jnp.transpose(jnp.concatenate([wide, wide], axis=0))[0:8]
        dst[...] = jnp.take_along_axis(turned, twice, axis=1, mode="promise_in_bounds").astype(dst.dtype)
    for load in loads:
        load.wait()
    copies = []
    for i in range(3):
        copies.append((c_ref.at[plane_of(par, i)], b_hbm.at[i]))
        copies.append((c_ref.at[plane_of(par, 3 - i)], a_hbm.at[i]))
    copies.append((p_ref.at[plane_of(par, 0)], b_hbm.at[3]))
    copies.append((p_ref.at[plane_of(par, 3)], a_hbm.at[3]))
    for k, src in enumerate((c_ref, p_ref)):
        copies.append((src.at[:, 56:64], up_hbm.at[4 * k : 4 * k + 4]))
        copies.append((src.at[:, 0:8], down_hbm.at[4 * k : 4 * k + 4]))
    sends = begin(copies, sem, 8)
    sub = iota((8, 128), 0)
    low = sub < 4
    lane_row = iota((1, 128), 1)

    def body(kk, carry):
        x = kk // 4
        blocks = [r[pl.ds(pl.multiple_of(8 * kk, 8), 8), :] & 4095 for r in (in_ref, ex_ref)]
        for q in range(2):
            row = pl.multiple_of((2 * (kk % 4) + q) * 8, 8)
            tiles = [p_ref[x, pl.ds(row, 8), 128 * z : 128 * z + 128] for z in range(8)]
            for h in range(2):
                picked = []
                for block in blocks:
                    a = jnp.broadcast_to(block[4 * q + h : 4 * q + h + 1], (8, 128))
                    b = jnp.broadcast_to(block[4 * q + 2 + h : 4 * q + 3 + h], (8, 128))
                    o = jnp.where(low, a, b)
                    lane = o & 127
                    z_of = (o >> 7) & 7
                    got = jnp.take_along_axis(tiles[0], lane, axis=1, mode="promise_in_bounds")
                    for z in range(1, 8):
                        new = jnp.take_along_axis(tiles[z], lane, axis=1, mode="promise_in_bounds")
                        got = jnp.where(z_of == z, new, got)
                    picked.append(jnp.where((o >> 10) == (sub & 3), got, 0.0))
                d = picked[0] - picked[1]
                d = d + pltpu.roll(d, 7, 0)
                d = d + pltpu.roll(d, 6, 0)
                for i in range(2):
                    at = pl.ds(8 * kk + 4 * q + 2 * i + h, 1)
                    volt_ref[at, :] = d[4 * i : 4 * i + 1]
                    used = lane_row + 128 * h < cnt[4 * kk + 2 * q + i]
                    act_ref[at, :] = jnp.where(used, 1.0, 0.0)
        return carry

    lax.fori_loop(0, 16, body, 0, unroll=4)
    act = act_ref[...]
    total = jnp.sum(jnp.transpose(volt_ref[...] * act), axis=0, keepdims=True)
    count = jnp.sum(jnp.transpose(act), axis=0, keepdims=True)
    cells = pair_sum(total) / jnp.maximum(pair_sum(count), 1.0)
    cell_ref[...] = cells
    note[...] = jnp.zeros((8, 1024), F32)
    note[0:1, 0:128] = cells
    sends += begin([(note, up_hbm.at[8]), (note, down_hbm.at[8])], sem, 20)
    for send in sends:
        send.wait()


def begin(copies, sem, start):
    made = [pltpu.make_async_copy(s, d, sem.at[start + n]) for n, (s, d) in enumerate(copies)]
    for m in made:
        m.start()
    return made


def ionic_kernel(cnt, typ, volt_ref, st_ref, rate_ref, out_ref, ion_ref):
    step = pl.program_id(0)
    cells = volt_ref.shape[0] // 2
    lane = iota((8, 128), 1)

    def body(group, carry):
        rows8 = pl.ds(pl.multiple_of(8 * group, 8), 8)
        volts = volt_ref[rows8, :]
        counts, types, v, active, cols = [], [], [], [], []
        for q in range(4):
            counts.append(cnt[step * cells + 4 * group + q])
            types.append(typ[step * cells + 4 * group + q])
        for r in range(8):
            v.append(jnp.broadcast_to(volts[r : r + 1], (8, 128)))
            active.append(lane + (r % 2) * 128 < counts[r // 2])
            cols.append(pl.ds(pl.multiple_of(1024 * group + 128 * r, 128), 128))
        w1, w2 = [None] * 8, [None] * 8
        for k in range(5):
            rows = slice(8 * k, 8 * k + 8)
            rate = [rate_ref[i, rows] for i in range(4)]
            for q in range(4):
                g, gr = rate_ref[4 + types[q], rows], rate_ref[7 + types[q], rows]
                for r in (2 * q, 2 * q + 1):
                    st = st_ref[rows, cols[r]]
                    opening = jnp.exp2(rate[0] * v[r] + rate[1])
                    closing = jnp.exp2(rate[2] * v[r] + rate[3])
                    total = opening + closing
                    rec = pl.reciprocal(total, approx=True)
                    rec = rec * (2.0 - total * rec)
                    steady = opening * rec
                    fresh = steady + (st - steady) * jnp.exp2(total * (-0.5 * LOG2E))
                    out_ref[rows, cols[r]] = jnp.where(active[r], fresh, st)
                    w1[r] = g * fresh if k == 0 else w1[r] + g * fresh
                    w2[r] = gr * fresh if k == 0 else w2[r] + gr * fresh
        act = jnp.concatenate([jnp.where(a, 1.0, 0.0)[0:1] for a in active], axis=0)
        ion = [jnp.sum(w1[r] * v[r] - w2[r], axis=0, keepdims=True) for r in range(8)]
        val = jnp.concatenate(ion, axis=0) * act
        ion_ref[rows8, :] = val

        return carry

    lax.fori_loop(0, cells // 4, body, 0)


def scatter_kernel(ion_ref, act_ref, in_ref, ex_ref, after, s_ref, n_ref):
    row_iota = iota((32, 512), 0)
    lane_iota = iota((128, 512), 0)
    low = iota((8, 128), 0) < 4
    odd_row = (iota((8, 128), 0) & 2) // 2

    def body(kk, carry):
        rows8 = pl.ds(pl.multiple_of(8 * kk, 8), 8)
        x = kk // 4
        val = ion_ref[rows8, :]
        act = act_ref[rows8, :]
        hi = val.astype(BF16).astype(F32)
        lo = val - hi
        mids, lanes = [], []
        for ref in (in_ref, ex_ref):
            o = ref[rows8, :] & 4095
            mids.append((((o >> 7) & 7) ^ odd_row) * 4 + (o >> 10))
            lanes.append(o & 127)

        def line(a, b, s):
            r = 2 * s
            return jnp.concatenate([a[r : r + 1], a[r + 1 : r + 2], b[r : r + 1], b[r + 1 : r + 2]], axis=1)

        for q in range(2):
            results = []
            for s in (2 * q, 2 * q + 1):
                hit = line(mids[0], mids[1], s) == row_iota
                left = jnp.concatenate(
                    [jnp.where(hit, line(piece, -piece, s), 0.0).astype(BF16) for piece in (hi, lo, act)], axis=0
                )
                right = jnp.where(line(lanes[0], lanes[1], s) == lane_iota, 1.0, 0.0).astype(BF16)
                out = lax.dot_general(left, right, (((1,), (1,)), ((), ())), preferred_element_type=F32)
                results.append((out[0:32] + out[32:64], out[64:96]))
            row = pl.ds(pl.multiple_of((2 * (kk % 4) + q) * 8, 8), 8)
            for dst, e, o in ((s_ref, results[0][0], results[1][0]), (n_ref, results[0][1], results[1][1])):
                for j in range(4):
                    ej, oj = e[8 * j : 8 * j + 8], o[8 * j : 8 * j + 8]
                    dst[x, row, 256 * j : 256 * j + 128] = jnp.where(low, ej, oj)
                    dst[x, row, 256 * j + 128 : 256 * j + 256] = pltpu.roll(jnp.where(low, oj, ej), 4, 0)
        return carry

    lax.fori_loop(0, 16, body, 0, unroll=4)


def edge_rows(meta, below, above):
    sub = iota((8, 1024), 0)
    bottom = (sub < 3) & (meta[2] != 3)
    top = (sub >= 5) & (meta[2] != 0)
    return jnp.where(bottom, above, jnp.where(top, below, 0.0))


def early_edge_kernel(meta, below_ref, above_ref, far_ref, cell_ref, after, y_ref, table_ref, a_ref, b_ref):
    par = meta[0]
    for x in range(8):
        y_ref[x] = edge_rows(meta, below_ref[x], above_ref[x])
    table = jnp.concatenate(
        [cell_ref[...], below_ref[8, 0:1, 0:128], far_ref[...], above_ref[8, 0:1, 0:128],
         jnp.zeros((4, 128), F32)], axis=0)
    table_ref[...] = table
    for i in range(2):
        a_ref[i] = y_ref[plane_of(par, 3 - i)]
        b_ref[i] = y_ref[plane_of(par, i)]
    for ref in (a_ref, b_ref):
        ref[2] = jnp.zeros((8, 1024), F32)
        ref[2, :, 0:128] = table


def late_edge_kernel(meta, below_ref, above_ref, ua_in, ub_in, y_ref, ua_ref, ub_ref, sem):
    par = meta[0]
    for x in range(4):
        y_ref[x] = edge_rows(meta, below_ref[x], above_ref[x])
    copies = []
    for i in range(3):
        copies.append((y_ref.at[plane_of(par, 3 - i)], ua_ref.at[i, 64:72]))
        copies.append((y_ref.at[plane_of(par, i)], ub_ref.at[i, 64:72]))
    for m in begin(copies, sem, 0):
        m.wait()


def tile(ref, e, t):
    return ref[e, 8 * t : 8 * t + 8, :]


class Around:
    def __init__(self, ref, e):
        self.ref, self.e = ref, e
        self.sub = iota((8, 1024), 0)

    def at(self, t):
        ref, e = self.ref, self.e
        c = tile(ref, e, t)
        before, after = tile(ref, e, (t + 8) % 9), tile(ref, e, (t + 1) % 9)
        ym = jnp.where(self.sub == 0, pltpu.roll(before, 1, 0), pltpu.roll(c, 1, 0))
        yp = jnp.where(self.sub == 7, pltpu.roll(after, 7, 0), pltpu.roll(c, 7, 0))
        zm, zp = pltpu.roll(c, 1, 1), pltpu.roll(c, 1023, 1)
        return c, tile(ref, e - 1, t), tile(ref, e + 1, t), ym, yp, zm, zp


def couplings(around, t):
    lane = iota((8, 1024), 1)
    c, xm, xp, ym, yp, zm, zp = around.at(t)
    first, last = lane == 0, lane == 1023
    zm = jnp.where(first, 0.0, zm)
    zp = jnp.where(last, 0.0, zp)
    fs = [0.25 * (c + other) for other in (xm, xp, ym, yp, zm, zp)]
    diagonal = 1.0 + (((fs[0] + fs[1]) + (fs[2] + fs[3])) + (fs[4] + fs[5]))
    fs[4] = jnp.where(first, 0.0, fs[4])
    fs[5] = jnp.where(last, 0.0, fs[5])
    return fs, diagonal


def weighted(fs, views):
    t = [f * v for f, v in zip(fs, views)]
    return ((t[0] + t[1]) + (t[2] + t[3])) + (t[4] + t[5])


def first_kernel(meta, p_hbm, c_hbm, a_hbm, b_hbm, y_hbm, table_ref, ta_ref, tb_ref, part_ref, cond_ref,
                 ion_ref, act_ref, s_ref, n_ref, u_ref, a_ref, b_ref, up_ref, down_ref, mem_ref,
                 ce, pe, spread, sem):
    par, mine, v = meta[0], meta[2], meta[3]
    copies = []
    for e, hbm, yk in ((ce, c_hbm, 0), (pe, p_hbm, 4)):
        for j in range(4):
            copies.append((hbm.at[plane_of(par, j)], e.at[1 + j, 0:64]))
            copies.append((y_hbm.at[yk + plane_of(par, j)], e.at[1 + j, 64:72]))
    copies.append((a_hbm.at[0], ce.at[5, 0:64]))
    copies.append((b_hbm.at[0], ce.at[0, 0:64]))
    copies.append((a_hbm.at[3], pe.at[5, 0:64]))
    copies.append((b_hbm.at[3], pe.at[0, 0:64]))
    made = begin(copies, sem, 0)

    part = part_ref[...]
    brick = part >> 6
    bx, by = brick >> 2, brick & 3
    side = jnp.where(bx == v, 0, jnp.where(bx == (v ^ 1), 1, 2))
    row = side * 4 + ((mine - by) & 3)
    lane = (part & 63) * 2
    tables = (table_ref[...], ta_ref[2, :, 0:128], tb_ref[2, :, 0:128])
    other = jnp.zeros((8, 128), F32)
    for r in range(12):
        line = jnp.broadcast_to(tables[r // 4][r % 4 : r % 4 + 1], (8, 128))
        other = jnp.where(row == r, jnp.take_along_axis(line, lane, axis=1, mode="promise_in_bounds"), other)
    own = tables[0][0:1]
    current = jnp.sum(cond_ref[...] * (own - other), axis=0, keepdims=True)
    act = act_ref[...]
    count = pair_sum(jnp.sum(jnp.transpose(act), axis=0, keepdims=True))
    g = current / jnp.maximum(count, 1.0)
    g8 = jnp.broadcast_to(g, (8, 128))
    mem_ref[...] = ion_ref[...] + act * jnp.transpose(jnp.broadcast_to(g, (128, 128)))
    for half in range(2):
        at = 64 * half + 2 * (iota((8, 128), 1) // 4)
        wide = jnp.take_along_axis(g8, at, axis=1, mode="promise_in_bounds")[0:1]
        spread[128 * half : 128 * half + 128, :] = jnp.transpose(jnp.broadcast_to(wide, (128, 128)))
    for m in made:
        m.wait()

    def body(j, carry):
        x = plane_of(par, j)
        ca, pa = Around(ce, 1 + j), Around(pe, 1 + j)
        ja, jb = jnp.clip(3 - j, 0, 2), jnp.clip(j, 0, 2)
        for t in range(8):
            rows = slice(8 * t, 8 * t + 8)
            fs, diagonal = couplings(ca, t)
            inv = 1.0 / diagonal
            views = pa.at(t)
            p = views[0]
            gt = jnp.tile(spread[pl.ds(pl.multiple_of(x * 64 + 8 * t, 8), 8), :], (1, 8))
            source = s_ref[x, rows, :] + gt * n_ref[x, rows, :]
            u = (p + weighted(fs, views[1:]) - 0.5 * source) * inv - p
            u_ref[x, rows, :] = u
            if t == 0:
                down_ref[x] = u
            if t == 7:
                up_ref[x] = u

            @pl.when(j < 3)
            def _():
                b_ref[jb, rows, :] = u

            @pl.when(j > 0)
            def _():
                a_ref[ja, rows, :] = u

        return carry

    lax.fori_loop(0, 4, body, 0)


def operator_kernel(meta, c_hbm, a_hbm, b_hbm, y_hbm, ca_hbm, cb_hbm, after,
                    fx, fym, fyp, fzm, fzp, inv, c, sem):
    par, has_b, mine = meta[0], meta[1], meta[2]
    copies = []
    for j in range(4):
        copies.append((c_hbm.at[plane_of(par, j)], c.at[3 + j, 0:64]))
        copies.append((y_hbm.at[plane_of(par, j)], c.at[3 + j, 64:72]))
    for i in range(3):
        copies.append((a_hbm.at[i], c.at[7 + i, 0:64]))
        copies.append((b_hbm.at[i], c.at[2 - i, 0:64]))
    for i in range(2):
        copies.append((ca_hbm.at[i], c.at[7 + i, 64:72]))
        copies.append((cb_hbm.at[i], c.at[2 - i, 64:72]))
    made = begin(copies, sem, 0)
    zero8 = jnp.zeros((8, 1024), F32)
    c[0, 64:72, :] = zero8
    c[9, 64:72, :] = zero8
    sub = iota((8, 1024), 0)
    bottom = (sub < 3) & (mine != 3)
    top = (sub >= 5) & (mine != 0)
    keep = jnp.where(bottom | top, 1.0, 0.0)
    for m in made:
        m.wait()

    def build(e, carry):
        around = Around(c, e)
        inside = jnp.where((e >= 3) | (has_b == 1), 1.0, 0.0)
        for t in range(9):
            rows = slice(8 * t, 8 * t + 8)
            fs, diagonal = couplings(around, t)
            part = inside / diagonal
            inv[e - 1, rows, :] = part * keep if t == 8 else part
            fx[e - 1, rows, :] = fs[0]
            fx[e, rows, :] = fs[1]
            fym[e - 1, rows, :] = fs[2]
            fyp[e - 1, rows, :] = fs[3]
            fzm[e - 1, rows, :] = fs[4]
            fzp[e - 1, rows, :] = fs[5]
        return carry

    lax.fori_loop(1, 9, build, 0)


def sweep_kernel(meta, p_hbm, fx, fym, fyp, fzm, fzp, inv, u_hbm, ua_hbm, ub_hbm, uy_hbm,
                 out_ref, u0, u1, u2, r, p_ref, sem):
    par = meta[0]
    p_copies = begin([(p_hbm.at[x], p_ref.at[x]) for x in range(4)], sem, 14)
    copies = []
    for j in range(4):
        copies.append((u_hbm.at[plane_of(par, j)], u0.at[3 + j, 0:64]))
        copies.append((uy_hbm.at[plane_of(par, j)], u0.at[3 + j, 64:72]))
    for i in range(3):
        copies.append((ua_hbm.at[i], u0.at[7 + i]))
        copies.append((ub_hbm.at[i], u0.at[2 - i]))
    for m in begin(copies, sem, 0):
        m.wait()
    (a1, b1), (a2, b2), (a3, b3) = sweep_factors()

    def coupled(around, e, t):
        fs = [tile(fx, e - 1, t), tile(fx, e, t)] + [tile(f, e - 1, t) for f in (fym, fyp, fzm, fzp)]
        views = around.at(t)
        return views[0], tile(inv, e - 1, t) * weighted(fs, views[1:])

    def first(e, carry):
        around = Around(u0, e)
        for t in range(9):
            rows = slice(8 * t, 8 * t + 8)
            u, res = coupled(around, e, t)
            r[e, rows, :] = res
            u1[e, rows, :] = a1 * u + b1 * res
        return carry

    lax.fori_loop(1, 9, first, 0)

    def second(e, carry):
        around = Around(u1, e)
        for t in range(9):
            rows = slice(8 * t, 8 * t + 8)
            u, more = coupled(around, e, t)
            res = (tile(r, e, t) - u) + more
            r[e, rows, :] = res
            u2[e, rows, :] = a2 * u + b2 * res
        return carry

    lax.fori_loop(2, 8, second, 0)

    def third(j, carry):
        e = 3 + j
        x = plane_of(par, j)
        around = Around(u2, e)
        for t in range(8):
            rows = slice(8 * t, 8 * t + 8)
            u, more = coupled(around, e, t)
            res = (tile(r, e, t) - u) + more
            before = (p_ref[x, rows, :] + tile(u0, e, t)) + (tile(u1, e, t) + u)
            out_ref[x, rows, :] = before + (a3 * u + b3 * res)
        return carry

    for m in p_copies:
        m.wait()
    lax.fori_loop(0, 4, third, 0)


def shape(*dims, kind=F32):
    return jax.ShapeDtypeStruct(dims, kind)


def per_device(potential, conductivity, ion_states, rate_scale, rate_slope, type_cond, reversal,
               facet_counts, intra_voxel, extra_voxel, cell_type, gap_partner, gap_cond):
    v, m = lax.axis_index("vol"), lax.axis_index("mem")
    par = v & 1
    nv = lax.axis_size("vol")
    has_b = jnp.where((v == 0) | (v == nv - 1), 0, 1)
    meta = jnp.stack([par, has_b, m, v]).astype(jnp.int32)
    swap_a = [pair for i in range(0, nv, 2) for pair in ((i, i + 1), (i + 1, i))]
    swap_b = [pair for i in range(1, nv - 1, 2) for pair in ((i, i + 1), (i + 1, i))]
    on_mem = lambda x, pairs: lax.ppermute(x, "mem", pairs)
    ring = lambda d: [(i, (i + d) % 4) for i in range(4)]
    to_a = functools.partial(lax.ppermute, axis_name="vol", perm=swap_a)
    to_b = functools.partial(lax.ppermute, axis_name="vol", perm=swap_b)

    intra = intra_voxel.reshape(128, 128)
    extra = extra_voxel.reshape(128, 128)

    volt, cells, act, part_lane, cond_lane, send_a, send_b, send_up, send_down = pl.pallas_call(
        gather_kernel,
        out_shape=(shape(128, 128), shape(1, 128), shape(128, 128), shape(8, 128, kind=jnp.int32), shape(8, 128),
                   shape(4, 64, 1024), shape(4, 64, 1024), shape(9, 8, 1024), shape(9, 8, 1024)),
        in_specs=[SM, SM, HBM, HBM] + [VM] * 4,
        out_specs=(VM,) * 5 + (ANY,) * 4,
        scratch_shapes=[pltpu.VMEM((4, 64, 1024), F32), pltpu.VMEM((4, 64, 1024), F32), pltpu.VMEM((8, 1024), F32),
                        pltpu.SemaphoreType.DMA((22,))],
        compiler_params=grant(8),
        cost_estimate=pl.CostEstimate(flops=4000000, bytes_accessed=5000000, transcendentals=0),
        name="voltages",
    )(meta, facet_counts, potential, conductivity, intra, extra, gap_partner, gap_cond)

    below, above, far = on_mem(send_up, ring(1)), on_mem(send_down, ring(3)), on_mem(cells, ring(2))
    early_b, early_a = to_b(send_b), to_a(send_a)

    rates = jnp.concatenate([
        jnp.stack([rate_slope[0] * LOG2E, jnp.log2(rate_scale[0]), rate_slope[1] * (-LOG2E), jnp.log2(rate_scale[1])]),
        type_cond, type_cond * reversal[None, :]], axis=0)
    rates = jnp.broadcast_to(rates[:, :, None], (10, 40, 128))
    steps = 4
    width = 16384 // steps
    facet_rows = pl.BlockSpec((128 // steps, 128), lambda i, *_: (i, 0))
    state_block = pl.BlockSpec((40, width), lambda i, *_: (0, i))
    states_next, ion = pl.pallas_call(
        ionic_kernel,
        out_shape=(shape(40, 16384), shape(128, 128)),
        grid_spec=pltpu.PrefetchScalarGridSpec(
            num_scalar_prefetch=2,
            grid=(steps,),
            in_specs=[facet_rows, state_block, pl.BlockSpec((10, 40, 128), lambda i, *_: (0, 0, 0))],
            out_specs=(state_block, facet_rows),
        ),
        compiler_params=grant(12),
        cost_estimate=pl.CostEstimate(flops=16000000, bytes_accessed=7300000, transcendentals=2600000),
        name="ionic",
    )(facet_counts, cell_type, volt, ion_states, rates)

    y_early, table, more_a, more_b = pl.pallas_call(
        early_edge_kernel,
        out_shape=(shape(8, 8, 1024), shape(8, 128), shape(3, 8, 1024), shape(3, 8, 1024)),
        in_specs=[SM] + [VM] * 4 + [ANY],
        out_specs=(VM,) * 4,
        compiler_params=grant(6),
        cost_estimate=pl.CostEstimate(flops=300000, bytes_accessed=1000000, transcendentals=0),
        name="early_edges",
    )(meta, below, above, far, cells, ion)
    more_b, more_a = to_b(more_b), to_a(more_a)

    source, count = pl.pallas_call(
        scatter_kernel,
        out_shape=(shape(4, 64, 1024), shape(4, 64, 1024)),
        in_specs=[VM] * 4 + [ANY],
        out_specs=(VM, VM),
        compiler_params=grant(8),
        cost_estimate=pl.CostEstimate(flops=800000000, bytes_accessed=2300000, transcendentals=0),
        name="scatter",
    )(ion, act, intra, extra, table)

    u, u_a, u_b, u_up, u_down, membrane = pl.pallas_call(
        first_kernel,
        out_shape=(shape(4, 64, 1024), shape(3, 72, 1024), shape(3, 72, 1024), shape(4, 8, 1024),
                   shape(4, 8, 1024), shape(128, 128)),
        in_specs=[SM, HBM, HBM] + [ANY] * 3 + [VM] * 9,
        out_specs=(VM,) * 6,
        scratch_shapes=[pltpu.VMEM((6, 72, 1024), F32), pltpu.VMEM((6, 72, 1024), F32),
                        pltpu.VMEM((256, 128), F32), pltpu.SemaphoreType.DMA((20,))],
        compiler_params=grant(16),
        cost_estimate=pl.CostEstimate(flops=16000000, bytes_accessed=8000000, transcendentals=0),
        name="first",
    )(meta, potential, conductivity, early_a, early_b, y_early, table, more_a, more_b, part_lane, cond_lane,
      ion, act, source, count)

    low_rows = on_mem(u_up, [(i, i + 1) for i in range(3)])
    high_rows = on_mem(u_down, [(i + 1, i) for i in range(3)])

    big = lambda n: pltpu.VMEM((n, 72, 1024), F32)
    operator = pl.pallas_call(
        operator_kernel,
        out_shape=(shape(9, 72, 1024),) + (shape(8, 72, 1024),) * 5,
        in_specs=[SM, HBM] + [ANY] * 6,
        out_specs=(VM,) * 6,
        scratch_shapes=[big(10), pltpu.SemaphoreType.DMA((18,))],
        compiler_params=grant(20),
        cost_estimate=pl.CostEstimate(flops=16000000, bytes_accessed=17000000, transcendentals=0),
        name="operator",
    )(meta, conductivity, early_a, early_b, y_early, more_a, more_b, u_up)

    y_late, u_a, u_b = pl.pallas_call(
        late_edge_kernel,
        out_shape=(shape(4, 8, 1024), shape(3, 72, 1024), shape(3, 72, 1024)),
        in_specs=[SM, VM, VM, ANY, ANY],
        out_specs=(VM, ANY, ANY),
        input_output_aliases={3: 1, 4: 2},
        scratch_shapes=[pltpu.SemaphoreType.DMA((6,))],
        compiler_params=grant(4),
        cost_estimate=pl.CostEstimate(flops=100000, bytes_accessed=500000, transcendentals=0),
        name="late_edges",
    )(meta, low_rows, high_rows, u_a, u_b)
    late_b, late_a = to_b(u_b), to_a(u_a)

    potential_next = pl.pallas_call(
        sweep_kernel,
        out_shape=shape(4, 64, 1024),
        in_specs=[SM, HBM] + [VM] * 6 + [ANY] * 4,
        out_specs=VM,
        scratch_shapes=[big(10), big(9), big(8), big(9), pltpu.VMEM((4, 64, 1024), F32), pltpu.SemaphoreType.DMA((18,))],
        compiler_params=grant(30),
        cost_estimate=pl.CostEstimate(flops=50000000, bytes_accessed=10000000, transcendentals=0),
        name="sweeps",
    )(meta, potential, *operator, u, late_a, late_b, y_late)
    return potential_next, states_next, membrane.reshape(16384)


def solution(mesh):
    in_specs = (
        P("vol", "mem", None), P("vol", "mem", None), P(None, ("vol", "mem")),
        P(), P(), P(), P(),
        P(("vol", "mem")), P(("vol", "mem")), P(("vol", "mem")), P(("vol", "mem")),
        P(("vol", "mem"), None), P(("vol", "mem"), None),
    )
    out_specs = (P("vol", "mem", None), P(None, ("vol", "mem")), P(("vol", "mem")))
    return jax.shard_map(per_device, mesh=mesh, in_specs=in_specs, out_specs=out_specs, check_vma=False)
```

```python
import functools
import math

import jax
import jax.numpy as jnp
from jax import lax
from jax.experimental import pallas as pl
from jax.experimental.pallas import tpu as pltpu
from jax.sharding import PartitionSpec as P

LOG2E = math.log2(math.e)
SWEEPS = 4
F32 = jnp.float32
BF16 = jnp.bfloat16
ANY = pl.BlockSpec(memory_space=pl.ANY)
HBM = pl.BlockSpec(memory_space=pltpu.HBM)
VM = pl.BlockSpec(memory_space=pltpu.VMEM)
SM = pl.BlockSpec(memory_space=pltpu.SMEM)


def grant(mib):
    return pltpu.CompilerParams(vmem_limit_bytes=mib * 1024 * 1024)


def sweep_factors():
    theta, delta = 1.0, 0.8
    sigma = theta / delta
    rho = 1.0 / sigma
    factors = []
    for _ in range(SWEEPS - 1):
        rho_next = 1.0 / (2.0 * sigma - rho)
        factors.append((rho_next * rho, 2.0 * rho_next / delta))
        rho = rho_next
    return factors


def iota(shape, dim):
    return lax.broadcasted_iota(jnp.int32, shape, dim)


def plane_of(parity, j):
    return j + parity * (3 - 2 * j)


def pair_sum(row):
    even = (iota((1, 128), 1) & 1) == 0
    return row + jnp.where(even, pltpu.roll(row, 127, 1), pltpu.roll(row, 1, 1))


def gather_kernel(meta, cnt, p_hbm, c_hbm, in_ref, ex_ref, part_ref, cond_ref,
                  volt_ref, cell_ref, act_ref, part_out, cond_out, a_hbm, b_hbm, up_hbm, down_hbm,
                  p_ref, c_ref, note, sem):
    par = meta[0]
    loads = begin([(p_hbm.at[x], p_ref.at[x]) for x in range(4)] + [(c_hbm.at[x], c_ref.at[x]) for x in range(4)], sem, 0)
    twice = iota((8, 128), 1) // 2
    for src, dst in ((part_ref, part_out), (cond_ref, cond_out)):
        wide = jnp.concatenate([src[...], src[...]], axis=1)
        dst[...] = jnp.take_along_axis(wide, twice, axis=1, mode="promise_in_bounds")
    sub = iota((8, 128), 0)
    low = sub < 4
    lane_row = iota((1, 128), 1)

    def body(kk, carry):
        x = kk // 4
        blocks = [r[pl.ds(pl.multiple_of(8 * kk, 8), 8), :] & 4095 for r in (in_ref, ex_ref)]
        for q in range(2):
            row = pl.multiple_of((2 * (kk % 4) + q) * 8, 8)
            tiles = [p_ref[x, pl.ds(row, 8), 128 * z : 128 * z + 128] for z in range(8)]
            for h in range(2):
                picked = []
                for block in blocks:
                    a = jnp.broadcast_to(block[4 * q + h : 4 * q + h + 1], (8, 128))
                    b = jnp.broadcast_to(block[4 * q + 2 + h : 4 * q + 3 + h], (8, 128))
                    o = jnp.where(low, a, b)
                    lane = o & 127
                    z_of = (o >> 7) & 7
                    got = jnp.take_along_axis(tiles[0], lane, axis=1, mode="promise_in_bounds")
                    for z in range(1, 8):
                        new = jnp.take_along_axis(tiles[z], lane, axis=1, mode="promise_in_bounds")
                        got = jnp.where(z_of == z, new, got)
                    picked.append(jnp.where((o >> 10) == (sub & 3), got, 0.0))
                d = picked[0] - picked[1]
                d = d + pltpu.roll(d, 7, 0)
                d = d + pltpu.roll(d, 6, 0)
                for i in range(2):
                    at = pl.ds(8 * kk + 4 * q + 2 * i + h, 1)
                    volt_ref[at, :] = d[4 * i : 4 * i + 1]
                    used = lane_row + 128 * h < cnt[4 * kk + 2 * q + i]
                    act_ref[at, :] = jnp.where(used, 1.0, 0.0)
        return carry

    for x in range(4):
        if x < 2:
            loads[x].wait()
        lax.fori_loop(4 * x, 4 * x + 4, body, 0, unroll=4)
        if x == 1:
            for load in loads[2:]:
                load.wait()
            copies = []
            for i in range(3):
                copies.append((c_ref.at[plane_of(par, i)], b_hbm.at[i]))
                copies.append((c_ref.at[plane_of(par, 3 - i)], a_hbm.at[i]))
            copies.append((p_ref.at[plane_of(par, 0)], b_hbm.at[3]))
            copies.append((p_ref.at[plane_of(par, 3)], a_hbm.at[3]))
            for k, src in enumerate((c_ref, p_ref)):
                copies.append((src.at[:, 56:64], up_hbm.at[4 * k : 4 * k + 4]))
                copies.append((src.at[:, 0:8], down_hbm.at[4 * k : 4 * k + 4]))
            sends = begin(copies, sem, 8)
    act = act_ref[...]
    total = jnp.sum(jnp.transpose(volt_ref[...] * act), axis=0, keepdims=True)
    count = jnp.sum(jnp.transpose(act), axis=0, keepdims=True)
    cells = pair_sum(total) / jnp.maximum(pair_sum(count), 1.0)
    cell_ref[...] = cells
    note[...] = jnp.zeros((8, 1024), F32)
    note[0:1, 0:128] = cells
    sends += begin([(note, up_hbm.at[8]), (note, down_hbm.at[8])], sem, 20)
    for send in sends:
        send.wait()


def begin(copies, sem, start):
    made = [pltpu.make_async_copy(s, d, sem.at[start + n]) for n, (s, d) in enumerate(copies)]
    for m in made:
        m.start()
    return made


def ionic_kernel(cnt, typ, volt_ref, st_ref, rate_ref, out_ref, ion_ref):
    step = pl.program_id(0)
    cells = volt_ref.shape[0] // 2
    lane = iota((8, 128), 1)

    def body(group, carry):
        rows8 = pl.ds(pl.multiple_of(8 * group, 8), 8)
        volts = volt_ref[rows8, :]
        counts, types, v, active, cols = [], [], [], [], []
        for q in range(4):
            counts.append(cnt[step * cells + 4 * group + q])
            types.append(typ[step * cells + 4 * group + q])
        for r in range(8):
            v.append(jnp.broadcast_to(volts[r : r + 1], (8, 128)))
            active.append(lane + (r % 2) * 128 < counts[r // 2])
            cols.append(pl.ds(pl.multiple_of(1024 * group + 128 * r, 128), 128))
        w1, w2 = [None] * 8, [None] * 8
        for k in range(5):
            rows = slice(8 * k, 8 * k + 8)
            rate = [rate_ref[i, rows] for i in range(4)]
            for q in range(4):
                g, gr = rate_ref[4 + types[q], rows], rate_ref[7 + types[q], rows]
                for r in (2 * q, 2 * q + 1):
                    st = st_ref[rows, cols[r]]
                    opening = jnp.exp2(rate[0] * v[r] + rate[1])
                    closing = jnp.exp2(rate[2] * v[r] + rate[3])
                    total = opening + closing
                    rec = pl.reciprocal(total, approx=True)
                    rec = rec * (2.0 - total * rec)
                    steady = opening * rec
                    fresh = steady + (st - steady) * jnp.exp2(total * (-0.5 * LOG2E))
                    out_ref[rows, cols[r]] = jnp.where(active[r], fresh, st)
                    w1[r] = g * fresh if k == 0 else w1[r] + g * fresh
                    w2[r] = gr * fresh if k == 0 else w2[r] + gr * fresh
        act = jnp.concatenate([jnp.where(a, 1.0, 0.0)[0:1] for a in active], axis=0)
        ion = [jnp.sum(w1[r] * v[r] - w2[r], axis=0, keepdims=True) for r in range(8)]
        val = jnp.concatenate(ion, axis=0) * act
        ion_ref[rows8, :] = val

        return carry

    lax.fori_loop(0, cells // 4, body, 0)


def scatter_kernel(ion_ref, act_ref, in_ref, ex_ref, s_ref, n_ref):
    row_iota = iota((32, 512), 0)
    lane_iota = iota((128, 512), 0)
    low = iota((8, 128), 0) < 4
    odd_row = (iota((8, 128), 0) & 2) // 2

    def body(kk, carry):
        rows8 = pl.ds(pl.multiple_of(8 * kk, 8), 8)
        x = kk // 4
        val = ion_ref[rows8, :]
        act = act_ref[rows8, :]
        hi = val.astype(BF16).astype(F32)
        lo = val - hi
        mids, lanes = [], []
        for ref in (in_ref, ex_ref):
            o = ref[rows8, :] & 4095
            mids.append((((o >> 7) & 7) ^ odd_row) * 4 + (o >> 10))
            lanes.append(o & 127)

        def line(a, b, s):
            r = 2 * s
            return jnp.concatenate([a[r : r + 1], a[r + 1 : r + 2], b[r : r + 1], b[r + 1 : r + 2]], axis=1)

        for q in range(2):
            results = []
            for s in (2 * q, 2 * q + 1):
                hit = line(mids[0], mids[1], s) == row_iota
                left = jnp.concatenate(
                    [jnp.where(hit, line(piece, -piece, s), 0.0).astype(BF16) for piece in (hi, lo, act)], axis=0
                )
                right = jnp.where(line(lanes[0], lanes[1], s) == lane_iota, 1.0, 0.0).astype(BF16)
                out = lax.dot_general(left, right, (((1,), (1,)), ((), ())), preferred_element_type=F32)
                results.append((out[0:32] + out[32:64], out[64:96]))
            row = pl.ds(pl.multiple_of((2 * (kk % 4) + q) * 8, 8), 8)
            for dst, e, o in ((s_ref, results[0][0], results[1][0]), (n_ref, results[0][1], results[1][1])):
                for j in range(4):
                    ej, oj = e[8 * j : 8 * j + 8], o[8 * j : 8 * j + 8]
                    dst[x, row, 256 * j : 256 * j + 128] = jnp.where(low, ej, oj)
                    dst[x, row, 256 * j + 128 : 256 * j + 256] = pltpu.roll(jnp.where(low, oj, ej), 4, 0)
        return carry

    lax.fori_loop(0, 16, body, 0, unroll=4)


def edge_rows(meta, below, above):
    sub = iota((8, 1024), 0)
    bottom = (sub < 3) & (meta[2] != 3)
    top = (sub >= 5) & (meta[2] != 0)
    return jnp.where(bottom, above, jnp.where(top, below, 0.0))


def early_edge_kernel(meta, below_ref, above_ref, far_ref, cell_ref, after, y_ref, table_ref, a_ref, b_ref):
    par = meta[0]
    for x in range(8):
        y_ref[x] = edge_rows(meta, below_ref[x], above_ref[x])
    table = jnp.concatenate(
        [cell_ref[...], below_ref[8, 0:1, 0:128], far_ref[...], above_ref[8, 0:1, 0:128],
         jnp.zeros((4, 128), F32)], axis=0)
    table_ref[...] = table
    for i in range(2):
        a_ref[i] = y_ref[plane_of(par, 3 - i)]
        b_ref[i] = y_ref[plane_of(par, i)]
    for ref in (a_ref, b_ref):
        ref[2] = jnp.zeros((8, 1024), F32)
        ref[2, :, 0:128] = table


def late_edge_kernel(meta, below_ref, above_ref, after, y_ref, a_ref, b_ref):
    par = meta[0]
    for x in range(4):
        y_ref[x] = edge_rows(meta, below_ref[x], above_ref[x])
    for i in range(2):
        a_ref[i] = y_ref[plane_of(par, 3 - i)]
        b_ref[i] = y_ref[plane_of(par, i)]


def reader(par, own, a, b, y, ca=None, cb=None, own_y=0):
    def get(e, t):
        rows = slice(8 * t, 8 * t + 8)
        if 3 <= e <= 6:
            x = plane_of(par, e - 3)
            return own[x, rows, :] if t < 8 else y[own_y + x]
        halo, corner, i = (a, ca, e - 7) if e > 6 else (b, cb, 2 - e)
        return halo[i, rows, :] if t < 8 else corner[i]

    return get


def stored(*held):
    def get(e, t):
        for ref, start, stop in held:
            if start <= e < stop:
                return ref[e - start, 8 * t : 8 * t + 8, :]

    return get


class Plane:
    def __init__(self, get, e):
        self.get, self.e = get, e
        self.sub = iota((8, 1024), 0)
        self.kept = {}

    def turned(self, t, by, keep):
        found = self.kept.pop((t, by), None)
        if found is None:
            found = pltpu.roll(self.get(self.e, t), by, 0)
            if keep:
                self.kept[t, by] = found
        return found

    def views(self, t):
        get, e = self.get, self.e
        c = get(e, t)
        ym = jnp.where(self.sub == 0, self.turned((t + 8) % 9, 1, False), self.turned(t, 1, True))
        yp = jnp.where(self.sub == 7, self.turned((t + 1) % 9, 7, t < 8), self.turned(t, 7, False))
        return c, get(e - 1, t), get(e + 1, t), ym, yp, pltpu.roll(c, 1, 1), pltpu.roll(c, 1023, 1)


def inverse(x):
    rec = pl.reciprocal(x, approx=True)
    return rec * (2.0 - x * rec)


def couplings(plane, t):
    lane = iota((8, 1024), 1)
    c, xm, xp, ym, yp, zm, zp = plane.views(t)
    first, last = lane == 0, lane == 1023
    c = 0.25 * c
    xm, xp, ym, yp = (c + 0.25 * other for other in (xm, xp, ym, yp))
    zm = c + 0.25 * jnp.where(first, 0.0, zm)
    zp = c + 0.25 * jnp.where(last, 0.0, zp)
    inv = inverse(1.0 + (((xm + xp) + (ym + yp)) + (zm + zp)))
    return (xm, xp, ym, yp, jnp.where(first, 0.0, zm), jnp.where(last, 0.0, zp)), inv


def weighted(fs, views):
    t = [f * v for f, v in zip(fs, views)]
    return ((t[0] + t[1]) + (t[2] + t[3])) + (t[4] + t[5])


def prepare_kernel(meta, p_ref, c_ref, a_ref, b_ref, y_ref, s_ref, n_ref, w_ref, k_ref):
    par = meta[0]
    conduct = reader(par, c_ref, a_ref, b_ref, y_ref)
    own = reader(par, p_ref, a_ref.at[3:4], b_ref.at[3:4], y_ref, own_y=4)
    for e in range(3, 7):
        x = plane_of(par, e - 3)
        pc, pp = Plane(conduct, e), Plane(own, e)
        for t in range(8):
            rows = slice(8 * t, 8 * t + 8)
            fs, inv = couplings(pc, t)
            p, *views = pp.views(t)
            w_ref[x, rows, :] = (p + weighted(fs, views) - 0.5 * s_ref[x, rows, :]) * inv - p
            k_ref[x, rows, :] = (-0.5 * inv) * n_ref[x, rows, :]


def gap_kernel(meta, table_ref, ta_ref, tb_ref, part_ref, cond_ref, ion_ref, act_ref, w_ref, k_ref,
               u_ref, a_ref, b_ref, up_ref, down_ref, mem_ref, spread):
    par, mine, v = meta[0], meta[2], meta[3]
    part = part_ref[...]
    brick = part >> 6
    bx, by = brick >> 2, brick & 3
    side = jnp.where(bx == v, 0, jnp.where(bx == (v ^ 1), 1, 2))
    row = side * 4 + ((mine - by) & 3)
    lane = (part & 63) * 2
    tables = (table_ref[...], ta_ref[2, :, 0:128], tb_ref[2, :, 0:128])
    other = jnp.zeros((8, 128), F32)
    for r in range(12):
        line = jnp.broadcast_to(tables[r // 4][r % 4 : r % 4 + 1], (8, 128))
        other = jnp.where(row == r, jnp.take_along_axis(line, lane, axis=1, mode="promise_in_bounds"), other)
    own = tables[0][0:1]
    current = jnp.sum(cond_ref[...] * (own - other), axis=0, keepdims=True)
    act = act_ref[...]
    count = pair_sum(jnp.sum(jnp.transpose(act), axis=0, keepdims=True))
    g = current / jnp.maximum(count, 1.0)
    g8 = jnp.broadcast_to(g, (8, 128))
    mem_ref[...] = ion_ref[...] + act * jnp.transpose(jnp.broadcast_to(g, (128, 128)))
    for half in range(2):
        at = 64 * half + 2 * (iota((8, 128), 1) // 4)
        wide = jnp.take_along_axis(g8, at, axis=1, mode="promise_in_bounds")[0:1]
        spread[128 * half : 128 * half + 128, :] = jnp.transpose(jnp.broadcast_to(wide, (128, 128)))
    for j in range(4):
        x = plane_of(par, j)
        for t in range(8):
            rows = slice(8 * t, 8 * t + 8)
            gt = jnp.tile(spread[pl.ds(pl.multiple_of(x * 64 + 8 * t, 8), 8), :], (1, 8))
            u = w_ref[x, rows, :] + k_ref[x, rows, :] * gt
            u_ref[x, rows, :] = u
            if t == 0:
                down_ref[x] = u
            if t == 7:
                up_ref[x] = u
            if j < 3:
                b_ref[j, rows, :] = u
            if j > 0:
                a_ref[3 - j, rows, :] = u


def operator_kernel(meta, c_ref, a_ref, b_ref, y_ref, ca_ref, cb_ref, after, fx, fym, fyp, fzm, fzp, inv_ref):
    par, has_b, mine = meta[0], meta[1], meta[2]
    conduct = reader(par, c_ref, a_ref, b_ref, y_ref, ca_ref, cb_ref)
    sub = iota((8, 1024), 0)
    bottom = (sub < 3) & (mine != 3)
    top = (sub >= 5) & (mine != 0)
    keep = jnp.where(bottom | top, 1.0, 0.0)
    inside = jnp.where(has_b == 1, 1.0, 0.0)
    for e in range(1, 9):
        plane = Plane(conduct, e)
        for t in range(8 if e in (1, 8) else 9):
            rows = slice(8 * t, 8 * t + 8)
            fs, inv = couplings(plane, t)
            if e < 3:
                inv = inv * inside
            inv_ref[e - 1, rows, :] = inv * keep if t == 8 else inv
            if e == 1 or (e == 2 and t == 8):
                fx[e - 1, rows, :] = fs[0]
            fx[e, rows, :] = fs[1]
            for ref, f in zip((fym, fyp, fzm, fzp), fs[2:]):
                ref[e - 1, rows, :] = f


def coupled(coef, get, plane, t):
    fx, fym, fyp, fzm, fzp, inv = coef
    e = plane.e
    rows = slice(8 * t, 8 * t + 8)
    fs = [fx[e - 1, rows, :], fx[e, rows, :]] + [f[e - 1, rows, :] for f in (fym, fyp, fzm, fzp)]
    u, *views = plane.views(t)
    return u, inv[e - 1, rows, :] * weighted(fs, views)


def put(held, e, t, value):
    for ref, start, stop in held:
        if start <= e < stop:
            ref[e - start, 8 * t : 8 * t + 8, :] = value


def step_one(coef, u0, e, r_held, u1_held):
    a, b = sweep_factors()[0]
    plane = Plane(u0, e)
    for t in range(8 if e in (1, 8) else 9):
        u, res = coupled(coef, u0, plane, t)
        put(r_held, e, t, res)
        put(u1_held, e, t, a * u + b * res)


def step_two(coef, u1, r, e, r_held, u2_held):
    a, b = sweep_factors()[1]
    plane = Plane(u1, e)
    for t in range(8 if e in (2, 7) else 9):
        u, more = coupled(coef, u1, plane, t)
        res = (r(e, t) - u) + more
        put(r_held, e, t, res)
        put(u2_held, e, t, a * u + b * res)


def step_three(coef, p_ref, u0, u1, u2, r, e, x, out_ref, at):
    a, b = sweep_factors()[2]
    plane = Plane(u2, e)
    for t in range(8):
        rows = slice(8 * t, 8 * t + 8)
        u, more = coupled(coef, u2, plane, t)
        res = (r(e, t) - u) + more
        before = (p_ref[x, rows, :] + u0(e, t)) + (u1(e, t) + u)
        out_ref[at, rows, :] = before + (a * u + b * res)


def near_kernel(meta, p_ref, fx, fym, fyp, fzm, fzp, inv, u_ref, a_ref, y_ref, ca_ref,
                u1_out, r_out, u2_out, done_ref, u1_far, r_far, u2_far):
    par = meta[0]
    coef = (fx, fym, fyp, fzm, fzp, inv)
    u0 = reader(par, u_ref, a_ref, None, y_ref, ca_ref)
    u1_held = ((u1_out, 4, 6), (u1_far, 6, 9))
    r1_held = ((r_out, 4, 5), (r_far, 5, 8))
    r2_held = ((r_out.at[1:2], 5, 6), (r_far.at[1:2], 6, 7))
    u2_held = ((u2_out, 5, 7), (u2_far, 7, 8))
    for e in (8, 7, 6, 5, 4):
        step_one(coef, u0, e, r1_held, u1_held)
    for e in (7, 6, 5):
        step_two(coef, stored(*u1_held), stored(*r1_held), e, r2_held, u2_held)
    step_three(coef, p_ref, u0, stored(*u1_held), stored(*u2_held), stored(*r2_held), 6, plane_of(par, 3), done_ref, 0)


def far_kernel(meta, p_ref, fx, fym, fyp, fzm, fzp, inv, u_ref, b_ref, y_ref, cb_ref, u1_in, r_in, u2_in, done_ref,
               out_ref, u1_far, r_far, u2_far):
    par = meta[0]
    coef = (fx, fym, fyp, fzm, fzp, inv)
    u0 = reader(par, u_ref, None, b_ref, y_ref, None, cb_ref)
    u1_new = ((u1_far, 1, 4),)
    u1 = stored(*u1_new, (u1_in, 4, 6))
    r1_new = ((r_far, 2, 4),)
    r1 = stored(*r1_new, (r_in, 4, 5))
    r2_new = ((r_far.at[2:4], 3, 5),)
    r2 = stored(*r2_new, (r_in.at[1:2], 5, 6))
    u2_new = ((u2_far, 2, 5),)
    u2 = stored(*u2_new, (u2_in, 5, 7))
    for e in (1, 2, 3):
        step_one(coef, u0, e, r1_new, u1_new)
    for e in (2, 3, 4):
        step_two(coef, u1, r1, e, r2_new, u2_new)
    for e in (3, 4, 5):
        x = plane_of(par, e - 3)
        step_three(coef, p_ref, u0, u1, u2, r2, e, x, out_ref, x)
    out_ref[plane_of(par, 3)] = done_ref[0]


def shape(*dims, kind=F32):
    return jax.ShapeDtypeStruct(dims, kind)


def per_device(potential, conductivity, ion_states, rate_scale, rate_slope, type_cond, reversal,
               facet_counts, intra_voxel, extra_voxel, cell_type, gap_partner, gap_cond):
    v, m = lax.axis_index("vol"), lax.axis_index("mem")
    par = v & 1
    nv = lax.axis_size("vol")
    has_b = jnp.where((v == 0) | (v == nv - 1), 0, 1)
    meta = jnp.stack([par, has_b, m, v]).astype(jnp.int32)
    swap_a = [pair for i in range(0, nv, 2) for pair in ((i, i + 1), (i + 1, i))]
    swap_b = [pair for i in range(1, nv - 1, 2) for pair in ((i, i + 1), (i + 1, i))]
    on_mem = lambda x, pairs: lax.ppermute(x, "mem", pairs)
    ring = lambda d: [(i, (i + d) % 4) for i in range(4)]
    to_a = functools.partial(lax.ppermute, axis_name="vol", perm=swap_a)
    to_b = functools.partial(lax.ppermute, axis_name="vol", perm=swap_b)

    intra = intra_voxel.reshape(128, 128)
    extra = extra_voxel.reshape(128, 128)

    volt, cells, act, part_lane, cond_lane, send_a, send_b, send_up, send_down = pl.pallas_call(
        gather_kernel,
        out_shape=(shape(128, 128), shape(1, 128), shape(128, 128), shape(8, 128, kind=jnp.int32), shape(8, 128),
                   shape(4, 64, 1024), shape(4, 64, 1024), shape(9, 8, 1024), shape(9, 8, 1024)),
        in_specs=[SM, SM, HBM, HBM] + [VM] * 4,
        out_specs=(VM,) * 5 + (ANY,) * 4,
        scratch_shapes=[pltpu.VMEM((4, 64, 1024), F32), pltpu.VMEM((4, 64, 1024), F32), pltpu.VMEM((8, 1024), F32),
                        pltpu.SemaphoreType.DMA((22,))],
        compiler_params=grant(60),
        cost_estimate=pl.CostEstimate(flops=4000000, bytes_accessed=5000000, transcendentals=0),
        name="voltages",
    )(meta, facet_counts, potential, conductivity, intra, extra, gap_partner.T, gap_cond.T)

    below, above, far = on_mem(send_up, ring(1)), on_mem(send_down, ring(3)), on_mem(cells, ring(2))
    early_b, early_a = to_b(send_b), to_a(send_a)

    rates = jnp.concatenate([
        jnp.stack([rate_slope[0] * LOG2E, jnp.log2(rate_scale[0]), rate_slope[1] * (-LOG2E), jnp.log2(rate_scale[1])]),
        type_cond, type_cond * reversal[None, :]], axis=0)
    rates = jnp.broadcast_to(rates[:, :, None], (10, 40, 128))
    steps = 4
    width = 16384 // steps
    facet_rows = pl.BlockSpec((128 // steps, 128), lambda i, *_: (i, 0))
    state_block = pl.BlockSpec((40, width), lambda i, *_: (0, i))
    states_next, ion = pl.pallas_call(
        ionic_kernel,
        out_shape=(shape(40, 16384), shape(128, 128)),
        grid_spec=pltpu.PrefetchScalarGridSpec(
            num_scalar_prefetch=2,
            grid=(steps,),
            in_specs=[facet_rows, state_block, pl.BlockSpec((10, 40, 128), lambda i, *_: (0, 0, 0))],
            out_specs=(state_block, facet_rows),
        ),
        compiler_params=grant(60),
        cost_estimate=pl.CostEstimate(flops=16000000, bytes_accessed=7300000, transcendentals=2600000),
        name="ionic",
    )(facet_counts, cell_type, volt, ion_states, rates)

    source, count = pl.pallas_call(
        scatter_kernel,
        out_shape=(shape(4, 64, 1024), shape(4, 64, 1024)),
        in_specs=[VM] * 4,
        out_specs=(VM, VM),
        compiler_params=grant(8),
        cost_estimate=pl.CostEstimate(flops=800000000, bytes_accessed=2300000, transcendentals=0),
        name="scatter",
    )(ion, act, intra, extra)

    y_early, table, more_a, more_b = pl.pallas_call(
        early_edge_kernel,
        out_shape=(shape(8, 8, 1024), shape(8, 128), shape(3, 8, 1024), shape(3, 8, 1024)),
        in_specs=[SM] + [VM] * 4 + [ANY],
        out_specs=(VM,) * 4,
        compiler_params=grant(6),
        cost_estimate=pl.CostEstimate(flops=300000, bytes_accessed=1000000, transcendentals=0),
        name="early_edges",
    )(meta, below, above, far, cells, source)
    more_b, more_a = to_b(more_b), to_a(more_a)

    w, k = pl.pallas_call(
        prepare_kernel,
        out_shape=(shape(4, 64, 1024), shape(4, 64, 1024)),
        in_specs=[SM] + [VM] * 7,
        out_specs=(VM, VM),
        compiler_params=grant(20),
        cost_estimate=pl.CostEstimate(flops=16000000, bytes_accessed=8000000, transcendentals=0),
        name="prepare",
    )(meta, potential, conductivity, early_a, early_b, y_early, source, count)

    u, u_a, u_b, u_up, u_down, membrane = pl.pallas_call(
        gap_kernel,
        out_shape=(shape(4, 64, 1024), shape(3, 64, 1024), shape(3, 64, 1024), shape(4, 8, 1024),
                   shape(4, 8, 1024), shape(128, 128)),
        in_specs=[SM] + [VM] * 9,
        out_specs=(VM,) * 6,
        scratch_shapes=[pltpu.VMEM((256, 128), F32)],
        compiler_params=grant(12),
        cost_estimate=pl.CostEstimate(flops=1000000, bytes_accessed=5000000, transcendentals=0),
        name="gap",
    )(meta, table, more_a, more_b, part_lane, cond_lane, ion, act, w, k)

    late_b = to_b(u_b)
    low_rows = on_mem(u_up, [(i, i + 1) for i in range(3)])
    high_rows = on_mem(u_down, [(i + 1, i) for i in range(3)])
    late_a = to_a(u_a)

    big = lambda n: pltpu.VMEM((n, 72, 1024), F32)
    operator = pl.pallas_call(
        operator_kernel,
        out_shape=(shape(9, 72, 1024),) + (shape(8, 72, 1024),) * 5,
        in_specs=[SM] + [VM] * 6 + [ANY],
        out_specs=(VM,) * 6,
        compiler_params=grant(22),
        cost_estimate=pl.CostEstimate(flops=16000000, bytes_accessed=17000000, transcendentals=0),
        name="operator",
    )(meta, conductivity, early_a, early_b, y_early, more_a, more_b, u_up)

    y_late, corner_a, corner_b = pl.pallas_call(
        late_edge_kernel,
        out_shape=(shape(4, 8, 1024), shape(2, 8, 1024), shape(2, 8, 1024)),
        in_specs=[SM, VM, VM, ANY],
        out_specs=(VM,) * 3,
        compiler_params=grant(4),
        cost_estimate=pl.CostEstimate(flops=100000, bytes_accessed=500000, transcendentals=0),
        name="late_edges",
    )(meta, low_rows, high_rows, operator[-1])
    corner_b, corner_a = to_b(corner_b), to_a(corner_a)

    u1, r, u2, done = pl.pallas_call(
        near_kernel,
        out_shape=(shape(2, 72, 1024), shape(2, 72, 1024), shape(2, 72, 1024), shape(1, 64, 1024)),
        in_specs=[SM] + [VM] * 11,
        out_specs=(VM,) * 4,
        scratch_shapes=[big(3), big(3), big(1)],
        compiler_params=grant(30),
        cost_estimate=pl.CostEstimate(flops=25000000, bytes_accessed=10000000, transcendentals=0),
        name="near",
    )(meta, potential, *operator, u, late_a, y_late, corner_a)

    potential_next = pl.pallas_call(
        far_kernel,
        out_shape=shape(4, 64, 1024),
        in_specs=[SM] + [VM] * 15,
        out_specs=VM,
        scratch_shapes=[big(3), big(4), big(3)],
        compiler_params=grant(30),
        cost_estimate=pl.CostEstimate(flops=25000000, bytes_accessed=10000000, transcendentals=0),
        name="far",
    )(meta, potential, *operator, u, late_b, y_late, corner_b, u1, r, u2, done)
    return potential_next, states_next, membrane.reshape(16384)


def solution(mesh):
    in_specs = (
        P("vol", "mem", None), P("vol", "mem", None), P(None, ("vol", "mem")),
        P(), P(), P(), P(),
        P(("vol", "mem")), P(("vol", "mem")), P(("vol", "mem")), P(("vol", "mem")),
        P(("vol", "mem"), None), P(("vol", "mem"), None),
    )
    out_specs = (P("vol", "mem", None), P(None, ("vol", "mem")), P(("vol", "mem")))
    return jax.shard_map(per_device, mesh=mesh, in_specs=in_specs, out_specs=out_specs, check_vma=False)
```

```python
import functools

import jax
import jax.numpy as jnp
from jax import lax
from jax.experimental import pallas as pl
from jax.experimental.pallas import tpu as pltpu
from jax.sharding import PartitionSpec as P

SWEEPS = 4
F32 = jnp.float32
BF16 = jnp.bfloat16
ANY = pl.BlockSpec(memory_space=pl.ANY)
HBM = pl.BlockSpec(memory_space=pltpu.HBM)
VM = pl.BlockSpec(memory_space=pltpu.VMEM)
SM = pl.BlockSpec(memory_space=pltpu.SMEM)


def grant(mib):
    return pltpu.CompilerParams(vmem_limit_bytes=mib * 1024 * 1024)


def sweep_factors():
    theta, delta = 1.0, 0.8
    sigma = theta / delta
    rho = 1.0 / sigma
    factors = []
    for _ in range(SWEEPS - 1):
        rho_next = 1.0 / (2.0 * sigma - rho)
        factors.append((rho_next * rho, 2.0 * rho_next / delta))
        rho = rho_next
    return factors


def iota(shape, dim):
    return lax.broadcasted_iota(jnp.int32, shape, dim)


def place():
    v, mine = lax.axis_index("vol"), lax.axis_index("mem")
    return v & 1, (v != 0) & (v != lax.axis_size("vol") - 1), mine, v


def plane_of(parity, j):
    return j + parity * (3 - 2 * j)


def pair_sum(row):
    even = (iota((1, 128), 1) & 1) == 0
    return row + jnp.where(even, pltpu.roll(row, 127, 1), pltpu.roll(row, 1, 1))


def gather_kernel(cnt, p_hbm, c_hbm, in_hbm, ex_hbm, part_hbm, cond_hbm, st_hbm,
                  st_near, volt_hbm, cell_hbm, act_hbm, part_out, cond_out, a_hbm, b_hbm, up_hbm, down_hbm,
                  p_ref, c_ref, in_ref, ex_ref, part_ref, cond_ref, volt_ref, cell_ref, act_ref, part_two, cond_two,
                  note, sem):
    par, has_b, mine, v = place()
    loads = begin(
        [(in_hbm, in_ref), (ex_hbm, ex_ref)] + [(p_hbm.at[x], p_ref.at[x]) for x in range(4)]
        + [(c_hbm.at[x], c_ref.at[x]) for x in range(4)] + [(part_hbm, part_ref), (cond_hbm, cond_ref)], sem, 0)
    states = begin([(st_hbm.at[:, 4096 * i : 4096 * i + 4096], st_near.at[:, 4096 * i : 4096 * i + 4096]) for i in range(4)], sem, 31)
    twice = iota((8, 128), 1) // 2
    sub = iota((8, 128), 0)
    low = sub < 4
    lane_row = iota((1, 128), 1)

    def body(kk, carry):
        x = kk // 4
        blocks = [r[pl.ds(pl.multiple_of(8 * kk, 8), 8), :] & 4095 for r in (in_ref, ex_ref)]
        for q in range(2):
            row = pl.multiple_of((2 * (kk % 4) + q) * 8, 8)
            tiles = [p_ref[x, pl.ds(row, 8), 128 * z : 128 * z + 128] for z in range(8)]
            for h in range(2):
                picked = []
                for block in blocks:
                    a = jnp.broadcast_to(block[4 * q + h : 4 * q + h + 1], (8, 128))
                    b = jnp.broadcast_to(block[4 * q + 2 + h : 4 * q + 3 + h], (8, 128))
                    o = jnp.where(low, a, b)
                    lane = o & 127
                    z_of = (o >> 7) & 7
                    got = jnp.take_along_axis(tiles[0], lane, axis=1, mode="promise_in_bounds")
                    for z in range(1, 8):
                        new = jnp.take_along_axis(tiles[z], lane, axis=1, mode="promise_in_bounds")
                        got = jnp.where(z_of == z, new, got)
                    picked.append(jnp.where((o >> 10) == (sub & 3), got, 0.0))
                d = picked[0] - picked[1]
                d = d + pltpu.roll(d, 7, 0)
                d = d + pltpu.roll(d, 6, 0)
                for i in range(2):
                    at = pl.ds(8 * kk + 4 * q + 2 * i + h, 1)
                    volt_ref[at, :] = d[4 * i : 4 * i + 1]
                    used = lane_row + 128 * h < cnt[4 * kk + 2 * q + i]
                    act_ref[at, :] = jnp.where(used, 1.0, 0.0)
        return carry

    loads[0].wait()
    loads[1].wait()
    for x in range(4):
        if x < 2:
            loads[2 + x].wait()
        lax.fori_loop(4 * x, 4 * x + 4, body, 0, unroll=4)
        if x == 1:
            for load in loads[4:]:
                load.wait()
            copies = []
            for i in range(3):
                copies.append((c_ref.at[plane_of(par, i)], b_hbm.at[i]))
                copies.append((c_ref.at[plane_of(par, 3 - i)], a_hbm.at[i]))
            copies.append((p_ref.at[plane_of(par, 0)], b_hbm.at[3]))
            copies.append((p_ref.at[plane_of(par, 3)], a_hbm.at[3]))
            for k, src in enumerate((c_ref, p_ref)):
                copies.append((src.at[:, 56:64], up_hbm.at[4 * k : 4 * k + 4]))
                copies.append((src.at[:, 0:8], down_hbm.at[4 * k : 4 * k + 4]))
            for src, dst in ((part_ref, part_two), (cond_ref, cond_two)):
                wide = jnp.concatenate([src[...], src[...]], axis=1)
                dst[...] = jnp.take_along_axis(wide, twice, axis=1, mode="promise_in_bounds")
            copies += [(part_two, part_out), (cond_two, cond_out)]
            sends = begin(copies, sem, 12)
    sends += begin([(volt_ref, volt_hbm), (act_ref, act_hbm)], sem, 26)
    act = act_ref[...]
    total = jnp.sum(jnp.transpose(volt_ref[...] * act), axis=0, keepdims=True)
    count = jnp.sum(jnp.transpose(act), axis=0, keepdims=True)
    cells = pair_sum(total) / jnp.maximum(pair_sum(count), 1.0)
    cell_ref[...] = cells
    note[...] = jnp.zeros((8, 1024), F32)
    note[0:1, 0:128] = cells
    sends += begin([(note, up_hbm.at[8]), (note, down_hbm.at[8]), (cell_ref, cell_hbm)], sem, 28)
    for send in sends + states:
        send.wait()


def begin(copies, sem, start):
    made = [pltpu.make_async_copy(s, d, sem.at[start + n]) for n, (s, d) in enumerate(copies)]
    for m in made:
        m.start()
    return made


CHUNKS = 16
ROOM = 24000000


def ionic_kernel(cnt, typ, volt_ref, act_ref, in_ref, ex_ref, scale_ref, slope_ref, cond_ref, rev_ref, st_ref,
                 out_hbm, ion_ref, s_ref, n_ref, out_ref, flat, rate_ref, sem):
    width = 16384 // CHUNKS
    at = lambda i: pl.ds(pl.multiple_of(i * width, width), width)
    store = lambda i: pltpu.make_async_copy(out_ref.at[:, at(i)], out_hbm.at[:, at(i)], sem.at[i])
    flat[...] = jnp.zeros((128, 128), F32)
    logs = jnp.log(scale_ref[...])
    flat[0:1, 0:40] = slope_ref[0:1]
    flat[1:2, 0:40] = logs[0:1]
    flat[2:3, 0:40] = -slope_ref[1:2]
    flat[3:4, 0:40] = logs[1:2]
    flat[4:7, 0:40] = cond_ref[...]
    flat[7:10, 0:40] = cond_ref[...] * rev_ref[...]
    turned = jnp.transpose(flat[...])
    for i in range(10):
        rate_ref[i] = jnp.broadcast_to(turned[0:40, i : i + 1], (40, 128))
    lane = iota((8, 128), 1)
    row_iota = iota((32, 512), 0)
    lane_iota = iota((128, 512), 0)
    low = iota((8, 128), 0) < 4
    odd_row = (iota((8, 128), 0) & 2) // 2

    def body(group, carry):
        rows8 = pl.ds(pl.multiple_of(8 * group, 8), 8)
        volts = volt_ref[rows8, :]
        counts, types, v, active, cols = [], [], [], [], []
        for q in range(4):
            counts.append(cnt[4 * group + q])
            types.append(typ[4 * group + q])
        for r in range(8):
            v.append(jnp.broadcast_to(volts[r : r + 1], (8, 128)))
            active.append(lane + (r % 2) * 128 < counts[r // 2])
            cols.append(pl.ds(pl.multiple_of(1024 * group + 128 * r, 128), 128))
        w1, w2 = [None] * 8, [None] * 8
        for k in range(5):
            rows = slice(8 * k, 8 * k + 8)
            rate = [rate_ref[i, rows] for i in range(4)]
            for q in range(4):
                g, gr = rate_ref[4 + types[q], rows], rate_ref[7 + types[q], rows]
                for r in (2 * q, 2 * q + 1):
                    st = st_ref[rows, cols[r]]
                    opening = jnp.exp(rate[0] * v[r] + rate[1])
                    closing = jnp.exp(rate[2] * v[r] + rate[3])
                    total = opening + closing
                    steady = opening * inverse(total)
                    fresh = steady + (st - steady) * jnp.exp(total * -0.5)
                    out_ref[rows, cols[r]] = jnp.where(active[r], fresh, st)
                    w1[r] = g * fresh if k == 0 else w1[r] + g * fresh
                    w2[r] = gr * fresh if k == 0 else w2[r] + gr * fresh
        store(group).start()
        act = act_ref[rows8, :]
        ion = [jnp.sum(w1[r] * v[r] - w2[r], axis=0, keepdims=True) for r in range(8)]
        val = jnp.concatenate(ion, axis=0) * act
        ion_ref[rows8, :] = val

        x = group // 4
        hi = val.astype(BF16).astype(F32)
        lo = val - hi
        mids, lanes = [], []
        for ref in (in_ref, ex_ref):
            o = ref[rows8, :] & 4095
            mids.append((((o >> 7) & 7) ^ odd_row) * 4 + (o >> 10))
            lanes.append(o & 127)

        def line(a, b, s):
            r = 2 * s
            return jnp.concatenate([a[r : r + 1], a[r + 1 : r + 2], b[r : r + 1], b[r + 1 : r + 2]], axis=1)

        for q in range(2):
            results = []
            for s in (2 * q, 2 * q + 1):
                hit = line(mids[0], mids[1], s) == row_iota
                left = jnp.concatenate(
                    [jnp.where(hit, line(piece, -piece, s), 0.0).astype(BF16) for piece in (hi, lo, act)], axis=0
                )
                right = jnp.where(line(lanes[0], lanes[1], s) == lane_iota, 1.0, 0.0).astype(BF16)
                out = lax.dot_general(left, right, (((1,), (1,)), ((), ())), preferred_element_type=F32)
                results.append((out[0:32] + out[32:64], out[64:96]))
            row = pl.ds(pl.multiple_of((2 * (group % 4) + q) * 8, 8), 8)
            for dst, e, o in ((s_ref, results[0][0], results[1][0]), (n_ref, results[0][1], results[1][1])):
                for j in range(4):
                    ej, oj = e[8 * j : 8 * j + 8], o[8 * j : 8 * j + 8]
                    dst[x, row, 256 * j : 256 * j + 128] = jnp.where(low, ej, oj)
                    dst[x, row, 256 * j + 128 : 256 * j + 256] = pltpu.roll(jnp.where(low, oj, ej), 4, 0)
        return carry

    lax.fori_loop(0, CHUNKS, body, 0, unroll=2)
    for i in range(CHUNKS):
        store(i).wait()


def edge_rows(mine, below, above):
    sub = iota((8, 1024), 0)
    bottom = (sub < 3) & (mine != 3)
    top = (sub >= 5) & (mine != 0)
    return jnp.where(bottom, above, jnp.where(top, below, 0.0))


def early_edge_kernel(below_ref, above_ref, far_ref, cell_ref, after, y_ref, table_ref, a_ref, b_ref):
    par, has_b, mine, v = place()
    for x in range(8):
        y_ref[x] = edge_rows(mine, below_ref[x], above_ref[x])
    table = jnp.concatenate(
        [cell_ref[...], below_ref[8, 0:1, 0:128], far_ref[...], above_ref[8, 0:1, 0:128],
         jnp.zeros((4, 128), F32)], axis=0)
    table_ref[...] = table
    for i in range(2):
        a_ref[i] = y_ref[plane_of(par, 3 - i)]
        b_ref[i] = y_ref[plane_of(par, i)]
    for ref in (a_ref, b_ref):
        ref[2] = jnp.zeros((8, 1024), F32)
        ref[2, :, 0:128] = table


def late_edge_kernel(below_ref, above_ref, after, y_ref, a_ref, b_ref):
    par, has_b, mine, v = place()
    for x in range(4):
        y_ref[x] = edge_rows(mine, below_ref[x], above_ref[x])
    for i in range(2):
        a_ref[i] = y_ref[plane_of(par, 3 - i)]
        b_ref[i] = y_ref[plane_of(par, i)]


def reader(par, own, a, b, y, ca=None, cb=None, own_y=0):
    def get(e, t):
        rows = slice(8 * t, 8 * t + 8)
        if 3 <= e <= 6:
            x = plane_of(par, e - 3)
            return own[x, rows, :] if t < 8 else y[own_y + x]
        halo, corner, i = (a, ca, e - 7) if e > 6 else (b, cb, 2 - e)
        return halo[i, rows, :] if t < 8 else corner[i]

    return get


def stored(*held):
    def get(e, t):
        for ref, start, stop in held:
            if start <= e < stop:
                return ref[e - start, 8 * t : 8 * t + 8, :]

    return get


class Plane:
    def __init__(self, get, e):
        self.get, self.e = get, e
        self.sub = iota((8, 1024), 0)
        self.kept = {}

    def turned(self, t, by, keep):
        found = self.kept.pop((t, by), None)
        if found is None:
            found = pltpu.roll(self.get(self.e, t), by, 0)
            if keep:
                self.kept[t, by] = found
        return found

    def views(self, t):
        get, e = self.get, self.e
        c = get(e, t)
        ym = jnp.where(self.sub == 0, self.turned((t + 8) % 9, 1, False), self.turned(t, 1, True))
        yp = jnp.where(self.sub == 7, self.turned((t + 1) % 9, 7, t < 8), self.turned(t, 7, False))
        return c, get(e - 1, t), get(e + 1, t), ym, yp, pltpu.roll(c, 1, 1), pltpu.roll(c, 1023, 1)


def inverse(x):
    rec = pl.reciprocal(x, approx=True)
    return rec * (2.0 - x * rec)


def couplings(plane, t):
    lane = iota((8, 1024), 1)
    c, xm, xp, ym, yp, zm, zp = plane.views(t)
    first, last = lane == 0, lane == 1023
    c = 0.25 * c
    xm, xp, ym, yp = (c + 0.25 * other for other in (xm, xp, ym, yp))
    zm = c + 0.25 * jnp.where(first, 0.0, zm)
    zp = c + 0.25 * jnp.where(last, 0.0, zp)
    inv = inverse(1.0 + (((xm + xp) + (ym + yp)) + (zm + zp)))
    return (xm, xp, ym, yp, jnp.where(first, 0.0, zm), jnp.where(last, 0.0, zp)), inv


def weighted(fs, views):
    t = [f * v for f, v in zip(fs, views)]
    return ((t[0] + t[1]) + (t[2] + t[3])) + (t[4] + t[5])


def prepare_kernel(p_ref, c_ref, a_ref, b_ref, y_ref, s_ref, n_ref, w_ref, k_ref):
    par, has_b, mine, v = place()
    conduct = reader(par, c_ref, a_ref, b_ref, y_ref)
    own = reader(par, p_ref, a_ref.at[3:4], b_ref.at[3:4], y_ref, own_y=4)
    for e in range(3, 7):
        x = plane_of(par, e - 3)
        pc, pp = Plane(conduct, e), Plane(own, e)
        for t in range(8):
            rows = slice(8 * t, 8 * t + 8)
            fs, inv = couplings(pc, t)
            p, *views = pp.views(t)
            w_ref[x, rows, :] = (p + weighted(fs, views) - 0.5 * s_ref[x, rows, :]) * inv - p
            k_ref[x, rows, :] = (-0.5 * inv) * n_ref[x, rows, :]


def gap_kernel(table_ref, ta_ref, tb_ref, part_ref, cond_ref, ion_ref, act_ref, w_ref, k_ref,
               u_ref, a_ref, b_ref, up_ref, down_ref, mem_ref, spread):
    par, has_b, mine, v = place()
    part = part_ref[...]
    brick = part >> 6
    bx, by = brick >> 2, brick & 3
    side = jnp.where(bx == v, 0, jnp.where(bx == (v ^ 1), 1, 2))
    row = side * 4 + ((mine - by) & 3)
    lane = (part & 63) * 2
    tables = (table_ref[...], ta_ref[2, :, 0:128], tb_ref[2, :, 0:128])
    other = jnp.zeros((8, 128), F32)
    for r in range(12):
        line = jnp.broadcast_to(tables[r // 4][r % 4 : r % 4 + 1], (8, 128))
        other = jnp.where(row == r, jnp.take_along_axis(line, lane, axis=1, mode="promise_in_bounds"), other)
    own = tables[0][0:1]
    current = jnp.sum(cond_ref[...] * (own - other), axis=0, keepdims=True)
    act = act_ref[...]
    count = pair_sum(jnp.sum(jnp.transpose(act), axis=0, keepdims=True))
    g = current / jnp.maximum(count, 1.0)
    g8 = jnp.broadcast_to(g, (8, 128))
    mem_ref[...] = ion_ref[...] + act * jnp.transpose(jnp.broadcast_to(g, (128, 128)))
    for half in range(2):
        at = 64 * half + 2 * (iota((8, 128), 1) // 4)
        wide = jnp.take_along_axis(g8, at, axis=1, mode="promise_in_bounds")[0:1]
        spread[128 * half : 128 * half + 128, :] = jnp.transpose(jnp.broadcast_to(wide, (128, 128)))
    for j in range(4):
        x = plane_of(par, j)
        for t in range(8):
            rows = slice(8 * t, 8 * t + 8)
            gt = jnp.tile(spread[pl.ds(pl.multiple_of(x * 64 + 8 * t, 8), 8), :], (1, 8))
            u = w_ref[x, rows, :] + k_ref[x, rows, :] * gt
            u_ref[x, rows, :] = u
            if t == 0:
                down_ref[x] = u
            if t == 7:
                up_ref[x] = u
            if j < 3:
                b_ref[j, rows, :] = u
            if j > 0:
                a_ref[3 - j, rows, :] = u


def operator_kernel(c_ref, a_ref, b_ref, y_ref, ca_ref, cb_ref, after, fx, fym, fyp, fzm, fzp, inv_ref):
    par, has_b, mine, v = place()
    conduct = reader(par, c_ref, a_ref, b_ref, y_ref, ca_ref, cb_ref)
    sub = iota((8, 1024), 0)
    bottom = (sub < 3) & (mine != 3)
    top = (sub >= 5) & (mine != 0)
    keep = jnp.where(bottom | top, 1.0, 0.0)
    inside = jnp.where(has_b, 1.0, 0.0)
    for e in range(1, 9):
        plane = Plane(conduct, e)
        for t in range(8 if e in (1, 8) else 9):
            rows = slice(8 * t, 8 * t + 8)
            fs, inv = couplings(plane, t)
            if e < 3:
                inv = inv * inside
            inv_ref[e - 1, rows, :] = inv * keep if t == 8 else inv
            if e == 1 or (e == 2 and t == 8):
                fx[e - 1, rows, :] = fs[0]
            fx[e, rows, :] = fs[1]
            for ref, f in zip((fym, fyp, fzm, fzp), fs[2:]):
                ref[e - 1, rows, :] = f


def coupled(coef, get, plane, t):
    fx, fym, fyp, fzm, fzp, inv = coef
    e = plane.e
    rows = slice(8 * t, 8 * t + 8)
    fs = [fx[e - 1, rows, :], fx[e, rows, :]] + [f[e - 1, rows, :] for f in (fym, fyp, fzm, fzp)]
    u, *views = plane.views(t)
    return u, inv[e - 1, rows, :] * weighted(fs, views)


def put(held, e, t, value):
    for ref, start, stop in held:
        if start <= e < stop:
            ref[e - start, 8 * t : 8 * t + 8, :] = value


def step_one(coef, u0, e, r_held, u1_held):
    a, b = sweep_factors()[0]
    plane = Plane(u0, e)
    for t in range(8 if e in (1, 8) else 9):
        u, res = coupled(coef, u0, plane, t)
        put(r_held, e, t, res)
        put(u1_held, e, t, a * u + b * res)


def step_two(coef, u1, r, e, r_held, u2_held):
    a, b = sweep_factors()[1]
    plane = Plane(u1, e)
    for t in range(8 if e in (2, 7) else 9):
        u, more = coupled(coef, u1, plane, t)
        res = (r(e, t) - u) + more
        put(r_held, e, t, res)
        put(u2_held, e, t, a * u + b * res)


def step_three(coef, p_ref, u0, u1, u2, r, e, x, out_ref, at):
    a, b = sweep_factors()[2]
    plane = Plane(u2, e)
    for t in range(8):
        rows = slice(8 * t, 8 * t + 8)
        u, more = coupled(coef, u2, plane, t)
        res = (r(e, t) - u) + more
        before = (p_ref[x, rows, :] + u0(e, t)) + (u1(e, t) + u)
        out_ref[at, rows, :] = before + (a * u + b * res)


def near_kernel(p_ref, fx, fym, fyp, fzm, fzp, inv, u_ref, a_ref, y_ref, ca_ref,
                u1_out, r_out, u2_out, done_ref, u1_far, r_far, u2_far):
    par, has_b, mine, v = place()
    coef = (fx, fym, fyp, fzm, fzp, inv)
    u0 = reader(par, u_ref, a_ref, None, y_ref, ca_ref)
    u1_held = ((u1_out, 4, 6), (u1_far, 6, 9))
    r1_held = ((r_out, 4, 5), (r_far, 5, 8))
    r2_held = ((r_out.at[1:2], 5, 6), (r_far.at[1:2], 6, 7))
    u2_held = ((u2_out, 5, 7), (u2_far, 7, 8))
    for e in (8, 7, 6, 5, 4):
        step_one(coef, u0, e, r1_held, u1_held)
    for e in (7, 6, 5):
        step_two(coef, stored(*u1_held), stored(*r1_held), e, r2_held, u2_held)
    step_three(coef, p_ref, u0, stored(*u1_held), stored(*u2_held), stored(*r2_held), 6, plane_of(par, 3), done_ref, 0)


def far_kernel(p_ref, fx, fym, fyp, fzm, fzp, inv, u_ref, b_ref, y_ref, cb_ref, u1_in, r_in, u2_in, done_ref,
               out_hbm, u1_far, r_far, u2_far, out_ref, sem):
    par, has_b, mine, v = place()
    coef = (fx, fym, fyp, fzm, fzp, inv)
    u0 = reader(par, u_ref, None, b_ref, y_ref, None, cb_ref)
    u1_new = ((u1_far, 1, 4),)
    u1 = stored(*u1_new, (u1_in, 4, 6))
    r1_new = ((r_far, 2, 4),)
    r1 = stored(*r1_new, (r_in, 4, 5))
    r2_new = ((r_far.at[2:4], 3, 5),)
    r2 = stored(*r2_new, (r_in.at[1:2], 5, 6))
    u2_new = ((u2_far, 2, 5),)
    u2 = stored(*u2_new, (u2_in, 5, 7))
    sends = begin([(done_ref.at[0], out_hbm.at[plane_of(par, 3)])], sem, 3)
    for e in (1, 2, 3):
        step_one(coef, u0, e, r1_new, u1_new)
    for e in (2, 3, 4):
        step_two(coef, u1, r1, e, r2_new, u2_new)
    for e in (3, 4, 5):
        x = plane_of(par, e - 3)
        step_three(coef, p_ref, u0, u1, u2, r2, e, x, out_ref, e - 3)
        sends += begin([(out_ref.at[e - 3], out_hbm.at[x])], sem, e - 3)
    for send in sends:
        send.wait()


def near(*dims, kind=F32):
    return pltpu.VMEM(dims, kind)


def shape(*dims, kind=F32):
    return jax.ShapeDtypeStruct(dims, kind)


def per_device(potential, conductivity, ion_states, rate_scale, rate_slope, type_cond, reversal,
               facet_counts, intra_voxel, extra_voxel, cell_type, gap_partner, gap_cond):
    nv = lax.axis_size("vol")
    swap_a = [pair for i in range(0, nv, 2) for pair in ((i, i + 1), (i + 1, i))]
    swap_b = [pair for i in range(1, nv - 1, 2) for pair in ((i, i + 1), (i + 1, i))]
    on_mem = lambda x, pairs: lax.ppermute(x, "mem", pairs)
    ring = lambda d: [(i, (i + d) % 4) for i in range(4)]
    to_a = functools.partial(lax.ppermute, axis_name="vol", perm=swap_a)
    to_b = functools.partial(lax.ppermute, axis_name="vol", perm=swap_b)

    intra = intra_voxel.reshape(128, 128)
    extra = extra_voxel.reshape(128, 128)

    states_near, volt, cells, act, part_lane, cond_lane, send_a, send_b, send_up, send_down = pl.pallas_call(
        gather_kernel,
        out_shape=(near(40, 16384), near(128, 128), near(1, 128), near(128, 128),
                   near(8, 128, kind=jnp.int32), near(8, 128),
                   near(4, 64, 1024), near(4, 64, 1024), near(9, 8, 1024), near(9, 8, 1024)),
        in_specs=[SM] + [ANY] * 7,
        out_specs=(ANY,) * 10,
        scratch_shapes=[pltpu.VMEM((4, 64, 1024), F32), pltpu.VMEM((4, 64, 1024), F32),
                        pltpu.VMEM((128, 128), jnp.int32), pltpu.VMEM((128, 128), jnp.int32),
                        pltpu.VMEM((8, 64), jnp.int32), pltpu.VMEM((8, 64), F32), pltpu.VMEM((128, 128), F32),
                        pltpu.VMEM((1, 128), F32), pltpu.VMEM((128, 128), F32), pltpu.VMEM((8, 128), jnp.int32),
                        pltpu.VMEM((8, 128), F32), pltpu.VMEM((8, 1024), F32), pltpu.SemaphoreType.DMA((35,))],
        compiler_params=grant(54),
        cost_estimate=pl.CostEstimate(flops=4000000, bytes_accessed=5000000, transcendentals=0),
        name="voltages",
    )(facet_counts, potential, conductivity, intra, extra, gap_partner.T, gap_cond.T, ion_states)

    below, above, far = on_mem(send_up, ring(1)), on_mem(send_down, ring(3)), on_mem(cells, ring(2))
    early_b, early_a = to_b(send_b), to_a(send_a)

    states_next, ion, source, count = pl.pallas_call(
        ionic_kernel,
        out_shape=(shape(40, 16384), shape(128, 128), shape(4, 64, 1024), shape(4, 64, 1024)),
        in_specs=[SM, SM] + [VM] * 9,
        out_specs=(ANY, VM, VM, VM),
        scratch_shapes=[pltpu.VMEM((40, 16384), F32), pltpu.VMEM((128, 128), F32),
                        pltpu.VMEM((10, 40, 128), F32), pltpu.SemaphoreType.DMA((CHUNKS,))],
        compiler_params=pltpu.CompilerParams(vmem_limit_bytes=ROOM),
        cost_estimate=pl.CostEstimate(flops=816000000, bytes_accessed=7300000, transcendentals=2600000),
        name="ionic",
    )(facet_counts, cell_type, volt, act, intra, extra, rate_scale, rate_slope, type_cond, reversal.reshape(1, 40),
      states_near)

    y_early, table, more_a, more_b = pl.pallas_call(
        early_edge_kernel,
        out_shape=(shape(8, 8, 1024), shape(8, 128), shape(3, 8, 1024), shape(3, 8, 1024)),
        in_specs=[VM] * 4 + [ANY],
        out_specs=(VM,) * 4,
        compiler_params=grant(6),
        cost_estimate=pl.CostEstimate(flops=300000, bytes_accessed=1000000, transcendentals=0),
        name="early_edges",
    )(below, above, far, cells, source)
    more_b, more_a = to_b(more_b), to_a(more_a)

    w, k = pl.pallas_call(
        prepare_kernel,
        out_shape=(shape(4, 64, 1024), shape(4, 64, 1024)),
        in_specs=[VM] * 7,
        out_specs=(VM, VM),
        compiler_params=grant(20),
        cost_estimate=pl.CostEstimate(flops=16000000, bytes_accessed=8000000, transcendentals=0),
        name="prepare",
    )(potential, conductivity, early_a, early_b, y_early, source, count)

    u, u_a, u_b, u_up, u_down, membrane = pl.pallas_call(
        gap_kernel,
        out_shape=(shape(4, 64, 1024), shape(3, 64, 1024), shape(3, 64, 1024), shape(4, 8, 1024),
                   shape(4, 8, 1024), shape(128, 128)),
        in_specs=[VM] * 9,
        out_specs=(VM,) * 6,
        scratch_shapes=[pltpu.VMEM((256, 128), F32)],
        compiler_params=grant(12),
        cost_estimate=pl.CostEstimate(flops=1000000, bytes_accessed=5000000, transcendentals=0),
        name="gap",
    )(table, more_a, more_b, part_lane, cond_lane, ion, act, w, k)

    late_b = to_b(u_b)
    low_rows = on_mem(u_up, [(i, i + 1) for i in range(3)])
    high_rows = on_mem(u_down, [(i + 1, i) for i in range(3)])
    late_a = to_a(u_a)

    big = lambda n: pltpu.VMEM((n, 72, 1024), F32)
    operator = pl.pallas_call(
        operator_kernel,
        out_shape=(shape(9, 72, 1024),) + (shape(8, 72, 1024),) * 5,
        in_specs=[VM] * 6 + [ANY],
        out_specs=(VM,) * 6,
        compiler_params=grant(22),
        cost_estimate=pl.CostEstimate(flops=16000000, bytes_accessed=17000000, transcendentals=0),
        name="operator",
    )(conductivity, early_a, early_b, y_early, more_a, more_b, u_up)

    y_late, corner_a, corner_b = pl.pallas_call(
        late_edge_kernel,
        out_shape=(shape(4, 8, 1024), shape(2, 8, 1024), shape(2, 8, 1024)),
        in_specs=[VM, VM, ANY],
        out_specs=(VM,) * 3,
        compiler_params=grant(4),
        cost_estimate=pl.CostEstimate(flops=100000, bytes_accessed=500000, transcendentals=0),
        name="late_edges",
    )(low_rows, high_rows, operator[-1])
    corner_b, corner_a = to_b(corner_b), to_a(corner_a)

    u1, r, u2, done = pl.pallas_call(
        near_kernel,
        out_shape=(shape(2, 72, 1024), shape(2, 72, 1024), shape(2, 72, 1024), shape(1, 64, 1024)),
        in_specs=[VM] * 11,
        out_specs=(VM,) * 4,
        scratch_shapes=[big(3), big(3), big(1)],
        compiler_params=grant(30),
        cost_estimate=pl.CostEstimate(flops=25000000, bytes_accessed=10000000, transcendentals=0),
        name="near",
    )(potential, *operator, u, late_a, y_late, corner_a)

    potential_next = pl.pallas_call(
        far_kernel,
        out_shape=shape(4, 64, 1024),
        in_specs=[VM] * 15,
        out_specs=ANY,
        scratch_shapes=[big(3), big(4), big(3), pltpu.VMEM((3, 64, 1024), F32), pltpu.SemaphoreType.DMA((4,))],
        compiler_params=grant(30),
        cost_estimate=pl.CostEstimate(flops=25000000, bytes_accessed=10000000, transcendentals=0),
        name="far",
    )(potential, *operator, u, late_b, y_late, corner_b, u1, r, u2, done)
    return potential_next, states_next, membrane.reshape(16384)


def solution(mesh):
    in_specs = (
        P("vol", "mem", None), P("vol", "mem", None), P(None, ("vol", "mem")),
        P(), P(), P(), P(),
        P(("vol", "mem")), P(("vol", "mem")), P(("vol", "mem")), P(("vol", "mem")),
        P(("vol", "mem"), None), P(("vol", "mem"), None),
    )
    out_specs = (P("vol", "mem", None), P(None, ("vol", "mem")), P(("vol", "mem")))
    return jax.shard_map(per_device, mesh=mesh, in_specs=in_specs, out_specs=out_specs, check_vma=False)
```

```python
import functools

import jax
import jax.numpy as jnp
from jax import lax
from jax.experimental import pallas as pl
from jax.experimental.pallas import tpu as pltpu
from jax.sharding import PartitionSpec as P

SWEEPS = 4
F32 = jnp.float32
BF16 = jnp.bfloat16
ANY = pl.BlockSpec(memory_space=pl.ANY)
HBM = pl.BlockSpec(memory_space=pltpu.HBM)
VM = pl.BlockSpec(memory_space=pltpu.VMEM)
SM = pl.BlockSpec(memory_space=pltpu.SMEM)


def grant(mib):
    return pltpu.CompilerParams(vmem_limit_bytes=mib * 1024 * 1024)


def sweep_factors():
    theta, delta = 1.0, 0.8
    sigma = theta / delta
    rho = 1.0 / sigma
    factors = []
    for _ in range(SWEEPS - 1):
        rho_next = 1.0 / (2.0 * sigma - rho)
        factors.append((rho_next * rho, 2.0 * rho_next / delta))
        rho = rho_next
    return factors


def iota(shape, dim):
    return lax.broadcasted_iota(jnp.int32, shape, dim)


def place():
    v, mine = lax.axis_index("vol"), lax.axis_index("mem")
    return v & 1, (v != 0) & (v != lax.axis_size("vol") - 1), mine, v


def plane_of(parity, j):
    return j + parity * (3 - 2 * j)


def pair_sum(row):
    even = (iota((1, 128), 1) & 1) == 0
    return row + jnp.where(even, pltpu.roll(row, 127, 1), pltpu.roll(row, 1, 1))


def gather_kernel(cnt, p_hbm, c_hbm, in_hbm, ex_hbm, part_hbm, cond_hbm, st_hbm,
                  st_near, volt_hbm, cell_hbm, act_hbm, part_out, cond_out, a_hbm, b_hbm, up_hbm, down_hbm,
                  p_ref, c_ref, in_ref, ex_ref, part_ref, cond_ref, volt_ref, cell_ref, act_ref, part_two, cond_two,
                  note, sem):
    par, has_b, mine, v = place()
    loads = begin(
        [(in_hbm, in_ref), (ex_hbm, ex_ref)] + [(p_hbm.at[x], p_ref.at[x]) for x in range(4)]
        + [(c_hbm.at[x], c_ref.at[x]) for x in range(4)] + [(part_hbm, part_ref), (cond_hbm, cond_ref)], sem, 0)
    states = begin([(st_hbm.at[:, 4096 * i : 4096 * i + 4096], st_near.at[:, 4096 * i : 4096 * i + 4096]) for i in range(4)], sem, 31)
    twice = iota((8, 128), 1) // 2
    sub = iota((8, 128), 0)
    low = sub < 4
    lane_row = iota((1, 128), 1)

    def body(kk, carry):
        x = kk // 4
        blocks = [r[pl.ds(pl.multiple_of(8 * kk, 8), 8), :] & 4095 for r in (in_ref, ex_ref)]
        for q in range(2):
            row = pl.multiple_of((2 * (kk % 4) + q) * 8, 8)
            tiles = [p_ref[x, pl.ds(row, 8), 128 * z : 128 * z + 128] for z in range(8)]
            for h in range(2):
                picked = []
                for block in blocks:
                    a = jnp.broadcast_to(block[4 * q + h : 4 * q + h + 1], (8, 128))
                    b = jnp.broadcast_to(block[4 * q + 2 + h : 4 * q + 3 + h], (8, 128))
                    o = jnp.where(low, a, b)
                    lane = o & 127
                    z_of = (o >> 7) & 7
                    got = jnp.take_along_axis(tiles[0], lane, axis=1, mode="promise_in_bounds")
                    for z in range(1, 8):
                        new = jnp.take_along_axis(tiles[z], lane, axis=1, mode="promise_in_bounds")
                        got = jnp.where(z_of == z, new, got)
                    picked.append(jnp.where((o >> 10) == (sub & 3), got, 0.0))
                d = picked[0] - picked[1]
                d = d + pltpu.roll(d, 7, 0)
                d = d + pltpu.roll(d, 6, 0)
                for i in range(2):
                    at = pl.ds(8 * kk + 4 * q + 2 * i + h, 1)
                    volt_ref[at, :] = d[4 * i : 4 * i + 1]
                    used = lane_row + 128 * h < cnt[4 * kk + 2 * q + i]
                    act_ref[at, :] = jnp.where(used, 1.0, 0.0)
        return carry

    loads[0].wait()
    loads[1].wait()
    for x in range(4):
        if x < 2:
            loads[2 + x].wait()
        lax.fori_loop(4 * x, 4 * x + 4, body, 0, unroll=4)
        if x == 1:
            for load in loads[4:]:
                load.wait()
            copies = []
            for i in range(3):
                copies.append((c_ref.at[plane_of(par, i)], b_hbm.at[i]))
                copies.append((c_ref.at[plane_of(par, 3 - i)], a_hbm.at[i]))
            copies.append((p_ref.at[plane_of(par, 0)], b_hbm.at[3]))
            copies.append((p_ref.at[plane_of(par, 3)], a_hbm.at[3]))
            for k, src in enumerate((c_ref, p_ref)):
                copies.append((src.at[:, 56:64], up_hbm.at[4 * k : 4 * k + 4]))
                copies.append((src.at[:, 0:8], down_hbm.at[4 * k : 4 * k + 4]))
            for src, dst in ((part_ref, part_two), (cond_ref, cond_two)):
                wide = jnp.concatenate([src[...], src[...]], axis=1)
                dst[...] = jnp.take_along_axis(wide, twice, axis=1, mode="promise_in_bounds")
            copies += [(part_two, part_out), (cond_two, cond_out)]
            sends = begin(copies, sem, 12)
    sends += begin([(volt_ref, volt_hbm), (act_ref, act_hbm)], sem, 26)
    act = act_ref[...]
    total = jnp.sum(jnp.transpose(volt_ref[...] * act), axis=0, keepdims=True)
    count = jnp.sum(jnp.transpose(act), axis=0, keepdims=True)
    cells = pair_sum(total) / jnp.maximum(pair_sum(count), 1.0)
    cell_ref[...] = cells
    note[...] = jnp.zeros((8, 1024), F32)
    note[0:1, 0:128] = cells
    sends += begin([(note, up_hbm.at[8]), (note, down_hbm.at[8]), (cell_ref, cell_hbm)], sem, 28)
    for send in sends + states:
        send.wait()


def begin(copies, sem, start):
    made = [pltpu.make_async_copy(s, d, sem.at[start + n]) for n, (s, d) in enumerate(copies)]
    for m in made:
        m.start()
    return made


CHUNKS = 16
ROOM = 24000000


def ionic_kernel(cnt, typ, volt_ref, act_ref, in_ref, ex_ref, scale_ref, slope_ref, cond_ref, rev_ref, st_ref,
                 out_hbm, ion_ref, s_ref, n_ref, out_ref, flat, rate_ref, sem):
    width = 16384 // CHUNKS
    at = lambda i: pl.ds(pl.multiple_of(i * width, width), width)
    store = lambda i: pltpu.make_async_copy(out_ref.at[:, at(i)], out_hbm.at[:, at(i)], sem.at[i])
    flat[...] = jnp.zeros((128, 128), F32)
    logs = jnp.log(scale_ref[...])
    flat[0:1, 0:40] = slope_ref[0:1]
    flat[1:2, 0:40] = logs[0:1]
    flat[2:3, 0:40] = -slope_ref[1:2]
    flat[3:4, 0:40] = logs[1:2]
    flat[4:7, 0:40] = cond_ref[...]
    flat[7:10, 0:40] = cond_ref[...] * rev_ref[...]
    turned = jnp.transpose(flat[...])
    for i in range(10):
        rate_ref[i] = jnp.broadcast_to(turned[0:40, i : i + 1], (40, 128))
    lane = iota((8, 128), 1)
    numbers = [(iota((16, 512), 0) + 16 * k).astype(F32).astype(BF16) for k in range(8)]
    low = iota((8, 128), 0) < 4
    odd_row = (iota((8, 128), 0) & 2) // 2

    def body(group, carry):
        rows8 = pl.ds(pl.multiple_of(8 * group, 8), 8)
        volts = volt_ref[rows8, :]
        counts, types, v, active, cols = [], [], [], [], []
        for q in range(4):
            counts.append(cnt[4 * group + q])
            types.append(typ[4 * group + q])
        for r in range(8):
            v.append(jnp.broadcast_to(volts[r : r + 1], (8, 128)))
            active.append(lane + (r % 2) * 128 < counts[r // 2])
            cols.append(pl.ds(pl.multiple_of(1024 * group + 128 * r, 128), 128))
        w1, w2 = [None] * 8, [None] * 8
        for k in range(5):
            rows = slice(8 * k, 8 * k + 8)
            rate = [rate_ref[i, rows] for i in range(4)]
            for q in range(4):
                g, gr = rate_ref[4 + types[q], rows], rate_ref[7 + types[q], rows]
                for r in (2 * q, 2 * q + 1):
                    st = st_ref[rows, cols[r]]
                    opening = jnp.exp(rate[0] * v[r] + rate[1])
                    closing = jnp.exp(rate[2] * v[r] + rate[3])
                    total = opening + closing
                    steady = opening * inverse(total)
                    fresh = steady + (st - steady) * jnp.exp(total * -0.5)
                    out_ref[rows, cols[r]] = jnp.where(active[r], fresh, st)
                    w1[r] = g * fresh if k == 0 else w1[r] + g * fresh
                    w2[r] = gr * fresh if k == 0 else w2[r] + gr * fresh
        store(group).start()
        act = act_ref[rows8, :]
        ion = [jnp.sum(w1[r] * v[r] - w2[r], axis=0, keepdims=True) for r in range(8)]
        val = jnp.concatenate(ion, axis=0) * act
        ion_ref[rows8, :] = val

        x = group // 4
        hi = val.astype(BF16).astype(F32)
        lo = val - hi
        mids, lanes = [], []
        for ref in (in_ref, ex_ref):
            o = ref[rows8, :] & 4095
            mids.append(((((o >> 7) & 7) ^ odd_row) * 4 + (o >> 10)).astype(F32))
            lanes.append((o & 127).astype(F32))

        def line(a, b, s):
            r = 2 * s
            return jnp.concatenate([a[r : r + 1], a[r + 1 : r + 2], b[r : r + 1], b[r + 1 : r + 2]], axis=1)

        for q in range(2):
            results = []
            for s in (2 * q, 2 * q + 1):
                packed = lambda row: jnp.broadcast_to(row, (16, 512)).astype(BF16)
                mid, at = packed(line(mids[0], mids[1], s)), packed(line(lanes[0], lanes[1], s))
                pieces = [packed(line(piece, -piece, s)) for piece in (hi, lo, act)]
                hits = [mid == numbers[0], mid == numbers[1]]
                none, one = jnp.zeros((16, 512), BF16), jnp.ones((16, 512), BF16)
                left = jnp.concatenate([jnp.where(hit, piece, none) for piece in pieces for hit in hits], axis=0)
                right = jnp.concatenate([jnp.where(at == number, one, none) for number in numbers], axis=0)
                out = lax.dot_general(left, right, (((1,), (1,)), ((), ())), preferred_element_type=F32)
                results.append((out[0:32] + out[32:64], out[64:96]))
            row = pl.ds(pl.multiple_of((2 * (group % 4) + q) * 8, 8), 8)
            for dst, e, o in ((s_ref, results[0][0], results[1][0]), (n_ref, results[0][1], results[1][1])):
                for j in range(4):
                    ej, oj = e[8 * j : 8 * j + 8], o[8 * j : 8 * j + 8]
                    dst[x, row, 256 * j : 256 * j + 128] = jnp.where(low, ej, oj)
                    dst[x, row, 256 * j + 128 : 256 * j + 256] = pltpu.roll(jnp.where(low, oj, ej), 4, 0)
        return carry

    lax.fori_loop(0, CHUNKS, body, 0, unroll=2)
    for i in range(CHUNKS):
        store(i).wait()


def edge_rows(mine, below, above):
    sub = iota((8, 1024), 0)
    bottom = (sub < 3) & (mine != 3)
    top = (sub >= 5) & (mine != 0)
    return jnp.where(bottom, above, jnp.where(top, below, 0.0))


def early_edge_kernel(below_ref, above_ref, far_ref, cell_ref, after, y_ref, table_ref, a_ref, b_ref):
    par, has_b, mine, v = place()
    for x in range(8):
        y_ref[x] = edge_rows(mine, below_ref[x], above_ref[x])
    table = jnp.concatenate(
        [cell_ref[...], below_ref[8, 0:1, 0:128], far_ref[...], above_ref[8, 0:1, 0:128],
         jnp.zeros((4, 128), F32)], axis=0)
    table_ref[...] = table
    for i in range(2):
        a_ref[i] = y_ref[plane_of(par, 3 - i)]
        b_ref[i] = y_ref[plane_of(par, i)]
    for ref in (a_ref, b_ref):
        ref[2] = jnp.zeros((8, 1024), F32)
        ref[2, :, 0:128] = table


def late_edge_kernel(below_ref, above_ref, after, y_ref, a_ref, b_ref):
    par, has_b, mine, v = place()
    for x in range(4):
        y_ref[x] = edge_rows(mine, below_ref[x], above_ref[x])
    for i in range(2):
        a_ref[i] = y_ref[plane_of(par, 3 - i)]
        b_ref[i] = y_ref[plane_of(par, i)]


def reader(par, inside, own, a, b, y, ca=None, cb=None, own_y=0):
    def get(e, t):
        rows = slice(8 * t, 8 * t + 8)
        if 3 <= e <= 6:
            x = plane_of(par, e - 3)
            return own[x, rows, :] if t < 8 else y[own_y + x]
        halo, corner, i = (a, ca, e - 7) if e > 6 else (b, cb, 2 - e)
        value = halo[i, rows, :] if t < 8 else corner[i]
        return value if e > 6 else value * inside

    return get


def stored(*held):
    def get(e, t):
        for ref, start, stop in held:
            if start <= e < stop:
                return ref[e - start, 8 * t : 8 * t + 8, :]

    return get


class Plane:
    def __init__(self, get, e):
        self.get, self.e = get, e
        self.sub = iota((8, 1024), 0)
        self.kept = {}

    def turned(self, t, by, keep):
        found = self.kept.pop((t, by), None)
        if found is None:
            found = pltpu.roll(self.get(self.e, t), by, 0)
            if keep:
                self.kept[t, by] = found
        return found

    def views(self, t):
        get, e = self.get, self.e
        c = get(e, t)
        ym = jnp.where(self.sub == 0, self.turned((t + 8) % 9, 1, False), self.turned(t, 1, True))
        yp = jnp.where(self.sub == 7, self.turned((t + 1) % 9, 7, t < 8), self.turned(t, 7, False))
        return c, get(e - 1, t), get(e + 1, t), ym, yp, pltpu.roll(c, 1, 1), pltpu.roll(c, 1023, 1)


def inverse(x):
    rec = pl.reciprocal(x, approx=True)
    return rec * (2.0 - x * rec)


def couplings(plane, t):
    lane = iota((8, 1024), 1)
    c, xm, xp, ym, yp, zm, zp = plane.views(t)
    first, last = lane == 0, lane == 1023
    c = 0.25 * c
    xm, xp, ym, yp = (c + 0.25 * other for other in (xm, xp, ym, yp))
    zm = c + 0.25 * jnp.where(first, 0.0, zm)
    zp = c + 0.25 * jnp.where(last, 0.0, zp)
    inv = inverse(1.0 + (((xm + xp) + (ym + yp)) + (zm + zp)))
    return (xm, xp, ym, yp, jnp.where(first, 0.0, zm), jnp.where(last, 0.0, zp)), inv


def weighted(fs, views):
    t = [f * v for f, v in zip(fs, views)]
    return ((t[0] + t[1]) + (t[2] + t[3])) + (t[4] + t[5])


def prepare_kernel(p_ref, c_ref, a_ref, b_ref, y_ref, s_ref, n_ref, w_ref, k_ref):
    par, has_b, mine, v = place()
    inside = jnp.where(has_b, 1.0, 0.0)
    conduct = reader(par, inside, c_ref, a_ref, b_ref, y_ref)
    own = reader(par, inside, p_ref, a_ref.at[3:4], b_ref.at[3:4], y_ref, own_y=4)
    for e in range(3, 7):
        x = plane_of(par, e - 3)
        pc, pp = Plane(conduct, e), Plane(own, e)
        for t in range(8):
            rows = slice(8 * t, 8 * t + 8)
            fs, inv = couplings(pc, t)
            p, *views = pp.views(t)
            w_ref[x, rows, :] = (p + weighted(fs, views) - 0.5 * s_ref[x, rows, :]) * inv - p
            k_ref[x, rows, :] = (-0.5 * inv) * n_ref[x, rows, :]


def gap_kernel(table_ref, ta_ref, tb_ref, part_ref, cond_ref, ion_ref, act_ref, w_ref, k_ref,
               u_ref, a_ref, b_ref, up_ref, down_ref, mem_ref, spread):
    par, has_b, mine, v = place()
    part = part_ref[...]
    brick = part >> 6
    bx, by = brick >> 2, brick & 3
    side = jnp.where(bx == v, 0, jnp.where(bx == (v ^ 1), 1, 2))
    row = side * 4 + ((mine - by) & 3)
    lane = (part & 63) * 2
    tables = (table_ref[...], ta_ref[2, :, 0:128], tb_ref[2, :, 0:128])
    other = jnp.zeros((8, 128), F32)
    for r in range(12):
        line = jnp.broadcast_to(tables[r // 4][r % 4 : r % 4 + 1], (8, 128))
        other = jnp.where(row == r, jnp.take_along_axis(line, lane, axis=1, mode="promise_in_bounds"), other)
    own = tables[0][0:1]
    current = jnp.sum(cond_ref[...] * (own - other), axis=0, keepdims=True)
    act = act_ref[...]
    count = pair_sum(jnp.sum(jnp.transpose(act), axis=0, keepdims=True))
    g = current / jnp.maximum(count, 1.0)
    g8 = jnp.broadcast_to(g, (8, 128))
    mem_ref[...] = ion_ref[...] + act * jnp.transpose(jnp.broadcast_to(g, (128, 128)))
    for half in range(2):
        at = 64 * half + 2 * (iota((8, 128), 1) // 4)
        wide = jnp.take_along_axis(g8, at, axis=1, mode="promise_in_bounds")[0:1]
        spread[128 * half : 128 * half + 128, :] = jnp.transpose(jnp.broadcast_to(wide, (128, 128)))
    for j in range(4):
        x = plane_of(par, j)
        for t in range(8):
            rows = slice(8 * t, 8 * t + 8)
            gt = jnp.tile(spread[pl.ds(pl.multiple_of(x * 64 + 8 * t, 8), 8), :], (1, 8))
            u = w_ref[x, rows, :] + k_ref[x, rows, :] * gt
            u_ref[x, rows, :] = u
            if t == 0:
                down_ref[x] = u
            if t == 7:
                up_ref[x] = u
            if j < 3:
                b_ref[j, rows, :] = u
            if j > 0:
                a_ref[3 - j, rows, :] = u


def operator_kernel(c_ref, a_ref, b_ref, y_ref, ca_ref, cb_ref, after, fx, fym, fyp, fzm, fzp, inv_ref):
    par, has_b, mine, v = place()
    inside = jnp.where(has_b, 1.0, 0.0)
    conduct = reader(par, inside, c_ref, a_ref, b_ref, y_ref, ca_ref, cb_ref)
    sub = iota((8, 1024), 0)
    bottom = (sub < 3) & (mine != 3)
    top = (sub >= 5) & (mine != 0)
    keep = jnp.where(bottom | top, 1.0, 0.0)
    for e in range(1, 9):
        plane = Plane(conduct, e)
        for t in range(8 if e in (1, 8) else 9):
            rows = slice(8 * t, 8 * t + 8)
            fs, inv = couplings(plane, t)
            if e < 3:
                inv = inv * inside
            inv_ref[e - 1, rows, :] = inv * keep if t == 8 else inv
            if e == 1 or (e == 2 and t == 8):
                fx[e - 1, rows, :] = fs[0]
            fx[e, rows, :] = fs[1]
            for ref, f in zip((fym, fyp, fzm, fzp), fs[2:]):
                ref[e - 1, rows, :] = f


def coupled(coef, get, plane, t):
    fx, fym, fyp, fzm, fzp, inv = coef
    e = plane.e
    rows = slice(8 * t, 8 * t + 8)
    fs = [fx[e - 1, rows, :], fx[e, rows, :]] + [f[e - 1, rows, :] for f in (fym, fyp, fzm, fzp)]
    u, *views = plane.views(t)
    return u, inv[e - 1, rows, :] * weighted(fs, views)


def put(held, e, t, value):
    for ref, start, stop in held:
        if start <= e < stop:
            ref[e - start, 8 * t : 8 * t + 8, :] = value


def step_one(coef, u0, e, r_held, u1_held):
    a, b = sweep_factors()[0]
    plane = Plane(u0, e)
    for t in range(8 if e in (1, 8) else 9):
        u, res = coupled(coef, u0, plane, t)
        put(r_held, e, t, res)
        put(u1_held, e, t, a * u + b * res)


def step_two(coef, u1, r, e, r_held, u2_held):
    a, b = sweep_factors()[1]
    plane = Plane(u1, e)
    for t in range(8 if e in (2, 7) else 9):
        u, more = coupled(coef, u1, plane, t)
        res = (r(e, t) - u) + more
        put(r_held, e, t, res)
        put(u2_held, e, t, a * u + b * res)


def step_three(coef, p_ref, u0, u1, u2, r, e, x, out_ref, at):
    a, b = sweep_factors()[2]
    plane = Plane(u2, e)
    for t in range(8):
        rows = slice(8 * t, 8 * t + 8)
        u, more = coupled(coef, u2, plane, t)
        res = (r(e, t) - u) + more
        before = (p_ref[x, rows, :] + u0(e, t)) + (u1(e, t) + u)
        out_ref[at, rows, :] = before + (a * u + b * res)


def near_kernel(p_ref, fx, fym, fyp, fzm, fzp, inv, u_ref, a_ref, y_ref, ca_ref,
                u1_out, r_out, u2_out, done_ref, u1_far, r_far, u2_far):
    par, has_b, mine, v = place()
    inside = jnp.where(has_b, 1.0, 0.0)
    coef = (fx, fym, fyp, fzm, fzp, inv)
    u0 = reader(par, inside, u_ref, a_ref, None, y_ref, ca_ref)
    u1_held = ((u1_out, 4, 6), (u1_far, 6, 9))
    r1_held = ((r_out, 4, 5), (r_far, 5, 8))
    r2_held = ((r_out.at[1:2], 5, 6), (r_far.at[1:2], 6, 7))
    u2_held = ((u2_out, 5, 7), (u2_far, 7, 8))
    for e in (8, 7, 6, 5, 4):
        step_one(coef, u0, e, r1_held, u1_held)
    for e in (7, 6, 5):
        step_two(coef, stored(*u1_held), stored(*r1_held), e, r2_held, u2_held)
    step_three(coef, p_ref, u0, stored(*u1_held), stored(*u2_held), stored(*r2_held), 6, plane_of(par, 3), done_ref, 0)


def far_kernel(p_ref, fx, fym, fyp, fzm, fzp, inv, u_ref, b_ref, y_ref, cb_ref, u1_in, r_in, u2_in, done_ref,
               out_hbm, u1_far, r_far, u2_far, out_ref, sem):
    par, has_b, mine, v = place()
    inside = jnp.where(has_b, 1.0, 0.0)
    coef = (fx, fym, fyp, fzm, fzp, inv)
    u0 = reader(par, inside, u_ref, None, b_ref, y_ref, None, cb_ref)
    u1_new = ((u1_far, 1, 4),)
    u1 = stored(*u1_new, (u1_in, 4, 6))
    r1_new = ((r_far, 2, 4),)
    r1 = stored(*r1_new, (r_in, 4, 5))
    r2_new = ((r_far.at[2:4], 3, 5),)
    r2 = stored(*r2_new, (r_in.at[1:2], 5, 6))
    u2_new = ((u2_far, 2, 5),)
    u2 = stored(*u2_new, (u2_in, 5, 7))
    sends = begin([(done_ref.at[0], out_hbm.at[plane_of(par, 3)])], sem, 3)
    for e in (1, 2, 3):
        step_one(coef, u0, e, r1_new, u1_new)
    for e in (2, 3, 4):
        step_two(coef, u1, r1, e, r2_new, u2_new)
    for e in (3, 4, 5):
        x = plane_of(par, e - 3)
        step_three(coef, p_ref, u0, u1, u2, r2, e, x, out_ref, e - 3)
        sends += begin([(out_ref.at[e - 3], out_hbm.at[x])], sem, e - 3)
    for send in sends:
        send.wait()


def near(*dims, kind=F32):
    return pltpu.VMEM(dims, kind)


def shape(*dims, kind=F32):
    return jax.ShapeDtypeStruct(dims, kind)


def per_device(potential, conductivity, ion_states, rate_scale, rate_slope, type_cond, reversal,
               facet_counts, intra_voxel, extra_voxel, cell_type, gap_partner, gap_cond):
    nv = lax.axis_size("vol")
    swap_a = [pair for i in range(0, nv, 2) for pair in ((i, i + 1), (i + 1, i))]
    swap_b = [pair for i in range(1, nv - 1, 2) for pair in ((i, i + 1), (i + 1, i))] + [(0, 0), (nv - 1, nv - 1)]
    on_mem = lambda x, pairs: lax.ppermute(x, "mem", pairs)
    ring = lambda d: [(i, (i + d) % 4) for i in range(4)]
    to_a = functools.partial(lax.ppermute, axis_name="vol", perm=swap_a)
    to_b = functools.partial(lax.ppermute, axis_name="vol", perm=swap_b)

    intra = intra_voxel.reshape(128, 128)
    extra = extra_voxel.reshape(128, 128)

    states_near, volt, cells, act, part_lane, cond_lane, send_a, send_b, send_up, send_down = pl.pallas_call(
        gather_kernel,
        out_shape=(near(40, 16384), near(128, 128), near(1, 128), near(128, 128),
                   near(8, 128, kind=jnp.int32), near(8, 128),
                   near(4, 64, 1024), near(4, 64, 1024), near(9, 8, 1024), near(9, 8, 1024)),
        in_specs=[SM] + [ANY] * 7,
        out_specs=(ANY,) * 10,
        scratch_shapes=[pltpu.VMEM((4, 64, 1024), F32), pltpu.VMEM((4, 64, 1024), F32),
                        pltpu.VMEM((128, 128), jnp.int32), pltpu.VMEM((128, 128), jnp.int32),
                        pltpu.VMEM((8, 64), jnp.int32), pltpu.VMEM((8, 64), F32), pltpu.VMEM((128, 128), F32),
                        pltpu.VMEM((1, 128), F32), pltpu.VMEM((128, 128), F32), pltpu.VMEM((8, 128), jnp.int32),
                        pltpu.VMEM((8, 128), F32), pltpu.VMEM((8, 1024), F32), pltpu.SemaphoreType.DMA((35,))],
        compiler_params=grant(54),
        cost_estimate=pl.CostEstimate(flops=4000000, bytes_accessed=5000000, transcendentals=0),
        name="voltages",
    )(facet_counts, potential, conductivity, intra, extra, gap_partner.T, gap_cond.T, ion_states)

    below, above, far = on_mem(send_up, ring(1)), on_mem(send_down, ring(3)), on_mem(cells, ring(2))
    early_b, early_a = to_b(send_b), to_a(send_a)

    states_next, ion, source, count = pl.pallas_call(
        ionic_kernel,
        out_shape=(shape(40, 16384), shape(128, 128), shape(4, 64, 1024), shape(4, 64, 1024)),
        in_specs=[SM, SM] + [VM] * 9,
        out_specs=(ANY, VM, VM, VM),
        scratch_shapes=[pltpu.VMEM((40, 16384), F32), pltpu.VMEM((128, 128), F32),
                        pltpu.VMEM((10, 40, 128), F32), pltpu.SemaphoreType.DMA((CHUNKS,))],
        compiler_params=pltpu.CompilerParams(vmem_limit_bytes=ROOM),
        cost_estimate=pl.CostEstimate(flops=816000000, bytes_accessed=7300000, transcendentals=2600000),
        name="ionic",
    )(facet_counts, cell_type, volt, act, intra, extra, rate_scale, rate_slope, type_cond, reversal.reshape(1, 40),
      states_near)

    y_early, table, more_a, more_b = pl.pallas_call(
        early_edge_kernel,
        out_shape=(shape(8, 8, 1024), shape(8, 128), shape(3, 8, 1024), shape(3, 8, 1024)),
        in_specs=[VM] * 4 + [ANY],
        out_specs=(VM,) * 4,
        compiler_params=grant(6),
        cost_estimate=pl.CostEstimate(flops=300000, bytes_accessed=1000000, transcendentals=0),
        name="early_edges",
    )(below, above, far, cells, source)
    more_b, more_a = to_b(more_b), to_a(more_a)

    w, k = pl.pallas_call(
        prepare_kernel,
        out_shape=(shape(4, 64, 1024), shape(4, 64, 1024)),
        in_specs=[VM] * 7,
        out_specs=(VM, VM),
        compiler_params=grant(20),
        cost_estimate=pl.CostEstimate(flops=16000000, bytes_accessed=8000000, transcendentals=0),
        name="prepare",
    )(potential, conductivity, early_a, early_b, y_early, source, count)

    u, u_a, u_b, u_up, u_down, membrane = pl.pallas_call(
        gap_kernel,
        out_shape=(shape(4, 64, 1024), shape(3, 64, 1024), shape(3, 64, 1024), shape(4, 8, 1024),
                   shape(4, 8, 1024), shape(128, 128)),
        in_specs=[VM] * 9,
        out_specs=(VM,) * 6,
        scratch_shapes=[pltpu.VMEM((256, 128), F32)],
        compiler_params=grant(12),
        cost_estimate=pl.CostEstimate(flops=1000000, bytes_accessed=5000000, transcendentals=0),
        name="gap",
    )(table, more_a, more_b, part_lane, cond_lane, ion, act, w, k)

    late_b = to_b(u_b)
    low_rows, high_rows = on_mem(u_up, ring(1)), on_mem(u_down, ring(3))
    late_a = to_a(u_a)

    big = lambda n: pltpu.VMEM((n, 72, 1024), F32)
    operator = pl.pallas_call(
        operator_kernel,
        out_shape=(shape(9, 72, 1024),) + (shape(8, 72, 1024),) * 5,
        in_specs=[VM] * 6 + [ANY],
        out_specs=(VM,) * 6,
        compiler_params=grant(22),
        cost_estimate=pl.CostEstimate(flops=16000000, bytes_accessed=17000000, transcendentals=0),
        name="operator",
    )(conductivity, early_a, early_b, y_early, more_a, more_b, u_up)

    y_late, corner_a, corner_b = pl.pallas_call(
        late_edge_kernel,
        out_shape=(shape(4, 8, 1024), shape(2, 8, 1024), shape(2, 8, 1024)),
        in_specs=[VM, VM, ANY],
        out_specs=(VM,) * 3,
        compiler_params=grant(4),
        cost_estimate=pl.CostEstimate(flops=100000, bytes_accessed=500000, transcendentals=0),
        name="late_edges",
    )(low_rows, high_rows, operator[-1])
    corner_b, corner_a = to_b(corner_b), to_a(corner_a)

    u1, r, u2, done = pl.pallas_call(
        near_kernel,
        out_shape=(shape(2, 72, 1024), shape(2, 72, 1024), shape(2, 72, 1024), shape(1, 64, 1024)),
        in_specs=[VM] * 11,
        out_specs=(VM,) * 4,
        scratch_shapes=[big(3), big(3), big(1)],
        compiler_params=grant(30),
        cost_estimate=pl.CostEstimate(flops=25000000, bytes_accessed=10000000, transcendentals=0),
        name="near",
    )(potential, *operator, u, late_a, y_late, corner_a)

    potential_next = pl.pallas_call(
        far_kernel,
        out_shape=shape(4, 64, 1024),
        in_specs=[VM] * 15,
        out_specs=ANY,
        scratch_shapes=[big(3), big(4), big(3), pltpu.VMEM((3, 64, 1024), F32), pltpu.SemaphoreType.DMA((4,))],
        compiler_params=grant(30),
        cost_estimate=pl.CostEstimate(flops=25000000, bytes_accessed=10000000, transcendentals=0),
        name="far",
    )(potential, *operator, u, late_b, y_late, corner_b, u1, r, u2, done)
    return potential_next, states_next, membrane.reshape(16384)


def solution(mesh):
    in_specs = (
        P("vol", "mem", None), P("vol", "mem", None), P(None, ("vol", "mem")),
        P(), P(), P(), P(),
        P(("vol", "mem")), P(("vol", "mem")), P(("vol", "mem")), P(("vol", "mem")),
        P(("vol", "mem"), None), P(("vol", "mem"), None),
    )
    out_specs = (P("vol", "mem", None), P(None, ("vol", "mem")), P(("vol", "mem")))
    return jax.shard_map(per_device, mesh=mesh, in_specs=in_specs, out_specs=out_specs, check_vma=False)
```

```python
import functools

import jax
import jax.numpy as jnp
from jax import lax
from jax.experimental import pallas as pl
from jax.experimental.pallas import tpu as pltpu
from jax.sharding import PartitionSpec as P

SWEEPS = 4
F32 = jnp.float32
BF16 = jnp.bfloat16
ANY = pl.BlockSpec(memory_space=pl.ANY)
HBM = pl.BlockSpec(memory_space=pltpu.HBM)
VM = pl.BlockSpec(memory_space=pltpu.VMEM)
SM = pl.BlockSpec(memory_space=pltpu.SMEM)


def grant(mib):
    return pltpu.CompilerParams(vmem_limit_bytes=mib * 1024 * 1024)


def sweep_factors():
    theta, delta = 1.0, 0.8
    sigma = theta / delta
    rho = 1.0 / sigma
    factors = []
    for _ in range(SWEEPS - 1):
        rho_next = 1.0 / (2.0 * sigma - rho)
        factors.append((rho_next * rho, 2.0 * rho_next / delta))
        rho = rho_next
    return factors


def iota(shape, dim):
    return lax.broadcasted_iota(jnp.int32, shape, dim)


def place():
    v, mine = lax.axis_index("vol"), lax.axis_index("mem")
    return v & 1, (v != 0) & (v != lax.axis_size("vol") - 1), mine, v


def plane_of(parity, j):
    return j + parity * (3 - 2 * j)


def pair_sum(row):
    even = (iota((1, 128), 1) & 1) == 0
    return row + jnp.where(even, pltpu.roll(row, 127, 1), pltpu.roll(row, 1, 1))


def gather_kernel(cnt, p_hbm, c_hbm, in_hbm, ex_hbm, part_hbm, cond_hbm, st_hbm,
                  st_near, volt_hbm, cell_hbm, act_hbm, part_out, cond_out, a_hbm, b_hbm, up_hbm, down_hbm,
                  p_ref, c_ref, in_ref, ex_ref, part_ref, cond_ref, volt_ref, cell_ref, act_ref, part_two, cond_two,
                  note, sem):
    par, has_b, mine, v = place()
    loads = begin(
        [(in_hbm, in_ref), (ex_hbm, ex_ref)] + [(p_hbm.at[x], p_ref.at[x]) for x in range(4)]
        + [(c_hbm.at[x], c_ref.at[x]) for x in range(4)] + [(part_hbm, part_ref), (cond_hbm, cond_ref)], sem, 0)
    states = begin([(st_hbm.at[:, 4096 * i : 4096 * i + 4096], st_near.at[:, 4096 * i : 4096 * i + 4096]) for i in range(4)], sem, 31)
    twice = iota((8, 128), 1) // 2
    sub = iota((8, 128), 0)
    low = sub < 4
    lane_row = iota((1, 128), 1)

    def body(kk, carry):
        x = kk // 4
        blocks = [r[pl.ds(pl.multiple_of(8 * kk, 8), 8), :] & 4095 for r in (in_ref, ex_ref)]
        for q in range(2):
            row = pl.multiple_of((2 * (kk % 4) + q) * 8, 8)
            tiles = [p_ref[x, pl.ds(row, 8), 128 * z : 128 * z + 128] for z in range(8)]
            for h in range(2):
                picked = []
                for block in blocks:
                    a = jnp.broadcast_to(block[4 * q + h : 4 * q + h + 1], (8, 128))
                    b = jnp.broadcast_to(block[4 * q + 2 + h : 4 * q + 3 + h], (8, 128))
                    o = jnp.where(low, a, b)
                    lane = o & 127
                    z_of = (o >> 7) & 7
                    got = jnp.take_along_axis(tiles[0], lane, axis=1, mode="promise_in_bounds")
                    for z in range(1, 8):
                        new = jnp.take_along_axis(tiles[z], lane, axis=1, mode="promise_in_bounds")
                        got = jnp.where(z_of == z, new, got)
                    picked.append(jnp.where((o >> 10) == (sub & 3), got, 0.0))
                d = picked[0] - picked[1]
                d = d + pltpu.roll(d, 7, 0)
                d = d + pltpu.roll(d, 6, 0)
                for i in range(2):
                    at = pl.ds(8 * kk + 4 * q + 2 * i + h, 1)
                    volt_ref[at, :] = d[4 * i : 4 * i + 1]
                    used = lane_row + 128 * h < cnt[4 * kk + 2 * q + i]
                    act_ref[at, :] = jnp.where(used, 1.0, 0.0)
        return carry

    loads[0].wait()
    loads[1].wait()
    for x in range(4):
        if x < 2:
            loads[2 + x].wait()
        lax.fori_loop(4 * x, 4 * x + 4, body, 0, unroll=4)
        if x == 1:
            for load in loads[4:]:
                load.wait()
            copies = []
            for i in range(3):
                copies.append((c_ref.at[plane_of(par, i)], b_hbm.at[i]))
                copies.append((c_ref.at[plane_of(par, 3 - i)], a_hbm.at[i]))
            copies.append((p_ref.at[plane_of(par, 0)], b_hbm.at[3]))
            copies.append((p_ref.at[plane_of(par, 3)], a_hbm.at[3]))
            for k, src in enumerate((c_ref, p_ref)):
                copies.append((src.at[:, 56:64], up_hbm.at[4 * k : 4 * k + 4]))
                copies.append((src.at[:, 0:8], down_hbm.at[4 * k : 4 * k + 4]))
            for src, dst in ((part_ref, part_two), (cond_ref, cond_two)):
                wide = jnp.concatenate([src[...], src[...]], axis=1)
                dst[...] = jnp.take_along_axis(wide, twice, axis=1, mode="promise_in_bounds")
            copies += [(part_two, part_out), (cond_two, cond_out)]
            sends = begin(copies, sem, 12)
    sends += begin([(volt_ref, volt_hbm), (act_ref, act_hbm)], sem, 26)
    act = act_ref[...]
    total = jnp.sum(jnp.transpose(volt_ref[...] * act), axis=0, keepdims=True)
    count = jnp.sum(jnp.transpose(act), axis=0, keepdims=True)
    cells = pair_sum(total) / jnp.maximum(pair_sum(count), 1.0)
    cell_ref[...] = cells
    note[...] = jnp.zeros((8, 1024), F32)
    note[0:1, 0:128] = cells
    sends += begin([(note, up_hbm.at[8]), (note, down_hbm.at[8]), (cell_ref, cell_hbm)], sem, 28)
    for send in sends + states:
        send.wait()


def begin(copies, sem, start):
    made = [pltpu.make_async_copy(s, d, sem.at[start + n]) for n, (s, d) in enumerate(copies)]
    for m in made:
        m.start()
    return made


CHUNKS = 16
ROOM = 24000000


def ionic_kernel(cnt, typ, volt_ref, act_ref, scale_ref, slope_ref, cond_ref, rev_ref, st_ref,
                 out_hbm, ion_ref, out_ref, flat, rate_ref, sem):
    width = 16384 // CHUNKS
    at = lambda i: pl.ds(pl.multiple_of(i * width, width), width)
    store = lambda i: pltpu.make_async_copy(out_ref.at[:, at(i)], out_hbm.at[:, at(i)], sem.at[i])
    flat[...] = jnp.zeros((128, 128), F32)
    logs = jnp.log(scale_ref[...])
    flat[0:1, 0:40] = slope_ref[0:1]
    flat[1:2, 0:40] = logs[0:1]
    flat[2:3, 0:40] = -slope_ref[1:2]
    flat[3:4, 0:40] = logs[1:2]
    flat[4:7, 0:40] = cond_ref[...]
    flat[7:10, 0:40] = cond_ref[...] * rev_ref[...]
    turned = jnp.transpose(flat[...])
    for i in range(10):
        rate_ref[i] = jnp.broadcast_to(turned[0:40, i : i + 1], (40, 128))
    lane = iota((8, 128), 1)

    def body(group, carry):
        rows8 = pl.ds(pl.multiple_of(8 * group, 8), 8)
        volts = volt_ref[rows8, :]
        counts, types, v, active, cols = [], [], [], [], []
        for q in range(4):
            counts.append(cnt[4 * group + q])
            types.append(typ[4 * group + q])
        for r in range(8):
            v.append(jnp.broadcast_to(volts[r : r + 1], (8, 128)))
            active.append(lane + (r % 2) * 128 < counts[r // 2])
            cols.append(pl.ds(pl.multiple_of(1024 * group + 128 * r, 128), 128))
        w1, w2 = [None] * 8, [None] * 8
        for k in range(5):
            rows = slice(8 * k, 8 * k + 8)
            rate = [rate_ref[i, rows] for i in range(4)]
            for q in range(4):
                g, gr = rate_ref[4 + types[q], rows], rate_ref[7 + types[q], rows]
                for r in (2 * q, 2 * q + 1):
                    st = st_ref[rows, cols[r]]
                    opening = jnp.exp(rate[0] * v[r] + rate[1])
                    closing = jnp.exp(rate[2] * v[r] + rate[3])
                    total = opening + closing
                    steady = opening * inverse(total)
                    fresh = steady + (st - steady) * jnp.exp(total * -0.5)
                    out_ref[rows, cols[r]] = jnp.where(active[r], fresh, st)
                    w1[r] = g * fresh if k == 0 else w1[r] + g * fresh
                    w2[r] = gr * fresh if k == 0 else w2[r] + gr * fresh
        store(group).start()
        act = act_ref[rows8, :]
        ion = [jnp.sum(w1[r] * v[r] - w2[r], axis=0, keepdims=True) for r in range(8)]
        val = jnp.concatenate(ion, axis=0) * act
        ion_ref[rows8, :] = val
        return carry

    lax.fori_loop(0, CHUNKS, body, 0, unroll=2)
    for i in range(CHUNKS):
        store(i).wait()


def scatter_kernel(ion_ref, act_ref, in_ref, ex_ref, after, s_ref, n_ref):
    numbers = [(iota((16, 512), 0) + 16 * k).astype(F32).astype(BF16) for k in range(8)]
    low = iota((8, 128), 0) < 4
    odd_row = (iota((8, 128), 0) & 2) // 2

    def body(group, carry):
        rows8 = pl.ds(pl.multiple_of(8 * group, 8), 8)
        val, act = ion_ref[rows8, :], act_ref[rows8, :]
        x = group // 4
        hi = val.astype(BF16).astype(F32)
        lo = val - hi
        mids, lanes = [], []
        for ref in (in_ref, ex_ref):
            o = ref[rows8, :] & 4095
            mids.append(((((o >> 7) & 7) ^ odd_row) * 4 + (o >> 10)).astype(F32))
            lanes.append((o & 127).astype(F32))

        def line(a, b, s):
            r = 2 * s
            return jnp.concatenate([a[r : r + 1], a[r + 1 : r + 2], b[r : r + 1], b[r + 1 : r + 2]], axis=1)

        for q in range(2):
            results = []
            for s in (2 * q, 2 * q + 1):
                packed = lambda row: jnp.broadcast_to(row, (16, 512)).astype(BF16)
                mid, at = packed(line(mids[0], mids[1], s)), packed(line(lanes[0], lanes[1], s))
                pieces = [packed(line(piece, -piece, s)) for piece in (hi, lo, act)]
                hits = [mid == numbers[0], mid == numbers[1]]
                none, one = jnp.zeros((16, 512), BF16), jnp.ones((16, 512), BF16)
                left = jnp.concatenate([jnp.where(hit, piece, none) for piece in pieces for hit in hits], axis=0)
                right = jnp.concatenate([jnp.where(at == number, one, none) for number in numbers], axis=0)
                out = lax.dot_general(left, right, (((1,), (1,)), ((), ())), preferred_element_type=F32)
                results.append((out[0:32] + out[32:64], out[64:96]))
            row = pl.ds(pl.multiple_of((2 * (group % 4) + q) * 8, 8), 8)
            for dst, e, o in ((s_ref, results[0][0], results[1][0]), (n_ref, results[0][1], results[1][1])):
                for j in range(4):
                    ej, oj = e[8 * j : 8 * j + 8], o[8 * j : 8 * j + 8]
                    dst[x, row, 256 * j : 256 * j + 128] = jnp.where(low, ej, oj)
                    dst[x, row, 256 * j + 128 : 256 * j + 256] = pltpu.roll(jnp.where(low, oj, ej), 4, 0)
        return carry

    lax.fori_loop(0, 16, body, 0, unroll=4)


def edge_rows(mine, below, above):
    sub = iota((8, 1024), 0)
    bottom = (sub < 3) & (mine != 3)
    top = (sub >= 5) & (mine != 0)
    return jnp.where(bottom, above, jnp.where(top, below, 0.0))


def early_edge_kernel(below_ref, above_ref, far_ref, cell_ref, after, y_ref, table_ref, a_ref, b_ref):
    par, has_b, mine, v = place()
    for x in range(8):
        y_ref[x] = edge_rows(mine, below_ref[x], above_ref[x])
    table = jnp.concatenate(
        [cell_ref[...], below_ref[8, 0:1, 0:128], far_ref[...], above_ref[8, 0:1, 0:128],
         jnp.zeros((4, 128), F32)], axis=0)
    table_ref[...] = table
    for i in range(2):
        a_ref[i] = y_ref[plane_of(par, 3 - i)]
        b_ref[i] = y_ref[plane_of(par, i)]
    for ref in (a_ref, b_ref):
        ref[2] = jnp.zeros((8, 1024), F32)
        ref[2, :, 0:128] = table


def late_edge_kernel(below_ref, above_ref, after, y_ref, a_ref, b_ref):
    par, has_b, mine, v = place()
    for x in range(4):
        y_ref[x] = edge_rows(mine, below_ref[x], above_ref[x])
    for i in range(2):
        a_ref[i] = y_ref[plane_of(par, 3 - i)]
        b_ref[i] = y_ref[plane_of(par, i)]


def reader(par, inside, own, a, b, y, ca=None, cb=None, own_y=0):
    def get(e, t):
        rows = slice(8 * t, 8 * t + 8)
        if 3 <= e <= 6:
            x = plane_of(par, e - 3)
            return own[x, rows, :] if t < 8 else y[own_y + x]
        halo, corner, i = (a, ca, e - 7) if e > 6 else (b, cb, 2 - e)
        value = halo[i, rows, :] if t < 8 else corner[i]
        return value if e > 6 else value * inside

    return get


def stored(*held):
    def get(e, t):
        for ref, start, stop in held:
            if start <= e < stop:
                return ref[e - start, 8 * t : 8 * t + 8, :]

    return get


class Plane:
    def __init__(self, get, e):
        self.get, self.e = get, e
        self.sub = iota((8, 1024), 0)
        self.kept = {}

    def turned(self, t, by, keep):
        found = self.kept.pop((t, by), None)
        if found is None:
            found = pltpu.roll(self.get(self.e, t), by, 0)
            if keep:
                self.kept[t, by] = found
        return found

    def views(self, t):
        get, e = self.get, self.e
        c = get(e, t)
        ym = jnp.where(self.sub == 0, self.turned((t + 8) % 9, 1, False), self.turned(t, 1, True))
        yp = jnp.where(self.sub == 7, self.turned((t + 1) % 9, 7, t < 8), self.turned(t, 7, False))
        return c, get(e - 1, t), get(e + 1, t), ym, yp, pltpu.roll(c, 1, 1), pltpu.roll(c, 1023, 1)


def inverse(x):
    rec = pl.reciprocal(x, approx=True)
    return rec * (2.0 - x * rec)


def couplings(plane, t):
    lane = iota((8, 1024), 1)
    c, xm, xp, ym, yp, zm, zp = plane.views(t)
    first, last = lane == 0, lane == 1023
    c = 0.25 * c
    xm, xp, ym, yp = (c + 0.25 * other for other in (xm, xp, ym, yp))
    zm = c + 0.25 * jnp.where(first, 0.0, zm)
    zp = c + 0.25 * jnp.where(last, 0.0, zp)
    inv = inverse(1.0 + (((xm + xp) + (ym + yp)) + (zm + zp)))
    return (xm, xp, ym, yp, jnp.where(first, 0.0, zm), jnp.where(last, 0.0, zp)), inv


def weighted(fs, views):
    t = [f * v for f, v in zip(fs, views)]
    return ((t[0] + t[1]) + (t[2] + t[3])) + (t[4] + t[5])


def prepare_kernel(p_ref, c_ref, a_ref, b_ref, y_ref, s_ref, n_ref, w_ref, k_ref):
    par, has_b, mine, v = place()
    inside = jnp.where(has_b, 1.0, 0.0)
    conduct = reader(par, inside, c_ref, a_ref, b_ref, y_ref)
    own = reader(par, inside, p_ref, a_ref.at[3:4], b_ref.at[3:4], y_ref, own_y=4)
    for e in range(3, 7):
        x = plane_of(par, e - 3)
        pc, pp = Plane(conduct, e), Plane(own, e)
        for t in range(8):
            rows = slice(8 * t, 8 * t + 8)
            fs, inv = couplings(pc, t)
            p, *views = pp.views(t)
            w_ref[x, rows, :] = (p + weighted(fs, views) - 0.5 * s_ref[x, rows, :]) * inv - p
            k_ref[x, rows, :] = (-0.5 * inv) * n_ref[x, rows, :]


def gap_kernel(table_ref, ta_ref, tb_ref, part_ref, cond_ref, ion_ref, act_ref, w_ref, k_ref,
               u_ref, a_ref, b_ref, up_ref, down_ref, mem_ref, spread):
    par, has_b, mine, v = place()
    part = part_ref[...]
    brick = part >> 6
    bx, by = brick >> 2, brick & 3
    side = jnp.where(bx == v, 0, jnp.where(bx == (v ^ 1), 1, 2))
    row = side * 4 + ((mine - by) & 3)
    lane = (part & 63) * 2
    tables = (table_ref[...], ta_ref[2, :, 0:128], tb_ref[2, :, 0:128])
    other = jnp.zeros((8, 128), F32)
    for r in range(12):
        line = jnp.broadcast_to(tables[r // 4][r % 4 : r % 4 + 1], (8, 128))
        other = jnp.where(row == r, jnp.take_along_axis(line, lane, axis=1, mode="promise_in_bounds"), other)
    own = tables[0][0:1]
    current = jnp.sum(cond_ref[...] * (own - other), axis=0, keepdims=True)
    act = act_ref[...]
    count = pair_sum(jnp.sum(jnp.transpose(act), axis=0, keepdims=True))
    g = current / jnp.maximum(count, 1.0)
    g8 = jnp.broadcast_to(g, (8, 128))
    mem_ref[...] = ion_ref[...] + act * jnp.transpose(jnp.broadcast_to(g, (128, 128)))
    for half in range(2):
        at = 64 * half + 2 * (iota((8, 128), 1) // 4)
        wide = jnp.take_along_axis(g8, at, axis=1, mode="promise_in_bounds")[0:1]
        spread[128 * half : 128 * half + 128, :] = jnp.transpose(jnp.broadcast_to(wide, (128, 128)))
    for j in range(4):
        x = plane_of(par, j)
        for t in range(8):
            rows = slice(8 * t, 8 * t + 8)
            gt = jnp.tile(spread[pl.ds(pl.multiple_of(x * 64 + 8 * t, 8), 8), :], (1, 8))
            u = w_ref[x, rows, :] + k_ref[x, rows, :] * gt
            u_ref[x, rows, :] = u
            if t == 0:
                down_ref[x] = u
            if t == 7:
                up_ref[x] = u
            if j < 3:
                b_ref[j, rows, :] = u
            if j > 0:
                a_ref[3 - j, rows, :] = u


def operator_kernel(c_ref, a_ref, b_ref, y_ref, ca_ref, cb_ref, after, fx, fym, fyp, fzm, fzp, inv_ref):
    par, has_b, mine, v = place()
    inside = jnp.where(has_b, 1.0, 0.0)
    conduct = reader(par, inside, c_ref, a_ref, b_ref, y_ref, ca_ref, cb_ref)
    sub = iota((8, 1024), 0)
    bottom = (sub < 3) & (mine != 3)
    top = (sub >= 5) & (mine != 0)
    keep = jnp.where(bottom | top, 1.0, 0.0)
    for e in range(1, 9):
        plane = Plane(conduct, e)
        for t in range(8 if e in (1, 8) else 9):
            rows = slice(8 * t, 8 * t + 8)
            fs, inv = couplings(plane, t)
            if e < 3:
                inv = inv * inside
            inv_ref[e - 1, rows, :] = inv * keep if t == 8 else inv
            if e == 1 or (e == 2 and t == 8):
                fx[e - 1, rows, :] = fs[0]
            fx[e, rows, :] = fs[1]
            for ref, f in zip((fym, fyp, fzm, fzp), fs[2:]):
                ref[e - 1, rows, :] = f


def coupled(coef, get, plane, t):
    fx, fym, fyp, fzm, fzp, inv = coef
    e = plane.e
    rows = slice(8 * t, 8 * t + 8)
    fs = [fx[e - 1, rows, :], fx[e, rows, :]] + [f[e - 1, rows, :] for f in (fym, fyp, fzm, fzp)]
    u, *views = plane.views(t)
    return u, inv[e - 1, rows, :] * weighted(fs, views)


def put(held, e, t, value):
    for ref, start, stop in held:
        if start <= e < stop:
            ref[e - start, 8 * t : 8 * t + 8, :] = value


def step_one(coef, u0, e, r_held, u1_held):
    a, b = sweep_factors()[0]
    plane = Plane(u0, e)
    for t in range(8 if e in (1, 8) else 9):
        u, res = coupled(coef, u0, plane, t)
        put(r_held, e, t, res)
        put(u1_held, e, t, a * u + b * res)


def step_two(coef, u1, r, e, r_held, u2_held):
    a, b = sweep_factors()[1]
    plane = Plane(u1, e)
    for t in range(8 if e in (2, 7) else 9):
        u, more = coupled(coef, u1, plane, t)
        res = (r(e, t) - u) + more
        put(r_held, e, t, res)
        put(u2_held, e, t, a * u + b * res)


def step_three(coef, p_ref, u0, u1, u2, r, e, x, out_ref, at):
    a, b = sweep_factors()[2]
    plane = Plane(u2, e)
    for t in range(8):
        rows = slice(8 * t, 8 * t + 8)
        u, more = coupled(coef, u2, plane, t)
        res = (r(e, t) - u) + more
        before = (p_ref[x, rows, :] + u0(e, t)) + (u1(e, t) + u)
        out_ref[at, rows, :] = before + (a * u + b * res)


def near_kernel(p_ref, fx, fym, fyp, fzm, fzp, inv, u_ref, a_ref, y_ref, ca_ref,
                u1_out, r_out, u2_out, done_ref, u1_far, r_far, u2_far):
    par, has_b, mine, v = place()
    inside = jnp.where(has_b, 1.0, 0.0)
    coef = (fx, fym, fyp, fzm, fzp, inv)
    u0 = reader(par, inside, u_ref, a_ref, None, y_ref, ca_ref)
    u1_held = ((u1_out, 4, 6), (u1_far, 6, 9))
    r1_held = ((r_out, 4, 5), (r_far, 5, 8))
    r2_held = ((r_out.at[1:2], 5, 6), (r_far.at[1:2], 6, 7))
    u2_held = ((u2_out, 5, 7), (u2_far, 7, 8))
    for e in (8, 7, 6, 5, 4):
        step_one(coef, u0, e, r1_held, u1_held)
    for e in (7, 6, 5):
        step_two(coef, stored(*u1_held), stored(*r1_held), e, r2_held, u2_held)
    step_three(coef, p_ref, u0, stored(*u1_held), stored(*u2_held), stored(*r2_held), 6, plane_of(par, 3), done_ref, 0)


def far_kernel(p_ref, fx, fym, fyp, fzm, fzp, inv, u_ref, b_ref, y_ref, cb_ref, u1_in, r_in, u2_in, done_ref,
               out_hbm, u1_far, r_far, u2_far, out_ref, sem):
    par, has_b, mine, v = place()
    inside = jnp.where(has_b, 1.0, 0.0)
    coef = (fx, fym, fyp, fzm, fzp, inv)
    u0 = reader(par, inside, u_ref, None, b_ref, y_ref, None, cb_ref)
    u1_new = ((u1_far, 1, 4),)
    u1 = stored(*u1_new, (u1_in, 4, 6))
    r1_new = ((r_far, 2, 4),)
    r1 = stored(*r1_new, (r_in, 4, 5))
    r2_new = ((r_far.at[2:4], 3, 5),)
    r2 = stored(*r2_new, (r_in.at[1:2], 5, 6))
    u2_new = ((u2_far, 2, 5),)
    u2 = stored(*u2_new, (u2_in, 5, 7))
    sends = begin([(done_ref.at[0], out_hbm.at[plane_of(par, 3)])], sem, 3)
    for e in (1, 2, 3):
        step_one(coef, u0, e, r1_new, u1_new)
    for e in (2, 3, 4):
        step_two(coef, u1, r1, e, r2_new, u2_new)
    for e in (3, 4, 5):
        x = plane_of(par, e - 3)
        step_three(coef, p_ref, u0, u1, u2, r2, e, x, out_ref, e - 3)
        sends += begin([(out_ref.at[e - 3], out_hbm.at[x])], sem, e - 3)
    for send in sends:
        send.wait()


def near(*dims, kind=F32):
    return pltpu.VMEM(dims, kind)


def shape(*dims, kind=F32):
    return jax.ShapeDtypeStruct(dims, kind)


def per_device(potential, conductivity, ion_states, rate_scale, rate_slope, type_cond, reversal,
               facet_counts, intra_voxel, extra_voxel, cell_type, gap_partner, gap_cond):
    nv = lax.axis_size("vol")
    swap_a = [pair for i in range(0, nv, 2) for pair in ((i, i + 1), (i + 1, i))]
    swap_b = [pair for i in range(1, nv - 1, 2) for pair in ((i, i + 1), (i + 1, i))] + [(0, 0), (nv - 1, nv - 1)]
    on_mem = lambda x, pairs: lax.ppermute(x, "mem", pairs)
    ring = lambda d: [(i, (i + d) % 4) for i in range(4)]
    to_a = functools.partial(lax.ppermute, axis_name="vol", perm=swap_a)
    to_b = functools.partial(lax.ppermute, axis_name="vol", perm=swap_b)

    intra = intra_voxel.reshape(128, 128)
    extra = extra_voxel.reshape(128, 128)

    states_near, volt, cells, act, part_lane, cond_lane, send_a, send_b, send_up, send_down = pl.pallas_call(
        gather_kernel,
        out_shape=(near(40, 16384), near(128, 128), near(1, 128), near(128, 128),
                   near(8, 128, kind=jnp.int32), near(8, 128),
                   near(4, 64, 1024), near(4, 64, 1024), near(9, 8, 1024), near(9, 8, 1024)),
        in_specs=[SM] + [ANY] * 7,
        out_specs=(ANY,) * 10,
        scratch_shapes=[pltpu.VMEM((4, 64, 1024), F32), pltpu.VMEM((4, 64, 1024), F32),
                        pltpu.VMEM((128, 128), jnp.int32), pltpu.VMEM((128, 128), jnp.int32),
                        pltpu.VMEM((8, 64), jnp.int32), pltpu.VMEM((8, 64), F32), pltpu.VMEM((128, 128), F32),
                        pltpu.VMEM((1, 128), F32), pltpu.VMEM((128, 128), F32), pltpu.VMEM((8, 128), jnp.int32),
                        pltpu.VMEM((8, 128), F32), pltpu.VMEM((8, 1024), F32), pltpu.SemaphoreType.DMA((35,))],
        compiler_params=grant(54),
        cost_estimate=pl.CostEstimate(flops=4000000, bytes_accessed=5000000, transcendentals=0),
        name="voltages",
    )(facet_counts, potential, conductivity, intra, extra, gap_partner.T, gap_cond.T, ion_states)

    below, above, far = on_mem(send_up, ring(1)), on_mem(send_down, ring(3)), on_mem(cells, ring(2))
    early_b, early_a = to_b(send_b), to_a(send_a)

    states_next, ion = pl.pallas_call(
        ionic_kernel,
        out_shape=(shape(40, 16384), near(128, 128)),
        in_specs=[SM, SM] + [VM] * 7,
        out_specs=(ANY, VM),
        scratch_shapes=[pltpu.VMEM((40, 16384), F32), pltpu.VMEM((128, 128), F32),
                        pltpu.VMEM((10, 40, 128), F32), pltpu.SemaphoreType.DMA((CHUNKS,))],
        compiler_params=pltpu.CompilerParams(vmem_limit_bytes=ROOM),
        cost_estimate=pl.CostEstimate(flops=16000000, bytes_accessed=5300000, transcendentals=2600000),
        name="ionic",
    )(facet_counts, cell_type, volt, act, rate_scale, rate_slope, type_cond, reversal.reshape(1, 40), states_near)

    y_early, table, more_a, more_b = pl.pallas_call(
        early_edge_kernel,
        out_shape=(shape(8, 8, 1024), shape(8, 128), shape(3, 8, 1024), shape(3, 8, 1024)),
        in_specs=[VM] * 4 + [ANY],
        out_specs=(VM,) * 4,
        compiler_params=grant(6),
        cost_estimate=pl.CostEstimate(flops=300000, bytes_accessed=1000000, transcendentals=0),
        name="early_edges",
    )(below, above, far, cells, ion)
    more_b, more_a = to_b(more_b), to_a(more_a)

    source, count = pl.pallas_call(
        scatter_kernel,
        out_shape=(near(4, 64, 1024), near(4, 64, 1024)),
        in_specs=[VM] * 4 + [ANY],
        out_specs=(VM, VM),
        compiler_params=grant(12),
        cost_estimate=pl.CostEstimate(flops=800000000, bytes_accessed=2300000, transcendentals=0),
        name="scatter",
    )(ion, act, intra, extra, table)

    w, k = pl.pallas_call(
        prepare_kernel,
        out_shape=(shape(4, 64, 1024), shape(4, 64, 1024)),
        in_specs=[VM] * 7,
        out_specs=(VM, VM),
        compiler_params=grant(20),
        cost_estimate=pl.CostEstimate(flops=16000000, bytes_accessed=8000000, transcendentals=0),
        name="prepare",
    )(potential, conductivity, early_a, early_b, y_early, source, count)

    u, u_a, u_b, u_up, u_down, membrane = pl.pallas_call(
        gap_kernel,
        out_shape=(shape(4, 64, 1024), shape(3, 64, 1024), shape(3, 64, 1024), shape(4, 8, 1024),
                   shape(4, 8, 1024), shape(128, 128)),
        in_specs=[VM] * 9,
        out_specs=(VM,) * 6,
        scratch_shapes=[pltpu.VMEM((256, 128), F32)],
        compiler_params=grant(12),
        cost_estimate=pl.CostEstimate(flops=1000000, bytes_accessed=5000000, transcendentals=0),
        name="gap",
    )(table, more_a, more_b, part_lane, cond_lane, ion, act, w, k)

    late_b = to_b(u_b)
    low_rows, high_rows = on_mem(u_up, ring(1)), on_mem(u_down, ring(3))
    late_a = to_a(u_a)

    big = lambda n: pltpu.VMEM((n, 72, 1024), F32)
    operator = pl.pallas_call(
        operator_kernel,
        out_shape=(shape(9, 72, 1024),) + (shape(8, 72, 1024),) * 5,
        in_specs=[VM] * 6 + [ANY],
        out_specs=(VM,) * 6,
        compiler_params=grant(22),
        cost_estimate=pl.CostEstimate(flops=16000000, bytes_accessed=17000000, transcendentals=0),
        name="operator",
    )(conductivity, early_a, early_b, y_early, more_a, more_b, u_up)

    y_late, corner_a, corner_b = pl.pallas_call(
        late_edge_kernel,
        out_shape=(shape(4, 8, 1024), shape(2, 8, 1024), shape(2, 8, 1024)),
        in_specs=[VM, VM, ANY],
        out_specs=(VM,) * 3,
        compiler_params=grant(4),
        cost_estimate=pl.CostEstimate(flops=100000, bytes_accessed=500000, transcendentals=0),
        name="late_edges",
    )(low_rows, high_rows, operator[-1])
    corner_b, corner_a = to_b(corner_b), to_a(corner_a)

    u1, r, u2, done = pl.pallas_call(
        near_kernel,
        out_shape=(shape(2, 72, 1024), shape(2, 72, 1024), shape(2, 72, 1024), shape(1, 64, 1024)),
        in_specs=[VM] * 11,
        out_specs=(VM,) * 4,
        scratch_shapes=[big(3), big(3), big(1)],
        compiler_params=grant(30),
        cost_estimate=pl.CostEstimate(flops=25000000, bytes_accessed=10000000, transcendentals=0),
        name="near",
    )(potential, *operator, u, late_a, y_late, corner_a)

    potential_next = pl.pallas_call(
        far_kernel,
        out_shape=shape(4, 64, 1024),
        in_specs=[VM] * 15,
        out_specs=ANY,
        scratch_shapes=[big(3), big(4), big(3), pltpu.VMEM((3, 64, 1024), F32), pltpu.SemaphoreType.DMA((4,))],
        compiler_params=grant(30),
        cost_estimate=pl.CostEstimate(flops=25000000, bytes_accessed=10000000, transcendentals=0),
        name="far",
    )(potential, *operator, u, late_b, y_late, corner_b, u1, r, u2, done)
    return potential_next, states_next, membrane.reshape(16384)


def solution(mesh):
    in_specs = (
        P("vol", "mem", None), P("vol", "mem", None), P(None, ("vol", "mem")),
        P(), P(), P(), P(),
        P(("vol", "mem")), P(("vol", "mem")), P(("vol", "mem")), P(("vol", "mem")),
        P(("vol", "mem"), None), P(("vol", "mem"), None),
    )
    out_specs = (P("vol", "mem", None), P(None, ("vol", "mem")), P(("vol", "mem")))
    return jax.shard_map(per_device, mesh=mesh, in_specs=in_specs, out_specs=out_specs, check_vma=False)
```

```python
import functools

import jax
import jax.numpy as jnp
from jax import lax
from jax.experimental import pallas as pl
from jax.experimental.pallas import tpu as pltpu
from jax.sharding import PartitionSpec as P

SWEEPS = 4
F32 = jnp.float32
BF16 = jnp.bfloat16
ANY = pl.BlockSpec(memory_space=pl.ANY)
HBM = pl.BlockSpec(memory_space=pltpu.HBM)
VM = pl.BlockSpec(memory_space=pltpu.VMEM)
SM = pl.BlockSpec(memory_space=pltpu.SMEM)


def grant(mib):
    return pltpu.CompilerParams(vmem_limit_bytes=mib * 1024 * 1024)


def sweep_factors():
    theta, delta = 1.0, 0.8
    sigma = theta / delta
    rho = 1.0 / sigma
    factors = []
    for _ in range(SWEEPS - 1):
        rho_next = 1.0 / (2.0 * sigma - rho)
        factors.append((rho_next * rho, 2.0 * rho_next / delta))
        rho = rho_next
    return factors


def iota(shape, dim):
    return lax.broadcasted_iota(jnp.int32, shape, dim)


def place():
    v, mine = lax.axis_index("vol"), lax.axis_index("mem")
    return v & 1, (v != 0) & (v != lax.axis_size("vol") - 1), mine, v


def plane_of(parity, j):
    return j + parity * (3 - 2 * j)


def pair_sum(row):
    even = (iota((1, 128), 1) & 1) == 0
    return row + jnp.where(even, pltpu.roll(row, 127, 1), pltpu.roll(row, 1, 1))


def gather_kernel(cnt, p_hbm, c_hbm, in_hbm, ex_hbm, part_hbm, cond_hbm, st_hbm,
                  st_near, volt_hbm, cell_hbm, act_hbm, part_out, cond_out, a_hbm, b_hbm, up_hbm, down_hbm,
                  p_ref, c_ref, in_ref, ex_ref, part_ref, cond_ref, volt_ref, cell_ref, act_ref, part_two, cond_two,
                  note, sem):
    par, has_b, mine, v = place()
    loads = begin(
        [(in_hbm, in_ref), (ex_hbm, ex_ref)] + [(p_hbm.at[x], p_ref.at[x]) for x in range(4)]
        + [(c_hbm.at[x], c_ref.at[x]) for x in range(4)] + [(part_hbm, part_ref), (cond_hbm, cond_ref)], sem, 0)
    states = begin([(st_hbm.at[:, 4096 * i : 4096 * i + 4096], st_near.at[:, 4096 * i : 4096 * i + 4096]) for i in range(4)], sem, 31)
    twice = iota((8, 128), 1) // 2
    sub = iota((8, 128), 0)
    low = sub < 4
    lane_row = iota((1, 128), 1)

    def body(kk, carry):
        x = kk // 4
        blocks = [r[pl.ds(pl.multiple_of(8 * kk, 8), 8), :] & 4095 for r in (in_ref, ex_ref)]
        for q in range(2):
            row = pl.multiple_of((2 * (kk % 4) + q) * 8, 8)
            tiles = [p_ref[x, pl.ds(row, 8), 128 * z : 128 * z + 128] for z in range(8)]
            for h in range(2):
                picked = []
                for block in blocks:
                    a = jnp.broadcast_to(block[4 * q + h : 4 * q + h + 1], (8, 128))
                    b = jnp.broadcast_to(block[4 * q + 2 + h : 4 * q + 3 + h], (8, 128))
                    o = jnp.where(low, a, b)
                    lane = o & 127
                    z_of = (o >> 7) & 7
                    got = jnp.take_along_axis(tiles[0], lane, axis=1, mode="promise_in_bounds")
                    for z in range(1, 8):
                        new = jnp.take_along_axis(tiles[z], lane, axis=1, mode="promise_in_bounds")
                        got = jnp.where(z_of == z, new, got)
                    picked.append(jnp.where((o >> 10) == (sub & 3), got, 0.0))
                d = picked[0] - picked[1]
                d = d + pltpu.roll(d, 7, 0)
                d = d + pltpu.roll(d, 6, 0)
                for i in range(2):
                    at = pl.ds(8 * kk + 4 * q + 2 * i + h, 1)
                    volt_ref[at, :] = d[4 * i : 4 * i + 1]
                    used = lane_row + 128 * h < cnt[4 * kk + 2 * q + i]
                    act_ref[at, :] = jnp.where(used, 1.0, 0.0)
        return carry

    loads[0].wait()
    loads[1].wait()
    for x in range(4):
        if x < 2:
            loads[2 + x].wait()
        lax.fori_loop(4 * x, 4 * x + 4, body, 0, unroll=4)
        if x == 1:
            for load in loads[4:]:
                load.wait()
            copies = []
            for i in range(3):
                copies.append((c_ref.at[plane_of(par, i)], b_hbm.at[i]))
                copies.append((c_ref.at[plane_of(par, 3 - i)], a_hbm.at[i]))
            copies.append((p_ref.at[plane_of(par, 0)], b_hbm.at[3]))
            copies.append((p_ref.at[plane_of(par, 3)], a_hbm.at[3]))
            for k, src in enumerate((c_ref, p_ref)):
                copies.append((src.at[:, 56:64], up_hbm.at[4 * k : 4 * k + 4]))
                copies.append((src.at[:, 0:8], down_hbm.at[4 * k : 4 * k + 4]))
            for src, dst in ((part_ref, part_two), (cond_ref, cond_two)):
                wide = jnp.concatenate([src[...], src[...]], axis=1)
                dst[...] = jnp.take_along_axis(wide, twice, axis=1, mode="promise_in_bounds")
            copies += [(part_two, part_out), (cond_two, cond_out)]
            sends = begin(copies, sem, 12)
    sends += begin([(volt_ref, volt_hbm), (act_ref, act_hbm)], sem, 26)
    act = act_ref[...]
    total = jnp.sum(jnp.transpose(volt_ref[...] * act), axis=0, keepdims=True)
    count = jnp.sum(jnp.transpose(act), axis=0, keepdims=True)
    cells = pair_sum(total) / jnp.maximum(pair_sum(count), 1.0)
    cell_ref[...] = cells
    note[...] = jnp.zeros((8, 1024), F32)
    note[0:1, 0:128] = cells
    sends += begin([(note, up_hbm.at[8]), (note, down_hbm.at[8]), (cell_ref, cell_hbm)], sem, 28)
    for send in sends + states:
        send.wait()


def begin(copies, sem, start):
    made = [pltpu.make_async_copy(s, d, sem.at[start + n]) for n, (s, d) in enumerate(copies)]
    for m in made:
        m.start()
    return made


CHUNKS = 16
ROOM = 24000000


def ionic_kernel(cnt, typ, volt_ref, act_ref, scale_ref, slope_ref, cond_ref, rev_ref, st_ref,
                 out_hbm, ion_ref, out_ref, flat, rate_ref, sem):
    width = 16384 // CHUNKS
    at = lambda i: pl.ds(pl.multiple_of(i * width, width), width)
    store = lambda i: pltpu.make_async_copy(out_ref.at[:, at(i)], out_hbm.at[:, at(i)], sem.at[i])
    flat[...] = jnp.zeros((128, 128), F32)
    logs = jnp.log(scale_ref[...])
    flat[0:1, 0:40] = slope_ref[0:1]
    flat[1:2, 0:40] = logs[0:1]
    flat[2:3, 0:40] = -slope_ref[1:2]
    flat[3:4, 0:40] = logs[1:2]
    flat[4:7, 0:40] = cond_ref[...]
    flat[7:10, 0:40] = cond_ref[...] * rev_ref[...]
    turned = jnp.transpose(flat[...])
    for i in range(10):
        rate_ref[i] = jnp.broadcast_to(turned[0:40, i : i + 1], (40, 128))
    lane = iota((8, 128), 1)

    def body(group, carry):
        rows8 = pl.ds(pl.multiple_of(8 * group, 8), 8)
        volts = volt_ref[rows8, :]
        counts, types, v, active, cols = [], [], [], [], []
        for q in range(4):
            counts.append(cnt[4 * group + q])
            types.append(typ[4 * group + q])
        for r in range(8):
            v.append(jnp.broadcast_to(volts[r : r + 1], (8, 128)))
            active.append(lane + (r % 2) * 128 < counts[r // 2])
            cols.append(pl.ds(pl.multiple_of(1024 * group + 128 * r, 128), 128))
        w1, w2 = [None] * 8, [None] * 8
        for k in range(5):
            rows = slice(8 * k, 8 * k + 8)
            rate = [rate_ref[i, rows] for i in range(4)]
            for q in range(4):
                g, gr = rate_ref[4 + types[q], rows], rate_ref[7 + types[q], rows]
                for r in (2 * q, 2 * q + 1):
                    st = st_ref[rows, cols[r]]
                    opening = jnp.exp(rate[0] * v[r] + rate[1])
                    closing = jnp.exp(rate[2] * v[r] + rate[3])
                    total = opening + closing
                    steady = opening * inverse(total)
                    fresh = steady + (st - steady) * jnp.exp(total * -0.5)
                    out_ref[rows, cols[r]] = jnp.where(active[r], fresh, st)
                    w1[r] = g * fresh if k == 0 else w1[r] + g * fresh
                    w2[r] = gr * fresh if k == 0 else w2[r] + gr * fresh
        store(group).start()
        act = act_ref[rows8, :]
        ion = [jnp.sum(w1[r] * v[r] - w2[r], axis=0, keepdims=True) for r in range(8)]
        val = jnp.concatenate(ion, axis=0) * act
        ion_ref[rows8, :] = val
        return carry

    lax.fori_loop(0, CHUNKS, body, 0, unroll=2)
    for i in range(CHUNKS):
        store(i).wait()


def scatter_kernel(first, ion_ref, act_ref, in_ref, ex_ref, after, s_ref, n_ref):
    par, has_b, mine, v = place()
    numbers = [(iota((16, 512), 0) + 16 * k).astype(F32).astype(BF16) for k in range(8)]
    low = iota((8, 128), 0) < 4
    odd_row = (iota((8, 128), 0) & 2) // 2

    def body(turn, carry):
        group = 4 * plane_of(par, first + turn // 4) + turn % 4
        rows8 = pl.ds(pl.multiple_of(8 * group, 8), 8)
        val, act = ion_ref[rows8, :], act_ref[rows8, :]
        x = turn // 4
        hi = val.astype(BF16).astype(F32)
        lo = val - hi
        mids, lanes = [], []
        for ref in (in_ref, ex_ref):
            o = ref[rows8, :] & 4095
            mids.append(((((o >> 7) & 7) ^ odd_row) * 4 + (o >> 10)).astype(F32))
            lanes.append((o & 127).astype(F32))

        def line(a, b, s):
            r = 2 * s
            return jnp.concatenate([a[r : r + 1], a[r + 1 : r + 2], b[r : r + 1], b[r + 1 : r + 2]], axis=1)

        for q in range(2):
            results = []
            for s in (2 * q, 2 * q + 1):
                packed = lambda row: jnp.broadcast_to(row, (16, 512)).astype(BF16)
                mid, at = packed(line(mids[0], mids[1], s)), packed(line(lanes[0], lanes[1], s))
                pieces = [packed(line(piece, -piece, s)) for piece in (hi, lo, act)]
                hits = [mid == numbers[0], mid == numbers[1]]
                none, one = jnp.zeros((16, 512), BF16), jnp.ones((16, 512), BF16)
                left = jnp.concatenate([jnp.where(hit, piece, none) for piece in pieces for hit in hits], axis=0)
                right = jnp.concatenate([jnp.where(at == number, one, none) for number in numbers], axis=0)
                out = lax.dot_general(left, right, (((1,), (1,)), ((), ())), preferred_element_type=F32)
                results.append((out[0:32] + out[32:64], out[64:96]))
            row = pl.ds(pl.multiple_of((2 * (turn % 4) + q) * 8, 8), 8)
            for dst, e, o in ((s_ref, results[0][0], results[1][0]), (n_ref, results[0][1], results[1][1])):
                for j in range(4):
                    ej, oj = e[8 * j : 8 * j + 8], o[8 * j : 8 * j + 8]
                    dst[x, row, 256 * j : 256 * j + 128] = jnp.where(low, ej, oj)
                    dst[x, row, 256 * j + 128 : 256 * j + 256] = pltpu.roll(jnp.where(low, oj, ej), 4, 0)
        return carry

    lax.fori_loop(0, 8, body, 0, unroll=4)


def edge_rows(mine, below, above):
    sub = iota((8, 1024), 0)
    bottom = (sub < 3) & (mine != 3)
    top = (sub >= 5) & (mine != 0)
    return jnp.where(bottom, above, jnp.where(top, below, 0.0))


def early_edge_kernel(below_ref, above_ref, far_ref, cell_ref, after, y_ref, table_ref, a_ref, b_ref):
    par, has_b, mine, v = place()
    for x in range(8):
        y_ref[x] = edge_rows(mine, below_ref[x], above_ref[x])
    table = jnp.concatenate(
        [cell_ref[...], below_ref[8, 0:1, 0:128], far_ref[...], above_ref[8, 0:1, 0:128],
         jnp.zeros((4, 128), F32)], axis=0)
    table_ref[...] = table
    for i in range(2):
        a_ref[i] = y_ref[plane_of(par, 3 - i)]
        b_ref[i] = y_ref[plane_of(par, i)]
    for ref in (a_ref, b_ref):
        ref[2] = jnp.zeros((8, 1024), F32)
        ref[2, :, 0:128] = table


def late_edge_kernel(below_ref, above_ref, after, y_ref, a_ref, b_ref):
    par, has_b, mine, v = place()
    for x in range(4):
        y_ref[x] = edge_rows(mine, below_ref[x], above_ref[x])
    for i in range(2):
        a_ref[i] = y_ref[plane_of(par, 3 - i)]
        b_ref[i] = y_ref[plane_of(par, i)]


def reader(par, inside, own, a, b, y, ca=None, cb=None, own_y=0):
    def get(e, t):
        rows = slice(8 * t, 8 * t + 8)
        if 3 <= e <= 6:
            x = plane_of(par, e - 3)
            return own[x, rows, :] if t < 8 else y[own_y + x]
        halo, corner, i = (a, ca, e - 7) if e > 6 else (b, cb, 2 - e)
        value = halo[i, rows, :] if t < 8 else corner[i]
        return value if e > 6 else value * inside

    return get


def stored(*held):
    def get(e, t):
        for ref, start, stop in held:
            if start <= e < stop:
                return ref[e - start, 8 * t : 8 * t + 8, :]

    return get


class Plane:
    def __init__(self, get, e):
        self.get, self.e = get, e
        self.sub = iota((8, 1024), 0)
        self.kept = {}

    def turned(self, t, by, keep):
        found = self.kept.pop((t, by), None)
        if found is None:
            found = pltpu.roll(self.get(self.e, t), by, 0)
            if keep:
                self.kept[t, by] = found
        return found

    def views(self, t):
        get, e = self.get, self.e
        c = get(e, t)
        ym = jnp.where(self.sub == 0, self.turned((t + 8) % 9, 1, False), self.turned(t, 1, True))
        yp = jnp.where(self.sub == 7, self.turned((t + 1) % 9, 7, t < 8), self.turned(t, 7, False))
        return c, get(e - 1, t), get(e + 1, t), ym, yp, pltpu.roll(c, 1, 1), pltpu.roll(c, 1023, 1)


def inverse(x):
    rec = pl.reciprocal(x, approx=True)
    return rec * (2.0 - x * rec)


def couplings(plane, t):
    lane = iota((8, 1024), 1)
    c, xm, xp, ym, yp, zm, zp = plane.views(t)
    first, last = lane == 0, lane == 1023
    c = 0.25 * c
    xm, xp, ym, yp = (c + 0.25 * other for other in (xm, xp, ym, yp))
    zm = c + 0.25 * jnp.where(first, 0.0, zm)
    zp = c + 0.25 * jnp.where(last, 0.0, zp)
    inv = inverse(1.0 + (((xm + xp) + (ym + yp)) + (zm + zp)))
    return (xm, xp, ym, yp, jnp.where(first, 0.0, zm), jnp.where(last, 0.0, zp)), inv


def weighted(fs, views):
    t = [f * v for f, v in zip(fs, views)]
    return ((t[0] + t[1]) + (t[2] + t[3])) + (t[4] + t[5])


def prepare_kernel(p_ref, c_ref, a_ref, b_ref, y_ref, s_one, n_one, s_two, n_two, w_ref, k_ref):
    par, has_b, mine, v = place()
    inside = jnp.where(has_b, 1.0, 0.0)
    conduct = reader(par, inside, c_ref, a_ref, b_ref, y_ref)
    own = reader(par, inside, p_ref, a_ref.at[3:4], b_ref.at[3:4], y_ref, own_y=4)
    for e in range(3, 7):
        x = plane_of(par, e - 3)
        s_ref, n_ref = (s_one, n_one) if e < 5 else (s_two, n_two)
        at = (e - 3) % 2
        pc, pp = Plane(conduct, e), Plane(own, e)
        for t in range(8):
            rows = slice(8 * t, 8 * t + 8)
            fs, inv = couplings(pc, t)
            p, *views = pp.views(t)
            w_ref[x, rows, :] = (p + weighted(fs, views) - 0.5 * s_ref[at, rows, :]) * inv - p
            k_ref[x, rows, :] = (-0.5 * inv) * n_ref[at, rows, :]


def gap_kernel(table_ref, ta_ref, tb_ref, part_ref, cond_ref, ion_ref, act_ref, w_ref, k_ref,
               u_ref, a_ref, b_ref, up_ref, down_ref, mem_ref, spread):
    par, has_b, mine, v = place()
    part = part_ref[...]
    brick = part >> 6
    bx, by = brick >> 2, brick & 3
    side = jnp.where(bx == v, 0, jnp.where(bx == (v ^ 1), 1, 2))
    row = side * 4 + ((mine - by) & 3)
    lane = (part & 63) * 2
    tables = (table_ref[...], ta_ref[2, :, 0:128], tb_ref[2, :, 0:128])
    other = jnp.zeros((8, 128), F32)
    for r in range(12):
        line = jnp.broadcast_to(tables[r // 4][r % 4 : r % 4 + 1], (8, 128))
        other = jnp.where(row == r, jnp.take_along_axis(line, lane, axis=1, mode="promise_in_bounds"), other)
    own = tables[0][0:1]
    current = jnp.sum(cond_ref[...] * (own - other), axis=0, keepdims=True)
    act = act_ref[...]
    count = pair_sum(jnp.sum(jnp.transpose(act), axis=0, keepdims=True))
    g = current / jnp.maximum(count, 1.0)
    g8 = jnp.broadcast_to(g, (8, 128))
    mem_ref[...] = ion_ref[...] + act * jnp.transpose(jnp.broadcast_to(g, (128, 128)))
    for half in range(2):
        at = 64 * half + 2 * (iota((8, 128), 1) // 4)
        wide = jnp.take_along_axis(g8, at, axis=1, mode="promise_in_bounds")[0:1]
        spread[128 * half : 128 * half + 128, :] = jnp.transpose(jnp.broadcast_to(wide, (128, 128)))
    for j in range(4):
        x = plane_of(par, j)
        for t in range(8):
            rows = slice(8 * t, 8 * t + 8)
            gt = jnp.tile(spread[pl.ds(pl.multiple_of(x * 64 + 8 * t, 8), 8), :], (1, 8))
            u = w_ref[x, rows, :] + k_ref[x, rows, :] * gt
            u_ref[x, rows, :] = u
            if t == 0:
                down_ref[x] = u
            if t == 7:
                up_ref[x] = u
            if j < 3:
                b_ref[j, rows, :] = u
            if j > 0:
                a_ref[3 - j, rows, :] = u


def operator_kernel(c_ref, a_ref, b_ref, y_ref, ca_ref, cb_ref, after, fx, fym, fyp, fzm, fzp, inv_ref):
    par, has_b, mine, v = place()
    inside = jnp.where(has_b, 1.0, 0.0)
    conduct = reader(par, inside, c_ref, a_ref, b_ref, y_ref, ca_ref, cb_ref)
    sub = iota((8, 1024), 0)
    bottom = (sub < 3) & (mine != 3)
    top = (sub >= 5) & (mine != 0)
    keep = jnp.where(bottom | top, 1.0, 0.0)
    for e in range(1, 9):
        plane = Plane(conduct, e)
        for t in range(8 if e in (1, 8) else 9):
            rows = slice(8 * t, 8 * t + 8)
            fs, inv = couplings(plane, t)
            if e < 3:
                inv = inv * inside
            inv_ref[e - 1, rows, :] = inv * keep if t == 8 else inv
            if e == 1 or (e == 2 and t == 8):
                fx[e - 1, rows, :] = fs[0]
            fx[e, rows, :] = fs[1]
            for ref, f in zip((fym, fyp, fzm, fzp), fs[2:]):
                ref[e - 1, rows, :] = f


def coupled(coef, get, plane, t):
    fx, fym, fyp, fzm, fzp, inv = coef
    e = plane.e
    rows = slice(8 * t, 8 * t + 8)
    fs = [fx[e - 1, rows, :], fx[e, rows, :]] + [f[e - 1, rows, :] for f in (fym, fyp, fzm, fzp)]
    u, *views = plane.views(t)
    return u, inv[e - 1, rows, :] * weighted(fs, views)


def put(held, e, t, value):
    for ref, start, stop in held:
        if start <= e < stop:
            ref[e - start, 8 * t : 8 * t + 8, :] = value


def step_one(coef, u0, e, r_held, u1_held):
    a, b = sweep_factors()[0]
    plane = Plane(u0, e)
    for t in range(8 if e in (1, 8) else 9):
        u, res = coupled(coef, u0, plane, t)
        put(r_held, e, t, res)
        put(u1_held, e, t, a * u + b * res)


def step_two(coef, u1, r, e, r_held, u2_held):
    a, b = sweep_factors()[1]
    plane = Plane(u1, e)
    for t in range(8 if e in (2, 7) else 9):
        u, more = coupled(coef, u1, plane, t)
        res = (r(e, t) - u) + more
        put(r_held, e, t, res)
        put(u2_held, e, t, a * u + b * res)


def step_three(coef, p_ref, u0, u1, u2, r, e, x, out_ref, at):
    a, b = sweep_factors()[2]
    plane = Plane(u2, e)
    for t in range(8):
        rows = slice(8 * t, 8 * t + 8)
        u, more = coupled(coef, u2, plane, t)
        res = (r(e, t) - u) + more
        before = (p_ref[x, rows, :] + u0(e, t)) + (u1(e, t) + u)
        out_ref[at, rows, :] = before + (a * u + b * res)


def near_kernel(p_ref, fx, fym, fyp, fzm, fzp, inv, u_ref, a_ref, y_ref, ca_ref,
                u1_out, r_out, u2_out, done_ref, u1_far, r_far, u2_far):
    par, has_b, mine, v = place()
    inside = jnp.where(has_b, 1.0, 0.0)
    coef = (fx, fym, fyp, fzm, fzp, inv)
    u0 = reader(par, inside, u_ref, a_ref, None, y_ref, ca_ref)
    u1_held = ((u1_out, 4, 6), (u1_far, 6, 9))
    r1_held = ((r_out, 4, 5), (r_far, 5, 8))
    r2_held = ((r_out.at[1:2], 5, 6), (r_far.at[1:2], 6, 7))
    u2_held = ((u2_out, 5, 7), (u2_far, 7, 8))
    for e in (8, 7, 6, 5, 4):
        step_one(coef, u0, e, r1_held, u1_held)
    for e in (7, 6, 5):
        step_two(coef, stored(*u1_held), stored(*r1_held), e, r2_held, u2_held)
    step_three(coef, p_ref, u0, stored(*u1_held), stored(*u2_held), stored(*r2_held), 6, plane_of(par, 3), done_ref, 0)


def far_kernel(p_ref, fx, fym, fyp, fzm, fzp, inv, u_ref, b_ref, y_ref, cb_ref, u1_in, r_in, u2_in, done_ref,
               out_hbm, u1_far, r_far, u2_far, out_ref, sem):
    par, has_b, mine, v = place()
    inside = jnp.where(has_b, 1.0, 0.0)
    coef = (fx, fym, fyp, fzm, fzp, inv)
    u0 = reader(par, inside, u_ref, None, b_ref, y_ref, None, cb_ref)
    u1_new = ((u1_far, 1, 4),)
    u1 = stored(*u1_new, (u1_in, 4, 6))
    r1_new = ((r_far, 2, 4),)
    r1 = stored(*r1_new, (r_in, 4, 5))
    r2_new = ((r_far.at[2:4], 3, 5),)
    r2 = stored(*r2_new, (r_in.at[1:2], 5, 6))
    u2_new = ((u2_far, 2, 5),)
    u2 = stored(*u2_new, (u2_in, 5, 7))
    sends = begin([(done_ref.at[0], out_hbm.at[plane_of(par, 3)])], sem, 3)
    for e in (1, 2, 3):
        step_one(coef, u0, e, r1_new, u1_new)
    for e in (2, 3, 4):
        step_two(coef, u1, r1, e, r2_new, u2_new)
    for e in (3, 4, 5):
        x = plane_of(par, e - 3)
        step_three(coef, p_ref, u0, u1, u2, r2, e, x, out_ref, e - 3)
        sends += begin([(out_ref.at[e - 3], out_hbm.at[x])], sem, e - 3)
    for send in sends:
        send.wait()


def near(*dims, kind=F32):
    return pltpu.VMEM(dims, kind)


def shape(*dims, kind=F32):
    return jax.ShapeDtypeStruct(dims, kind)


def per_device(potential, conductivity, ion_states, rate_scale, rate_slope, type_cond, reversal,
               facet_counts, intra_voxel, extra_voxel, cell_type, gap_partner, gap_cond):
    nv = lax.axis_size("vol")
    swap_a = [pair for i in range(0, nv, 2) for pair in ((i, i + 1), (i + 1, i))]
    swap_b = [pair for i in range(1, nv - 1, 2) for pair in ((i, i + 1), (i + 1, i))] + [(0, 0), (nv - 1, nv - 1)]
    on_mem = lambda x, pairs: lax.ppermute(x, "mem", pairs)
    ring = lambda d: [(i, (i + d) % 4) for i in range(4)]
    to_a = functools.partial(lax.ppermute, axis_name="vol", perm=swap_a)
    to_b = functools.partial(lax.ppermute, axis_name="vol", perm=swap_b)

    intra = intra_voxel.reshape(128, 128)
    extra = extra_voxel.reshape(128, 128)

    states_near, volt, cells, act, part_lane, cond_lane, send_a, send_b, send_up, send_down = pl.pallas_call(
        gather_kernel,
        out_shape=(near(40, 16384), near(128, 128), near(1, 128), near(128, 128),
                   near(8, 128, kind=jnp.int32), near(8, 128),
                   near(4, 64, 1024), near(4, 64, 1024), near(9, 8, 1024), near(9, 8, 1024)),
        in_specs=[SM] + [ANY] * 7,
        out_specs=(ANY,) * 10,
        scratch_shapes=[pltpu.VMEM((4, 64, 1024), F32), pltpu.VMEM((4, 64, 1024), F32),
                        pltpu.VMEM((128, 128), jnp.int32), pltpu.VMEM((128, 128), jnp.int32),
                        pltpu.VMEM((8, 64), jnp.int32), pltpu.VMEM((8, 64), F32), pltpu.VMEM((128, 128), F32),
                        pltpu.VMEM((1, 128), F32), pltpu.VMEM((128, 128), F32), pltpu.VMEM((8, 128), jnp.int32),
                        pltpu.VMEM((8, 128), F32), pltpu.VMEM((8, 1024), F32), pltpu.SemaphoreType.DMA((35,))],
        compiler_params=grant(54),
        cost_estimate=pl.CostEstimate(flops=4000000, bytes_accessed=5000000, transcendentals=0),
        name="voltages",
    )(facet_counts, potential, conductivity, intra, extra, gap_partner.T, gap_cond.T, ion_states)

    below, above, far = on_mem(send_up, ring(1)), on_mem(send_down, ring(3)), on_mem(cells, ring(2))
    early_b, early_a = to_b(send_b), to_a(send_a)

    states_next, ion = pl.pallas_call(
        ionic_kernel,
        out_shape=(shape(40, 16384), near(128, 128)),
        in_specs=[SM, SM] + [VM] * 7,
        out_specs=(ANY, VM),
        scratch_shapes=[pltpu.VMEM((40, 16384), F32), pltpu.VMEM((128, 128), F32),
                        pltpu.VMEM((10, 40, 128), F32), pltpu.SemaphoreType.DMA((CHUNKS,))],
        compiler_params=pltpu.CompilerParams(vmem_limit_bytes=ROOM),
        cost_estimate=pl.CostEstimate(flops=16000000, bytes_accessed=5300000, transcendentals=2600000),
        name="ionic",
    )(facet_counts, cell_type, volt, act, rate_scale, rate_slope, type_cond, reversal.reshape(1, 40), states_near)

    def scatter(first, after):
        return pl.pallas_call(
            functools.partial(scatter_kernel, first),
            out_shape=(near(2, 64, 1024), near(2, 64, 1024)),
            in_specs=[VM] * 4 + [ANY],
            out_specs=(VM, VM),
            compiler_params=grant(12),
            cost_estimate=pl.CostEstimate(flops=400000000, bytes_accessed=1200000, transcendentals=0),
            name="scatter",
        )(ion, act, intra, extra, after)

    half_one = scatter(0, volt)

    y_early, table, more_a, more_b = pl.pallas_call(
        early_edge_kernel,
        out_shape=(shape(8, 8, 1024), shape(8, 128), shape(3, 8, 1024), shape(3, 8, 1024)),
        in_specs=[VM] * 4 + [ANY],
        out_specs=(VM,) * 4,
        compiler_params=grant(6),
        cost_estimate=pl.CostEstimate(flops=300000, bytes_accessed=1000000, transcendentals=0),
        name="early_edges",
    )(below, above, far, cells, half_one[0])
    more_b, more_a = to_b(more_b), to_a(more_a)

    half_two = scatter(2, table)

    w, k = pl.pallas_call(
        prepare_kernel,
        out_shape=(shape(4, 64, 1024), shape(4, 64, 1024)),
        in_specs=[VM] * 9,
        out_specs=(VM, VM),
        compiler_params=grant(20),
        cost_estimate=pl.CostEstimate(flops=16000000, bytes_accessed=8000000, transcendentals=0),
        name="prepare",
    )(potential, conductivity, early_a, early_b, y_early, *half_one, *half_two)

    u, u_a, u_b, u_up, u_down, membrane = pl.pallas_call(
        gap_kernel,
        out_shape=(shape(4, 64, 1024), shape(3, 64, 1024), shape(3, 64, 1024), shape(4, 8, 1024),
                   shape(4, 8, 1024), shape(128, 128)),
        in_specs=[VM] * 9,
        out_specs=(VM,) * 6,
        scratch_shapes=[pltpu.VMEM((256, 128), F32)],
        compiler_params=grant(12),
        cost_estimate=pl.CostEstimate(flops=1000000, bytes_accessed=5000000, transcendentals=0),
        name="gap",
    )(table, more_a, more_b, part_lane, cond_lane, ion, act, w, k)

    late_b = to_b(u_b)
    low_rows, high_rows = on_mem(u_up, ring(1)), on_mem(u_down, ring(3))
    late_a = to_a(u_a)

    big = lambda n: pltpu.VMEM((n, 72, 1024), F32)
    operator = pl.pallas_call(
        operator_kernel,
        out_shape=(shape(9, 72, 1024),) + (shape(8, 72, 1024),) * 5,
        in_specs=[VM] * 6 + [ANY],
        out_specs=(VM,) * 6,
        compiler_params=grant(22),
        cost_estimate=pl.CostEstimate(flops=16000000, bytes_accessed=17000000, transcendentals=0),
        name="operator",
    )(conductivity, early_a, early_b, y_early, more_a, more_b, u_up)

    y_late, corner_a, corner_b = pl.pallas_call(
        late_edge_kernel,
        out_shape=(shape(4, 8, 1024), shape(2, 8, 1024), shape(2, 8, 1024)),
        in_specs=[VM, VM, ANY],
        out_specs=(VM,) * 3,
        compiler_params=grant(4),
        cost_estimate=pl.CostEstimate(flops=100000, bytes_accessed=500000, transcendentals=0),
        name="late_edges",
    )(low_rows, high_rows, operator[-1])
    corner_b, corner_a = to_b(corner_b), to_a(corner_a)

    u1, r, u2, done = pl.pallas_call(
        near_kernel,
        out_shape=(shape(2, 72, 1024), shape(2, 72, 1024), shape(2, 72, 1024), shape(1, 64, 1024)),
        in_specs=[VM] * 11,
        out_specs=(VM,) * 4,
        scratch_shapes=[big(3), big(3), big(1)],
        compiler_params=grant(30),
        cost_estimate=pl.CostEstimate(flops=25000000, bytes_accessed=10000000, transcendentals=0),
        name="near",
    )(potential, *operator, u, late_a, y_late, corner_a)

    potential_next = pl.pallas_call(
        far_kernel,
        out_shape=shape(4, 64, 1024),
        in_specs=[VM] * 15,
        out_specs=ANY,
        scratch_shapes=[big(3), big(4), big(3), pltpu.VMEM((3, 64, 1024), F32), pltpu.SemaphoreType.DMA((4,))],
        compiler_params=grant(30),
        cost_estimate=pl.CostEstimate(flops=25000000, bytes_accessed=10000000, transcendentals=0),
        name="far",
    )(potential, *operator, u, late_b, y_late, corner_b, u1, r, u2, done)
    return potential_next, states_next, membrane.reshape(16384)


def solution(mesh):
    in_specs = (
        P("vol", "mem", None), P("vol", "mem", None), P(None, ("vol", "mem")),
        P(), P(), P(), P(),
        P(("vol", "mem")), P(("vol", "mem")), P(("vol", "mem")), P(("vol", "mem")),
        P(("vol", "mem"), None), P(("vol", "mem"), None),
    )
    out_specs = (P("vol", "mem", None), P(None, ("vol", "mem")), P(("vol", "mem")))
    return jax.shard_map(per_device, mesh=mesh, in_specs=in_specs, out_specs=out_specs, check_vma=False)
```

```python
import functools

import jax
import jax.numpy as jnp
from jax import lax
from jax.experimental import pallas as pl
from jax.experimental.pallas import tpu as pltpu
from jax.sharding import PartitionSpec as P

SWEEPS = 4
F32 = jnp.float32
BF16 = jnp.bfloat16
ANY = pl.BlockSpec(memory_space=pl.ANY)
HBM = pl.BlockSpec(memory_space=pltpu.HBM)
VM = pl.BlockSpec(memory_space=pltpu.VMEM)
SM = pl.BlockSpec(memory_space=pltpu.SMEM)


def grant(mib):
    return pltpu.CompilerParams(vmem_limit_bytes=mib * 1024 * 1024)


def sweep_factors():
    theta, delta = 1.0, 0.8
    sigma = theta / delta
    rho = 1.0 / sigma
    factors = []
    for _ in range(SWEEPS - 1):
        rho_next = 1.0 / (2.0 * sigma - rho)
        factors.append((rho_next * rho, 2.0 * rho_next / delta))
        rho = rho_next
    return factors


def iota(shape, dim):
    return lax.broadcasted_iota(jnp.int32, shape, dim)


def place():
    v, mine = lax.axis_index("vol"), lax.axis_index("mem")
    return v & 1, (v != 0) & (v != lax.axis_size("vol") - 1), mine, v


def plane_of(parity, j):
    return j + parity * (3 - 2 * j)


def pair_sum(row):
    even = (iota((1, 128), 1) & 1) == 0
    return row + jnp.where(even, pltpu.roll(row, 127, 1), pltpu.roll(row, 1, 1))


def gather_kernel(cnt, p_hbm, c_hbm, in_hbm, ex_hbm, part_hbm, cond_hbm, st_hbm,
                  st_near, volt_hbm, cell_hbm, act_hbm, part_out, cond_out, a_hbm, b_hbm, up_hbm, down_hbm,
                  p_ref, c_ref, in_ref, ex_ref, part_ref, cond_ref, volt_ref, cell_ref, act_ref, part_two, cond_two,
                  note, sem):
    par, has_b, mine, v = place()
    loads = begin(
        [(in_hbm, in_ref), (ex_hbm, ex_ref)] + [(p_hbm.at[x], p_ref.at[x]) for x in range(4)]
        + [(c_hbm.at[x], c_ref.at[x]) for x in range(4)] + [(part_hbm, part_ref), (cond_hbm, cond_ref)], sem, 0)
    states = begin([(st_hbm.at[:, 4096 * i : 4096 * i + 4096], st_near.at[:, 4096 * i : 4096 * i + 4096]) for i in range(4)], sem, 31)
    twice = iota((8, 128), 1) // 2
    sub = iota((8, 128), 0)
    low = sub < 4
    lane_row = iota((1, 128), 1)

    def body(kk, carry):
        x = kk // 4
        blocks = [r[pl.ds(pl.multiple_of(8 * kk, 8), 8), :] & 4095 for r in (in_ref, ex_ref)]
        for q in range(2):
            row = pl.multiple_of((2 * (kk % 4) + q) * 8, 8)
            tiles = [p_ref[x, pl.ds(row, 8), 128 * z : 128 * z + 128] for z in range(8)]
            for h in range(2):
                picked = []
                for block in blocks:
                    a = jnp.broadcast_to(block[4 * q + h : 4 * q + h + 1], (8, 128))
                    b = jnp.broadcast_to(block[4 * q + 2 + h : 4 * q + 3 + h], (8, 128))
                    o = jnp.where(low, a, b)
                    lane = o & 127
                    z_of = (o >> 7) & 7
                    got = jnp.take_along_axis(tiles[0], lane, axis=1, mode="promise_in_bounds")
                    for z in range(1, 8):
                        new = jnp.take_along_axis(tiles[z], lane, axis=1, mode="promise_in_bounds")
                        got = jnp.where(z_of == z, new, got)
                    picked.append(jnp.where((o >> 10) == (sub & 3), got, 0.0))
                d = picked[0] - picked[1]
                d = d + pltpu.roll(d, 7, 0)
                d = d + pltpu.roll(d, 6, 0)
                for i in range(2):
                    at = pl.ds(8 * kk + 4 * q + 2 * i + h, 1)
                    volt_ref[at, :] = d[4 * i : 4 * i + 1]
                    used = lane_row + 128 * h < cnt[4 * kk + 2 * q + i]
                    act_ref[at, :] = jnp.where(used, 1.0, 0.0)
        return carry

    loads[0].wait()
    loads[1].wait()
    for x in range(4):
        if x < 2:
            loads[2 + x].wait()
        lax.fori_loop(4 * x, 4 * x + 4, body, 0, unroll=4)
        if x == 1:
            for load in loads[4:]:
                load.wait()
            copies = []
            for i in range(3):
                copies.append((c_ref.at[plane_of(par, i)], b_hbm.at[i]))
                copies.append((c_ref.at[plane_of(par, 3 - i)], a_hbm.at[i]))
            copies.append((p_ref.at[plane_of(par, 0)], b_hbm.at[3]))
            copies.append((p_ref.at[plane_of(par, 3)], a_hbm.at[3]))
            for k, src in enumerate((c_ref, p_ref)):
                copies.append((src.at[:, 56:64], up_hbm.at[4 * k : 4 * k + 4]))
                copies.append((src.at[:, 0:8], down_hbm.at[4 * k : 4 * k + 4]))
            for src, dst in ((part_ref, part_two), (cond_ref, cond_two)):
                wide = jnp.concatenate([src[...], src[...]], axis=1)
                dst[...] = jnp.take_along_axis(wide, twice, axis=1, mode="promise_in_bounds")
            copies += [(part_two, part_out), (cond_two, cond_out)]
            sends = begin(copies, sem, 12)
    sends += begin([(volt_ref, volt_hbm), (act_ref, act_hbm)], sem, 26)
    act = act_ref[...]
    total = jnp.sum(jnp.transpose(volt_ref[...] * act), axis=0, keepdims=True)
    count = jnp.sum(jnp.transpose(act), axis=0, keepdims=True)
    cells = pair_sum(total) / jnp.maximum(pair_sum(count), 1.0)
    cell_ref[...] = cells
    note[...] = jnp.zeros((8, 1024), F32)
    note[0:1, 0:128] = cells
    sends += begin([(note, up_hbm.at[8]), (note, down_hbm.at[8]), (cell_ref, cell_hbm)], sem, 28)
    for send in sends + states:
        send.wait()


def begin(copies, sem, start):
    made = [pltpu.make_async_copy(s, d, sem.at[start + n]) for n, (s, d) in enumerate(copies)]
    for m in made:
        m.start()
    return made


CHUNKS = 16
ROOM = 24000000


def ionic_kernel(cnt, typ, volt_ref, act_ref, scale_ref, slope_ref, cond_ref, rev_ref, st_ref,
                 out_hbm, ion_ref, out_ref, flat, rate_ref, sem):
    width = 16384 // CHUNKS
    at = lambda i: pl.ds(pl.multiple_of(i * width, width), width)
    store = lambda i: pltpu.make_async_copy(out_ref.at[:, at(i)], out_hbm.at[:, at(i)], sem.at[i])
    flat[...] = jnp.zeros((128, 128), F32)
    logs = jnp.log(scale_ref[...])
    flat[0:1, 0:40] = slope_ref[0:1]
    flat[1:2, 0:40] = logs[0:1]
    flat[2:3, 0:40] = -slope_ref[1:2]
    flat[3:4, 0:40] = logs[1:2]
    flat[4:7, 0:40] = cond_ref[...]
    flat[7:10, 0:40] = cond_ref[...] * rev_ref[...]
    turned = jnp.transpose(flat[...])
    for i in range(10):
        rate_ref[i] = jnp.broadcast_to(turned[0:40, i : i + 1], (40, 128))
    lane = iota((8, 128), 1)

    def body(group, carry):
        rows8 = pl.ds(pl.multiple_of(8 * group, 8), 8)
        volts = volt_ref[rows8, :]
        counts, types, v, active, cols = [], [], [], [], []
        for q in range(4):
            counts.append(cnt[4 * group + q])
            types.append(typ[4 * group + q])
        for r in range(8):
            v.append(jnp.broadcast_to(volts[r : r + 1], (8, 128)))
            active.append(lane + (r % 2) * 128 < counts[r // 2])
            cols.append(pl.ds(pl.multiple_of(1024 * group + 128 * r, 128), 128))
        w1, w2 = [None] * 8, [None] * 8
        for k in range(5):
            rows = slice(8 * k, 8 * k + 8)
            rate = [rate_ref[i, rows] for i in range(4)]
            for q in range(4):
                g, gr = rate_ref[4 + types[q], rows], rate_ref[7 + types[q], rows]
                for r in (2 * q, 2 * q + 1):
                    st = st_ref[rows, cols[r]]
                    opening = jnp.exp(rate[0] * v[r] + rate[1])
                    closing = jnp.exp(rate[2] * v[r] + rate[3])
                    total = opening + closing
                    steady = opening * inverse(total)
                    fresh = steady + (st - steady) * jnp.exp(total * -0.5)
                    out_ref[rows, cols[r]] = jnp.where(active[r], fresh, st)
                    w1[r] = g * fresh if k == 0 else w1[r] + g * fresh
                    w2[r] = gr * fresh if k == 0 else w2[r] + gr * fresh
        store(group).start()
        act = act_ref[rows8, :]
        ion = [jnp.sum(w1[r] * v[r] - w2[r], axis=0, keepdims=True) for r in range(8)]
        val = jnp.concatenate(ion, axis=0) * act
        ion_ref[rows8, :] = val
        return carry

    lax.fori_loop(0, CHUNKS, body, 0, unroll=2)
    for i in range(CHUNKS):
        store(i).wait()


def scatter_kernel(first, ion_ref, act_ref, in_ref, ex_ref, after, s_ref, n_ref):
    par, has_b, mine, v = place()
    numbers = [(iota((16, 512), 0) + 16 * k).astype(F32).astype(BF16) for k in range(8)]
    low = iota((8, 128), 0) < 4
    odd_row = (iota((8, 128), 0) & 2) // 2

    def body(turn, carry):
        group = 4 * plane_of(par, first + turn // 4) + turn % 4
        rows8 = pl.ds(pl.multiple_of(8 * group, 8), 8)
        val, act = ion_ref[rows8, :], act_ref[rows8, :]
        x = turn // 4
        hi = val.astype(BF16).astype(F32)
        lo = val - hi
        mids, lanes = [], []
        for ref in (in_ref, ex_ref):
            o = ref[rows8, :] & 4095
            mids.append(((((o >> 7) & 7) ^ odd_row) * 4 + (o >> 10)).astype(F32))
            lanes.append((o & 127).astype(F32))

        def line(a, b, s):
            r = 2 * s
            return jnp.concatenate([a[r : r + 1], a[r + 1 : r + 2], b[r : r + 1], b[r + 1 : r + 2]], axis=1)

        for q in range(2):
            results = []
            for s in (2 * q, 2 * q + 1):
                packed = lambda row: jnp.broadcast_to(row, (16, 512)).astype(BF16)
                mid, at = packed(line(mids[0], mids[1], s)), packed(line(lanes[0], lanes[1], s))
                pieces = [packed(line(piece, -piece, s)) for piece in (hi, lo, act)]
                hits = [mid == numbers[0], mid == numbers[1]]
                none, one = jnp.zeros((16, 512), BF16), jnp.ones((16, 512), BF16)
                left = jnp.concatenate([jnp.where(hit, piece, none) for piece in pieces for hit in hits], axis=0)
                right = jnp.concatenate([jnp.where(at == number, one, none) for number in numbers], axis=0)
                out = lax.dot_general(left, right, (((1,), (1,)), ((), ())), preferred_element_type=F32)
                results.append((out[0:32] + out[32:64], out[64:96]))
            row = pl.ds(pl.multiple_of((2 * (turn % 4) + q) * 8, 8), 8)
            for dst, e, o in ((s_ref, results[0][0], results[1][0]), (n_ref, results[0][1], results[1][1])):
                for j in range(4):
                    ej, oj = e[8 * j : 8 * j + 8], o[8 * j : 8 * j + 8]
                    dst[x, row, 256 * j : 256 * j + 128] = jnp.where(low, ej, oj)
                    dst[x, row, 256 * j + 128 : 256 * j + 256] = pltpu.roll(jnp.where(low, oj, ej), 4, 0)
        return carry

    lax.fori_loop(0, 8, body, 0, unroll=8)


def edge_rows(mine, below, above):
    sub = iota((8, 1024), 0)
    bottom = (sub < 3) & (mine != 3)
    top = (sub >= 5) & (mine != 0)
    return jnp.where(bottom, above, jnp.where(top, below, 0.0))


def early_edge_kernel(below_ref, above_ref, far_ref, cell_ref, after, y_ref, table_ref, a_ref, b_ref):
    par, has_b, mine, v = place()
    for x in range(8):
        y_ref[x] = edge_rows(mine, below_ref[x], above_ref[x])
    table = jnp.concatenate(
        [cell_ref[...], below_ref[8, 0:1, 0:128], far_ref[...], above_ref[8, 0:1, 0:128],
         jnp.zeros((4, 128), F32)], axis=0)
    table_ref[...] = table
    for i in range(2):
        a_ref[i] = y_ref[plane_of(par, 3 - i)]
        b_ref[i] = y_ref[plane_of(par, i)]
    for ref in (a_ref, b_ref):
        ref[2] = jnp.zeros((8, 1024), F32)
        ref[2, :, 0:128] = table


def late_edge_kernel(below_ref, above_ref, after, y_ref, a_ref, b_ref):
    par, has_b, mine, v = place()
    for x in range(4):
        y_ref[x] = edge_rows(mine, below_ref[x], above_ref[x])
    for i in range(2):
        a_ref[i] = y_ref[plane_of(par, 3 - i)]
        b_ref[i] = y_ref[plane_of(par, i)]


def reader(par, inside, own, a, b, y, ca=None, cb=None, own_y=0):
    def get(e, t):
        rows = slice(8 * t, 8 * t + 8)
        if 3 <= e <= 6:
            x = plane_of(par, e - 3)
            return own[x, rows, :] if t < 8 else y[own_y + x]
        halo, corner, i = (a, ca, e - 7) if e > 6 else (b, cb, 2 - e)
        value = halo[i, rows, :] if t < 8 else corner[i]
        return value if e > 6 else value * inside

    return get


def stored(*held):
    def get(e, t):
        for ref, start, stop in held:
            if start <= e < stop:
                return ref[e - start, 8 * t : 8 * t + 8, :]

    return get


class Plane:
    def __init__(self, get, e):
        self.get, self.e = get, e
        self.sub = iota((8, 1024), 0)
        self.kept = {}

    def turned(self, t, by, keep):
        found = self.kept.pop((t, by), None)
        if found is None:
            found = pltpu.roll(self.get(self.e, t), by, 0)
            if keep:
                self.kept[t, by] = found
        return found

    def views(self, t):
        get, e = self.get, self.e
        c = get(e, t)
        ym = jnp.where(self.sub == 0, self.turned((t + 8) % 9, 1, False), self.turned(t, 1, True))
        yp = jnp.where(self.sub == 7, self.turned((t + 1) % 9, 7, t < 8), self.turned(t, 7, False))
        return c, get(e - 1, t), get(e + 1, t), ym, yp, pltpu.roll(c, 1, 1), pltpu.roll(c, 1023, 1)


def inverse(x):
    rec = pl.reciprocal(x, approx=True)
    return rec * (2.0 - x * rec)


def couplings(plane, t):
    lane = iota((8, 1024), 1)
    c, xm, xp, ym, yp, zm, zp = plane.views(t)
    first, last = lane == 0, lane == 1023
    c = 0.25 * c
    xm, xp, ym, yp = (c + 0.25 * other for other in (xm, xp, ym, yp))
    zm = c + 0.25 * jnp.where(first, 0.0, zm)
    zp = c + 0.25 * jnp.where(last, 0.0, zp)
    inv = inverse(1.0 + (((xm + xp) + (ym + yp)) + (zm + zp)))
    return (xm, xp, ym, yp, jnp.where(first, 0.0, zm), jnp.where(last, 0.0, zp)), inv


def weighted(fs, views):
    t = [f * v for f, v in zip(fs, views)]
    return ((t[0] + t[1]) + (t[2] + t[3])) + (t[4] + t[5])


def prepare_kernel(p_ref, c_ref, a_ref, b_ref, y_ref, s_one, n_one, s_two, n_two, w_ref, k_ref):
    par, has_b, mine, v = place()
    inside = jnp.where(has_b, 1.0, 0.0)
    conduct = reader(par, inside, c_ref, a_ref, b_ref, y_ref)
    own = reader(par, inside, p_ref, a_ref.at[3:4], b_ref.at[3:4], y_ref, own_y=4)
    for e in range(3, 7):
        x = plane_of(par, e - 3)
        s_ref, n_ref = (s_one, n_one) if e < 5 else (s_two, n_two)
        at = (e - 3) % 2
        pc, pp = Plane(conduct, e), Plane(own, e)
        for t in range(8):
            rows = slice(8 * t, 8 * t + 8)
            fs, inv = couplings(pc, t)
            p, *views = pp.views(t)
            w_ref[x, rows, :] = (p + weighted(fs, views) - 0.5 * s_ref[at, rows, :]) * inv - p
            k_ref[x, rows, :] = (-0.5 * inv) * n_ref[at, rows, :]


def gap_kernel(table_ref, ta_ref, tb_ref, part_ref, cond_ref, ion_ref, act_ref, w_ref, k_ref,
               u_ref, a_ref, b_ref, up_ref, down_ref, mem_ref, spread):
    par, has_b, mine, v = place()
    part = part_ref[...]
    brick = part >> 6
    bx, by = brick >> 2, brick & 3
    side = jnp.where(bx == v, 0, jnp.where(bx == (v ^ 1), 1, 2))
    row = side * 4 + ((mine - by) & 3)
    lane = (part & 63) * 2
    tables = (table_ref[...], ta_ref[2, :, 0:128], tb_ref[2, :, 0:128])
    other = jnp.zeros((8, 128), F32)
    for r in range(12):
        line = jnp.broadcast_to(tables[r // 4][r % 4 : r % 4 + 1], (8, 128))
        other = jnp.where(row == r, jnp.take_along_axis(line, lane, axis=1, mode="promise_in_bounds"), other)
    own = tables[0][0:1]
    current = jnp.sum(cond_ref[...] * (own - other), axis=0, keepdims=True)
    act = act_ref[...]
    count = pair_sum(jnp.sum(jnp.transpose(act), axis=0, keepdims=True))
    g = current / jnp.maximum(count, 1.0)
    g8 = jnp.broadcast_to(g, (8, 128))
    mem_ref[...] = ion_ref[...] + act * jnp.transpose(jnp.broadcast_to(g, (128, 128)))
    for half in range(2):
        at = 64 * half + 2 * (iota((8, 128), 1) // 4)
        wide = jnp.take_along_axis(g8, at, axis=1, mode="promise_in_bounds")[0:1]
        spread[128 * half : 128 * half + 128, :] = jnp.transpose(jnp.broadcast_to(wide, (128, 128)))
    for j in range(4):
        x = plane_of(par, j)
        for t in range(8):
            rows = slice(8 * t, 8 * t + 8)
            gt = jnp.tile(spread[pl.ds(pl.multiple_of(x * 64 + 8 * t, 8), 8), :], (1, 8))
            u = w_ref[x, rows, :] + k_ref[x, rows, :] * gt
            u_ref[x, rows, :] = u
            if t == 0:
                down_ref[x] = u
            if t == 7:
                up_ref[x] = u
            if j < 3:
                b_ref[j, rows, :] = u
            if j > 0:
                a_ref[3 - j, rows, :] = u


def operator_kernel(c_ref, a_ref, b_ref, y_ref, ca_ref, cb_ref, after, fx, fym, fyp, fzm, fzp, inv_ref):
    par, has_b, mine, v = place()
    inside = jnp.where(has_b, 1.0, 0.0)
    conduct = reader(par, inside, c_ref, a_ref, b_ref, y_ref, ca_ref, cb_ref)
    sub = iota((8, 1024), 0)
    bottom = (sub < 3) & (mine != 3)
    top = (sub >= 5) & (mine != 0)
    keep = jnp.where(bottom | top, 1.0, 0.0)
    for e in range(1, 9):
        plane = Plane(conduct, e)
        for t in range(8 if e in (1, 8) else 9):
            rows = slice(8 * t, 8 * t + 8)
            fs, inv = couplings(plane, t)
            if e < 3:
                inv = inv * inside
            inv_ref[e - 1, rows, :] = inv * keep if t == 8 else inv
            if e == 1 or (e == 2 and t == 8):
                fx[e - 1, rows, :] = fs[0]
            fx[e, rows, :] = fs[1]
            for ref, f in zip((fym, fyp, fzm, fzp), fs[2:]):
                ref[e - 1, rows, :] = f


def coupled(coef, get, plane, t):
    fx, fym, fyp, fzm, fzp, inv = coef
    e = plane.e
    rows = slice(8 * t, 8 * t + 8)
    fs = [fx[e - 1, rows, :], fx[e, rows, :]] + [f[e - 1, rows, :] for f in (fym, fyp, fzm, fzp)]
    u, *views = plane.views(t)
    return u, inv[e - 1, rows, :] * weighted(fs, views)


def put(held, e, t, value):
    for ref, start, stop in held:
        if start <= e < stop:
            ref[e - start, 8 * t : 8 * t + 8, :] = value


def step_one(coef, u0, e, r_held, u1_held, tiles=None):
    a, b = sweep_factors()[0]
    plane = Plane(u0, e)
    for t in tiles or range(8 if e in (1, 8) else 9):
        u, res = coupled(coef, u0, plane, t)
        put(r_held, e, t, res)
        put(u1_held, e, t, a * u + b * res)


def step_two(coef, u1, r, e, r_held, u2_held):
    a, b = sweep_factors()[1]
    plane = Plane(u1, e)
    for t in range(8 if e in (2, 7) else 9):
        u, more = coupled(coef, u1, plane, t)
        res = (r(e, t) - u) + more
        put(r_held, e, t, res)
        put(u2_held, e, t, a * u + b * res)


def step_three(coef, p_ref, u0, u1, u2, r, e, x, out_ref, at):
    a, b = sweep_factors()[2]
    plane = Plane(u2, e)
    for t in range(8):
        rows = slice(8 * t, 8 * t + 8)
        u, more = coupled(coef, u2, plane, t)
        res = (r(e, t) - u) + more
        before = (p_ref[x, rows, :] + u0(e, t)) + (u1(e, t) + u)
        out_ref[at, rows, :] = before + (a * u + b * res)


def near_kernel(p_ref, fx, fym, fyp, fzm, fzp, inv, u_ref, a_ref, y_ref, ca_ref,
                u1_out, r_out, u2_out, done_ref, u1_far, r_far, u2_far):
    par, has_b, mine, v = place()
    inside = jnp.where(has_b, 1.0, 0.0)
    coef = (fx, fym, fyp, fzm, fzp, inv)
    u0 = reader(par, inside, u_ref, a_ref, None, y_ref, ca_ref)
    u1_held = ((u1_out, 4, 6), (u1_far, 6, 9))
    r1_held = ((r_out, 4, 5), (r_far, 5, 8))
    r2_held = ((r_out.at[1:2], 5, 6), (r_far.at[1:2], 6, 7))
    u2_held = ((u2_out, 5, 7), (u2_far, 7, 8))
    for e in (8, 7, 6, 5, 4):
        step_one(coef, u0, e, r1_held, u1_held)
    for e in (7, 6, 5):
        step_two(coef, stored(*u1_held), stored(*r1_held), e, r2_held, u2_held)
    step_three(coef, p_ref, u0, stored(*u1_held), stored(*u2_held), stored(*r2_held), 6, plane_of(par, 3), done_ref, 0)


def either(early, late):
    return lambda e, t: early(e, t) if e < 4 and t in ahead(e) else late(e, t)


def ahead(e):
    return range(8) if e == 3 else range(1, 7)


def middle_kernel(fx, fym, fyp, fzm, fzp, inv, u_ref, b_ref, y_ref, after, u1_out, r_out):
    par, has_b, mine, v = place()
    inside = jnp.where(has_b, 1.0, 0.0)
    u0 = reader(par, inside, u_ref, None, b_ref, y_ref)
    for e in (1, 2, 3):
        step_one((fx, fym, fyp, fzm, fzp, inv), u0, e, ((r_out, 2, 4),), ((u1_out, 1, 4),), ahead(e))


def far_kernel(p_ref, fx, fym, fyp, fzm, fzp, inv, u_ref, b_ref, y_ref, cb_ref, u1_in, r_in, u2_in, done_ref,
               u1_mid, r_mid, out_hbm, u1_far, r_far, u2_far, out_ref, sem):
    par, has_b, mine, v = place()
    inside = jnp.where(has_b, 1.0, 0.0)
    coef = (fx, fym, fyp, fzm, fzp, inv)
    u0 = reader(par, inside, u_ref, None, b_ref, y_ref, None, cb_ref)
    u1_new = ((u1_far, 1, 4),)
    u1 = either(stored((u1_mid, 1, 4)), stored(*u1_new, (u1_in, 4, 6)))
    r1_new = ((r_far, 2, 4),)
    r1 = either(stored((r_mid, 2, 4)), stored(*r1_new, (r_in, 4, 5)))
    r2_new = ((r_far.at[2:4], 3, 5),)
    r2 = stored(*r2_new, (r_in.at[1:2], 5, 6))
    u2_new = ((u2_far, 2, 5),)
    u2 = stored(*u2_new, (u2_in, 5, 7))
    sends = begin([(done_ref.at[0], out_hbm.at[plane_of(par, 3)])], sem, 3)
    for e in (1, 2, 3):
        step_one(coef, u0, e, r1_new, u1_new, [t for t in range(8 if e == 1 else 9) if t not in ahead(e)])
    for e in (2, 3, 4):
        step_two(coef, u1, r1, e, r2_new, u2_new)
    for e in (3, 4, 5):
        x = plane_of(par, e - 3)
        step_three(coef, p_ref, u0, u1, u2, r2, e, x, out_ref, e - 3)
        sends += begin([(out_ref.at[e - 3], out_hbm.at[x])], sem, e - 3)
    for send in sends:
        send.wait()


def near(*dims, kind=F32):
    return pltpu.VMEM(dims, kind)


def shape(*dims, kind=F32):
    return jax.ShapeDtypeStruct(dims, kind)


def per_device(potential, conductivity, ion_states, rate_scale, rate_slope, type_cond, reversal,
               facet_counts, intra_voxel, extra_voxel, cell_type, gap_partner, gap_cond):
    nv = lax.axis_size("vol")
    swap_a = [pair for i in range(0, nv, 2) for pair in ((i, i + 1), (i + 1, i))]
    swap_b = [pair for i in range(1, nv - 1, 2) for pair in ((i, i + 1), (i + 1, i))] + [(0, 0), (nv - 1, nv - 1)]
    on_mem = lambda x, pairs: lax.ppermute(x, "mem", pairs)
    ring = lambda d: [(i, (i + d) % 4) for i in range(4)]
    to_a = functools.partial(lax.ppermute, axis_name="vol", perm=swap_a)
    to_b = functools.partial(lax.ppermute, axis_name="vol", perm=swap_b)

    intra = intra_voxel.reshape(128, 128)
    extra = extra_voxel.reshape(128, 128)

    states_near, volt, cells, act, part_lane, cond_lane, send_a, send_b, send_up, send_down = pl.pallas_call(
        gather_kernel,
        out_shape=(near(40, 16384), near(128, 128), near(1, 128), near(128, 128),
                   near(8, 128, kind=jnp.int32), near(8, 128),
                   near(4, 64, 1024), near(4, 64, 1024), near(9, 8, 1024), near(9, 8, 1024)),
        in_specs=[SM] + [ANY] * 7,
        out_specs=(ANY,) * 10,
        scratch_shapes=[pltpu.VMEM((4, 64, 1024), F32), pltpu.VMEM((4, 64, 1024), F32),
                        pltpu.VMEM((128, 128), jnp.int32), pltpu.VMEM((128, 128), jnp.int32),
                        pltpu.VMEM((8, 64), jnp.int32), pltpu.VMEM((8, 64), F32), pltpu.VMEM((128, 128), F32),
                        pltpu.VMEM((1, 128), F32), pltpu.VMEM((128, 128), F32), pltpu.VMEM((8, 128), jnp.int32),
                        pltpu.VMEM((8, 128), F32), pltpu.VMEM((8, 1024), F32), pltpu.SemaphoreType.DMA((35,))],
        compiler_params=grant(54),
        cost_estimate=pl.CostEstimate(flops=4000000, bytes_accessed=5000000, transcendentals=0),
        name="voltages",
    )(facet_counts, potential, conductivity, intra, extra, gap_partner.T, gap_cond.T, ion_states)

    below, above, far = on_mem(send_up, ring(1)), on_mem(send_down, ring(3)), on_mem(cells, ring(2))
    early_b, early_a = to_b(send_b), to_a(send_a)

    states_next, ion = pl.pallas_call(
        ionic_kernel,
        out_shape=(shape(40, 16384), near(128, 128)),
        in_specs=[SM, SM] + [VM] * 7,
        out_specs=(ANY, VM),
        scratch_shapes=[pltpu.VMEM((40, 16384), F32), pltpu.VMEM((128, 128), F32),
                        pltpu.VMEM((10, 40, 128), F32), pltpu.SemaphoreType.DMA((CHUNKS,))],
        compiler_params=pltpu.CompilerParams(vmem_limit_bytes=ROOM),
        cost_estimate=pl.CostEstimate(flops=16000000, bytes_accessed=5300000, transcendentals=2600000),
        name="ionic",
    )(facet_counts, cell_type, volt, act, rate_scale, rate_slope, type_cond, reversal.reshape(1, 40), states_near)

    def scatter(first, after):
        return pl.pallas_call(
            functools.partial(scatter_kernel, first),
            out_shape=(near(2, 64, 1024), near(2, 64, 1024)),
            in_specs=[VM] * 4 + [ANY],
            out_specs=(VM, VM),
            compiler_params=grant(12),
            cost_estimate=pl.CostEstimate(flops=400000000, bytes_accessed=1200000, transcendentals=0),
            name="scatter",
        )(ion, act, intra, extra, after)

    half_one = scatter(0, volt)

    y_early, table, more_a, more_b = pl.pallas_call(
        early_edge_kernel,
        out_shape=(shape(8, 8, 1024), shape(8, 128), shape(3, 8, 1024), shape(3, 8, 1024)),
        in_specs=[VM] * 4 + [ANY],
        out_specs=(VM,) * 4,
        compiler_params=grant(6),
        cost_estimate=pl.CostEstimate(flops=300000, bytes_accessed=1000000, transcendentals=0),
        name="early_edges",
    )(below, above, far, cells, half_one[0])
    more_b, more_a = to_b(more_b), to_a(more_a)

    half_two = scatter(2, table)

    w, k = pl.pallas_call(
        prepare_kernel,
        out_shape=(shape(4, 64, 1024), shape(4, 64, 1024)),
        in_specs=[VM] * 9,
        out_specs=(VM, VM),
        compiler_params=grant(20),
        cost_estimate=pl.CostEstimate(flops=16000000, bytes_accessed=8000000, transcendentals=0),
        name="prepare",
    )(potential, conductivity, early_a, early_b, y_early, *half_one, *half_two)

    u, u_a, u_b, u_up, u_down, membrane = pl.pallas_call(
        gap_kernel,
        out_shape=(shape(4, 64, 1024), shape(3, 64, 1024), shape(3, 64, 1024), shape(4, 8, 1024),
                   shape(4, 8, 1024), shape(128, 128)),
        in_specs=[VM] * 9,
        out_specs=(VM,) * 6,
        scratch_shapes=[pltpu.VMEM((256, 128), F32)],
        compiler_params=grant(12),
        cost_estimate=pl.CostEstimate(flops=1000000, bytes_accessed=5000000, transcendentals=0),
        name="gap",
    )(table, more_a, more_b, part_lane, cond_lane, ion, act, w, k)

    late_b = to_b(u_b)
    low_rows, high_rows = on_mem(u_up, ring(1)), on_mem(u_down, ring(3))
    late_a = to_a(u_a)

    big = lambda n: pltpu.VMEM((n, 72, 1024), F32)
    operator = pl.pallas_call(
        operator_kernel,
        out_shape=(shape(9, 72, 1024),) + (shape(8, 72, 1024),) * 5,
        in_specs=[VM] * 6 + [ANY],
        out_specs=(VM,) * 6,
        compiler_params=grant(22),
        cost_estimate=pl.CostEstimate(flops=16000000, bytes_accessed=17000000, transcendentals=0),
        name="operator",
    )(conductivity, early_a, early_b, y_early, more_a, more_b, u_up)

    y_late, corner_a, corner_b = pl.pallas_call(
        late_edge_kernel,
        out_shape=(shape(4, 8, 1024), shape(2, 8, 1024), shape(2, 8, 1024)),
        in_specs=[VM, VM, ANY],
        out_specs=(VM,) * 3,
        compiler_params=grant(4),
        cost_estimate=pl.CostEstimate(flops=100000, bytes_accessed=500000, transcendentals=0),
        name="late_edges",
    )(low_rows, high_rows, operator[-1])
    corner_b, corner_a = to_b(corner_b), to_a(corner_a)

    u1, r, u2, done = pl.pallas_call(
        near_kernel,
        out_shape=(shape(2, 72, 1024), shape(2, 72, 1024), shape(2, 72, 1024), shape(1, 64, 1024)),
        in_specs=[VM] * 11,
        out_specs=(VM,) * 4,
        scratch_shapes=[big(3), big(3), big(1)],
        compiler_params=grant(30),
        cost_estimate=pl.CostEstimate(flops=25000000, bytes_accessed=10000000, transcendentals=0),
        name="near",
    )(potential, *operator, u, late_a, y_late, corner_a)

    u1_mid, r_mid = pl.pallas_call(
        middle_kernel,
        out_shape=(shape(3, 72, 1024), shape(2, 72, 1024)),
        in_specs=[VM] * 9 + [ANY],
        out_specs=(VM,) * 2,
        compiler_params=grant(30),
        cost_estimate=pl.CostEstimate(flops=8000000, bytes_accessed=4000000, transcendentals=0),
        name="middle",
    )(*operator, u, late_b, y_late, done)

    potential_next = pl.pallas_call(
        far_kernel,
        out_shape=shape(4, 64, 1024),
        in_specs=[VM] * 17,
        out_specs=ANY,
        scratch_shapes=[big(3), big(4), big(3), pltpu.VMEM((3, 64, 1024), F32), pltpu.SemaphoreType.DMA((4,))],
        compiler_params=grant(30),
        cost_estimate=pl.CostEstimate(flops=25000000, bytes_accessed=10000000, transcendentals=0),
        name="far",
    )(potential, *operator, u, late_b, y_late, corner_b, u1, r, u2, done, u1_mid, r_mid)
    return potential_next, states_next, membrane.reshape(16384)


def solution(mesh):
    in_specs = (
        P("vol", "mem", None), P("vol", "mem", None), P(None, ("vol", "mem")),
        P(), P(), P(), P(),
        P(("vol", "mem")), P(("vol", "mem")), P(("vol", "mem")), P(("vol", "mem")),
        P(("vol", "mem"), None), P(("vol", "mem"), None),
    )
    out_specs = (P("vol", "mem", None), P(None, ("vol", "mem")), P(("vol", "mem")))
    return jax.shard_map(per_device, mesh=mesh, in_specs=in_specs, out_specs=out_specs, check_vma=False)
```

```python
import functools

import jax
import jax.numpy as jnp
from jax import lax
from jax.experimental import pallas as pl
from jax.experimental.pallas import tpu as pltpu
from jax.sharding import PartitionSpec as P

SWEEPS = 4
F32 = jnp.float32
BF16 = jnp.bfloat16
ANY = pl.BlockSpec(memory_space=pl.ANY)
HBM = pl.BlockSpec(memory_space=pltpu.HBM)
VM = pl.BlockSpec(memory_space=pltpu.VMEM)
SM = pl.BlockSpec(memory_space=pltpu.SMEM)


def grant(mib):
    return pltpu.CompilerParams(vmem_limit_bytes=mib * 1024 * 1024)


def sweep_factors():
    theta, delta = 1.0, 0.8
    sigma = theta / delta
    rho = 1.0 / sigma
    factors = []
    for _ in range(SWEEPS - 1):
        rho_next = 1.0 / (2.0 * sigma - rho)
        factors.append((rho_next * rho, 2.0 * rho_next / delta))
        rho = rho_next
    return factors


def iota(shape, dim):
    return lax.broadcasted_iota(jnp.int32, shape, dim)


def place():
    v, mine = lax.axis_index("vol"), lax.axis_index("mem")
    return v & 1, (v != 0) & (v != lax.axis_size("vol") - 1), mine, v


def plane_of(parity, j):
    return j + parity * (3 - 2 * j)


def pair_sum(row):
    even = (iota((1, 128), 1) & 1) == 0
    return row + jnp.where(even, pltpu.roll(row, 127, 1), pltpu.roll(row, 1, 1))


def gather_kernel(cnt, p_hbm, c_hbm, in_hbm, ex_hbm, part_hbm, cond_hbm, st_hbm,
                  st_near, volt_hbm, cell_hbm, act_hbm, part_out, cond_out, a_hbm, b_hbm, up_hbm, down_hbm,
                  p_ref, c_ref, in_ref, ex_ref, part_ref, cond_ref, volt_ref, cell_ref, act_ref, part_two, cond_two,
                  note, sem):
    par, has_b, mine, v = place()
    loads = begin(
        [(in_hbm, in_ref), (ex_hbm, ex_ref)] + [(p_hbm.at[x], p_ref.at[x]) for x in range(4)]
        + [(c_hbm.at[x], c_ref.at[x]) for x in range(4)] + [(part_hbm, part_ref), (cond_hbm, cond_ref)], sem, 0)
    states = begin([(st_hbm.at[:, 4096 * i : 4096 * i + 4096], st_near.at[:, 4096 * i : 4096 * i + 4096]) for i in range(4)], sem, 31)
    twice = iota((8, 128), 1) // 2
    sub = iota((8, 128), 0)
    low = sub < 4
    lane_row = iota((1, 128), 1)

    def body(kk, carry):
        x = kk // 4
        blocks = [r[pl.ds(pl.multiple_of(8 * kk, 8), 8), :] & 4095 for r in (in_ref, ex_ref)]
        for q in range(2):
            row = pl.multiple_of((2 * (kk % 4) + q) * 8, 8)
            tiles = [p_ref[x, pl.ds(row, 8), 128 * z : 128 * z + 128] for z in range(8)]
            for h in range(2):
                picked = []
                for block in blocks:
                    a = jnp.broadcast_to(block[4 * q + h : 4 * q + h + 1], (8, 128))
                    b = jnp.broadcast_to(block[4 * q + 2 + h : 4 * q + 3 + h], (8, 128))
                    o = jnp.where(low, a, b)
                    lane = o & 127
                    z_of = (o >> 7) & 7
                    got = jnp.take_along_axis(tiles[0], lane, axis=1, mode="promise_in_bounds")
                    for z in range(1, 8):
                        new = jnp.take_along_axis(tiles[z], lane, axis=1, mode="promise_in_bounds")
                        got = jnp.where(z_of == z, new, got)
                    picked.append(jnp.where((o >> 10) == (sub & 3), got, 0.0))
                d = picked[0] - picked[1]
                d = d + pltpu.roll(d, 7, 0)
                d = d + pltpu.roll(d, 6, 0)
                for i in range(2):
                    at = pl.ds(8 * kk + 4 * q + 2 * i + h, 1)
                    volt_ref[at, :] = d[4 * i : 4 * i + 1]
                    used = lane_row + 128 * h < cnt[4 * kk + 2 * q + i]
                    act_ref[at, :] = jnp.where(used, 1.0, 0.0)
        return carry

    loads[0].wait()
    loads[1].wait()
    for x in range(4):
        if x < 2:
            loads[2 + x].wait()
        lax.fori_loop(4 * x, 4 * x + 4, body, 0, unroll=4)
        if x == 1:
            for load in loads[4:]:
                load.wait()
            copies = []
            for i in range(3):
                copies.append((c_ref.at[plane_of(par, i)], b_hbm.at[i]))
                copies.append((c_ref.at[plane_of(par, 3 - i)], a_hbm.at[i]))
            copies.append((p_ref.at[plane_of(par, 0)], b_hbm.at[3]))
            copies.append((p_ref.at[plane_of(par, 3)], a_hbm.at[3]))
            for k, src in enumerate((c_ref, p_ref)):
                copies.append((src.at[:, 56:64], up_hbm.at[4 * k : 4 * k + 4]))
                copies.append((src.at[:, 0:8], down_hbm.at[4 * k : 4 * k + 4]))
            for src, dst in ((part_ref, part_two), (cond_ref, cond_two)):
                wide = jnp.concatenate([src[...], src[...]], axis=1)
                dst[...] = jnp.take_along_axis(wide, twice, axis=1, mode="promise_in_bounds")
            copies += [(part_two, part_out), (cond_two, cond_out)]
            sends = begin(copies, sem, 12)
    sends += begin([(volt_ref, volt_hbm), (act_ref, act_hbm)], sem, 26)
    act = act_ref[...]
    total = jnp.sum(jnp.transpose(volt_ref[...] * act), axis=0, keepdims=True)
    count = jnp.sum(jnp.transpose(act), axis=0, keepdims=True)
    cells = pair_sum(total) / jnp.maximum(pair_sum(count), 1.0)
    cell_ref[...] = cells
    note[...] = jnp.zeros((8, 1024), F32)
    note[0:1, 0:128] = cells
    sends += begin([(note, up_hbm.at[8]), (note, down_hbm.at[8]), (cell_ref, cell_hbm)], sem, 28)
    for send in sends + states:
        send.wait()


def begin(copies, sem, start):
    made = [pltpu.make_async_copy(s, d, sem.at[start + n]) for n, (s, d) in enumerate(copies)]
    for m in made:
        m.start()
    return made


CHUNKS = 16
ROOM = 24000000


def ionic_kernel(cnt, typ, volt_ref, act_ref, scale_ref, slope_ref, cond_ref, rev_ref, st_ref,
                 out_hbm, ion_ref, out_ref, flat, rate_ref, sem):
    width = 16384 // CHUNKS
    at = lambda i: pl.ds(pl.multiple_of(i * width, width), width)
    store = lambda i: pltpu.make_async_copy(out_ref.at[:, at(i)], out_hbm.at[:, at(i)], sem.at[i])
    flat[...] = jnp.zeros((128, 128), F32)
    logs = jnp.log(scale_ref[...])
    flat[0:1, 0:40] = slope_ref[0:1]
    flat[1:2, 0:40] = logs[0:1]
    flat[2:3, 0:40] = -slope_ref[1:2]
    flat[3:4, 0:40] = logs[1:2]
    flat[4:7, 0:40] = cond_ref[...]
    flat[7:10, 0:40] = cond_ref[...] * rev_ref[...]
    turned = jnp.transpose(flat[...])
    for i in range(10):
        rate_ref[i] = jnp.broadcast_to(turned[0:40, i : i + 1], (40, 128))
    lane = iota((8, 128), 1)

    def body(group, carry):
        rows8 = pl.ds(pl.multiple_of(8 * group, 8), 8)
        volts = volt_ref[rows8, :]
        counts, types, v, active, cols = [], [], [], [], []
        for q in range(4):
            counts.append(cnt[4 * group + q])
            types.append(typ[4 * group + q])
        for r in range(8):
            v.append(jnp.broadcast_to(volts[r : r + 1], (8, 128)))
            active.append(lane + (r % 2) * 128 < counts[r // 2])
            cols.append(pl.ds(pl.multiple_of(1024 * group + 128 * r, 128), 128))
        w1, w2 = [None] * 8, [None] * 8
        for k in range(5):
            rows = slice(8 * k, 8 * k + 8)
            rate = [rate_ref[i, rows] for i in range(4)]
            for q in range(4):
                g, gr = rate_ref[4 + types[q], rows], rate_ref[7 + types[q], rows]
                for r in (2 * q, 2 * q + 1):
                    st = st_ref[rows, cols[r]]
                    opening = jnp.exp(rate[0] * v[r] + rate[1])
                    closing = jnp.exp(rate[2] * v[r] + rate[3])
                    total = opening + closing
                    steady = opening * inverse(total)
                    fresh = steady + (st - steady) * jnp.exp(total * -0.5)
                    out_ref[rows, cols[r]] = jnp.where(active[r], fresh, st)
                    w1[r] = g * fresh if k == 0 else w1[r] + g * fresh
                    w2[r] = gr * fresh if k == 0 else w2[r] + gr * fresh
        store(group).start()
        act = act_ref[rows8, :]
        ion = [jnp.sum(w1[r] * v[r] - w2[r], axis=0, keepdims=True) for r in range(8)]
        val = jnp.concatenate(ion, axis=0) * act
        ion_ref[rows8, :] = val
        return carry

    lax.fori_loop(0, CHUNKS, body, 0, unroll=2)
    for i in range(CHUNKS):
        store(i).wait()


def scatter_kernel(first, ion_ref, act_ref, in_ref, ex_ref, after, s_ref, n_ref):
    par, has_b, mine, v = place()
    numbers = [(iota((16, 512), 0) + 16 * k).astype(F32).astype(BF16) for k in range(8)]
    low = iota((8, 128), 0) < 4
    odd_row = (iota((8, 128), 0) & 2) // 2

    def body(turn, carry):
        group = 4 * plane_of(par, first + turn // 4) + turn % 4
        rows8 = pl.ds(pl.multiple_of(8 * group, 8), 8)
        val, act = ion_ref[rows8, :], act_ref[rows8, :]
        x = turn // 4
        hi = val.astype(BF16).astype(F32)
        lo = val - hi
        mids, lanes = [], []
        for ref in (in_ref, ex_ref):
            o = ref[rows8, :] & 4095
            mids.append(((((o >> 7) & 7) ^ odd_row) * 4 + (o >> 10)).astype(F32))
            lanes.append((o & 127).astype(F32))

        def line(a, b, s):
            r = 2 * s
            return jnp.concatenate([a[r : r + 1], a[r + 1 : r + 2], b[r : r + 1], b[r + 1 : r + 2]], axis=1)

        for q in range(2):
            results = []
            for s in (2 * q, 2 * q + 1):
                packed = lambda row: jnp.broadcast_to(row, (16, 512)).astype(BF16)
                mid, at = packed(line(mids[0], mids[1], s)), packed(line(lanes[0], lanes[1], s))
                pieces = [packed(line(piece, -piece, s)) for piece in (hi, lo, act)]
                hits = [mid == numbers[0], mid == numbers[1]]
                none, one = jnp.zeros((16, 512), BF16), jnp.ones((16, 512), BF16)
                left = jnp.concatenate([jnp.where(hit, piece, none) for piece in pieces for hit in hits], axis=0)
                right = jnp.concatenate([jnp.where(at == number, one, none) for number in numbers], axis=0)
                out = lax.dot_general(left, right, (((1,), (1,)), ((), ())), preferred_element_type=F32)
                results.append((out[0:32] + out[32:64], out[64:96]))
            row = pl.ds(pl.multiple_of((2 * (turn % 4) + q) * 8, 8), 8)
            for dst, e, o in ((s_ref, results[0][0], results[1][0]), (n_ref, results[0][1], results[1][1])):
                for j in range(4):
                    ej, oj = e[8 * j : 8 * j + 8], o[8 * j : 8 * j + 8]
                    dst[x, row, 256 * j : 256 * j + 128] = jnp.where(low, ej, oj)
                    dst[x, row, 256 * j + 128 : 256 * j + 256] = pltpu.roll(jnp.where(low, oj, ej), 4, 0)
        return carry

    lax.fori_loop(0, 8, body, 0, unroll=8)


def edge_rows(mine, below, above):
    sub = iota((8, 1024), 0)
    bottom = (sub < 3) & (mine != 3)
    top = (sub >= 5) & (mine != 0)
    return jnp.where(bottom, above, jnp.where(top, below, 0.0))


def early_edge_kernel(below_ref, above_ref, far_ref, cell_ref, after, y_ref, table_ref, a_ref, b_ref):
    par, has_b, mine, v = place()
    for x in range(8):
        y_ref[x] = edge_rows(mine, below_ref[x], above_ref[x])
    table = jnp.concatenate(
        [cell_ref[...], below_ref[8, 0:1, 0:128], far_ref[...], above_ref[8, 0:1, 0:128],
         jnp.zeros((4, 128), F32)], axis=0)
    table_ref[...] = table
    for i in range(2):
        a_ref[i] = y_ref[plane_of(par, 3 - i)]
        b_ref[i] = y_ref[plane_of(par, i)]
    for ref in (a_ref, b_ref):
        ref[2] = jnp.zeros((8, 1024), F32)
        ref[2, :, 0:128] = table


def late_edge_kernel(below_ref, above_ref, after, y_ref, a_ref, b_ref):
    par, has_b, mine, v = place()
    for x in range(4):
        y_ref[x] = edge_rows(mine, below_ref[x], above_ref[x])
    for i in range(2):
        a_ref[i] = y_ref[plane_of(par, 3 - i)]
        b_ref[i] = y_ref[plane_of(par, i)]


def reader(par, inside, own, a, b, y, ca=None, cb=None, own_y=0):
    def get(e, t):
        rows = slice(8 * t, 8 * t + 8)
        if 3 <= e <= 6:
            x = plane_of(par, e - 3)
            return own[x, rows, :] if t < 8 else y[own_y + x]
        halo, corner, i = (a, ca, e - 7) if e > 6 else (b, cb, 2 - e)
        value = halo[i, rows, :] if t < 8 else corner[i]
        return value if e > 6 else value * inside

    return get


def stored(*held):
    def get(e, t):
        for ref, start, stop in held:
            if start <= e < stop:
                return ref[e - start, 8 * t : 8 * t + 8, :]

    return get


class Plane:
    def __init__(self, get, e):
        self.get, self.e = get, e
        self.sub = iota((8, 1024), 0)
        self.kept = {}

    def turned(self, t, by, keep):
        found = self.kept.pop((t, by), None)
        if found is None:
            found = pltpu.roll(self.get(self.e, t), by, 0)
            if keep:
                self.kept[t, by] = found
        return found

    def views(self, t):
        get, e = self.get, self.e
        c = get(e, t)
        ym = jnp.where(self.sub == 0, self.turned((t + 8) % 9, 1, False), self.turned(t, 1, True))
        yp = jnp.where(self.sub == 7, self.turned((t + 1) % 9, 7, t < 8), self.turned(t, 7, False))
        return c, get(e - 1, t), get(e + 1, t), ym, yp, pltpu.roll(c, 1, 1), pltpu.roll(c, 1023, 1)


def inverse(x):
    rec = pl.reciprocal(x, approx=True)
    return rec * (2.0 - x * rec)


def couplings(plane, t):
    lane = iota((8, 1024), 1)
    c, xm, xp, ym, yp, zm, zp = plane.views(t)
    first, last = lane == 0, lane == 1023
    c = 0.25 * c
    xm, xp, ym, yp = (c + 0.25 * other for other in (xm, xp, ym, yp))
    zm = c + 0.25 * jnp.where(first, 0.0, zm)
    zp = c + 0.25 * jnp.where(last, 0.0, zp)
    inv = inverse(1.0 + (((xm + xp) + (ym + yp)) + (zm + zp)))
    return (xm, xp, ym, yp, jnp.where(first, 0.0, zm), jnp.where(last, 0.0, zp)), inv


def weighted(fs, views):
    t = [f * v for f, v in zip(fs, views)]
    return ((t[0] + t[1]) + (t[2] + t[3])) + (t[4] + t[5])


def prepare_kernel(p_ref, c_ref, a_ref, b_ref, y_ref, s_one, n_one, s_two, n_two, w_ref, k_ref):
    par, has_b, mine, v = place()
    inside = jnp.where(has_b, 1.0, 0.0)
    conduct = reader(par, inside, c_ref, a_ref, b_ref, y_ref)
    own = reader(par, inside, p_ref, a_ref.at[3:4], b_ref.at[3:4], y_ref, own_y=4)
    for e in range(3, 7):
        x = plane_of(par, e - 3)
        s_ref, n_ref = (s_one, n_one) if e < 5 else (s_two, n_two)
        at = (e - 3) % 2
        pc, pp = Plane(conduct, e), Plane(own, e)
        for t in range(8):
            rows = slice(8 * t, 8 * t + 8)
            fs, inv = couplings(pc, t)
            p, *views = pp.views(t)
            w_ref[x, rows, :] = (p + weighted(fs, views) - 0.5 * s_ref[at, rows, :]) * inv - p
            k_ref[x, rows, :] = (-0.5 * inv) * n_ref[at, rows, :]


def gap_kernel(table_ref, ta_ref, tb_ref, part_ref, cond_ref, ion_ref, act_ref, w_ref, k_ref,
               u_ref, a_ref, b_ref, up_ref, down_ref, mem_ref, spread):
    par, has_b, mine, v = place()
    part = part_ref[...]
    brick = part >> 6
    bx, by = brick >> 2, brick & 3
    side = jnp.where(bx == v, 0, jnp.where(bx == (v ^ 1), 1, 2))
    row = side * 4 + ((mine - by) & 3)
    lane = (part & 63) * 2
    tables = (table_ref[...], ta_ref[2, :, 0:128], tb_ref[2, :, 0:128])
    other = jnp.zeros((8, 128), F32)
    for r in range(12):
        line = jnp.broadcast_to(tables[r // 4][r % 4 : r % 4 + 1], (8, 128))
        other = jnp.where(row == r, jnp.take_along_axis(line, lane, axis=1, mode="promise_in_bounds"), other)
    own = tables[0][0:1]
    current = jnp.sum(cond_ref[...] * (own - other), axis=0, keepdims=True)
    act = act_ref[...]
    count = pair_sum(jnp.sum(jnp.transpose(act), axis=0, keepdims=True))
    g = current / jnp.maximum(count, 1.0)
    g8 = jnp.broadcast_to(g, (8, 128))
    mem_ref[...] = ion_ref[...] + act * jnp.transpose(jnp.broadcast_to(g, (128, 128)))
    for half in range(2):
        at = 64 * half + 2 * (iota((8, 128), 1) // 4)
        wide = jnp.take_along_axis(g8, at, axis=1, mode="promise_in_bounds")[0:1]
        spread[128 * half : 128 * half + 128, :] = jnp.transpose(jnp.broadcast_to(wide, (128, 128)))
    for j in range(4):
        x = plane_of(par, j)
        for t in range(8):
            rows = slice(8 * t, 8 * t + 8)
            gt = jnp.tile(spread[pl.ds(pl.multiple_of(x * 64 + 8 * t, 8), 8), :], (1, 8))
            u = w_ref[x, rows, :] + k_ref[x, rows, :] * gt
            u_ref[x, rows, :] = u
            if t == 0:
                down_ref[x] = u
            if t == 7:
                up_ref[x] = u
            if j < 3:
                b_ref[j, rows, :] = u
            if j > 0:
                a_ref[3 - j, rows, :] = u


def operator_kernel(c_ref, a_ref, b_ref, y_ref, ca_ref, cb_ref, after, fx, fym, fyp, fzm, fzp, inv_ref):
    par, has_b, mine, v = place()
    inside = jnp.where(has_b, 1.0, 0.0)
    conduct = reader(par, inside, c_ref, a_ref, b_ref, y_ref, ca_ref, cb_ref)
    sub = iota((8, 1024), 0)
    bottom = (sub < 3) & (mine != 3)
    top = (sub >= 5) & (mine != 0)
    keep = jnp.where(bottom | top, 1.0, 0.0)
    for e in range(1, 9):
        plane = Plane(conduct, e)
        for t in range(8 if e in (1, 8) else 9):
            rows = slice(8 * t, 8 * t + 8)
            fs, inv = couplings(plane, t)
            if e < 3:
                inv = inv * inside
            inv_ref[e - 1, rows, :] = inv * keep if t == 8 else inv
            if e == 1 or (e == 2 and t == 8):
                fx[e - 1, rows, :] = fs[0]
            fx[e, rows, :] = fs[1]
            for ref, f in zip((fym, fyp, fzm, fzp), fs[2:]):
                ref[e - 1, rows, :] = f


def coupled(coef, get, plane, t):
    fx, fym, fyp, fzm, fzp, inv = coef
    e = plane.e
    rows = slice(8 * t, 8 * t + 8)
    fs = [fx[e - 1, rows, :], fx[e, rows, :]] + [f[e - 1, rows, :] for f in (fym, fyp, fzm, fzp)]
    u, *views = plane.views(t)
    return u, inv[e - 1, rows, :] * weighted(fs, views)


def put(held, e, t, value):
    for ref, start, stop in held:
        if start <= e < stop:
            ref[e - start, 8 * t : 8 * t + 8, :] = value


def step_one(coef, u0, e, r_held, u1_held):
    a, b = sweep_factors()[0]
    plane = Plane(u0, e)
    for t in range(8 if e in (1, 8) else 9):
        u, res = coupled(coef, u0, plane, t)
        put(r_held, e, t, res)
        put(u1_held, e, t, a * u + b * res)


def step_two(coef, u1, r, e, r_held, u2_held):
    a, b = sweep_factors()[1]
    plane = Plane(u1, e)
    for t in range(8 if e in (2, 7) else 9):
        u, more = coupled(coef, u1, plane, t)
        res = (r(e, t) - u) + more
        put(r_held, e, t, res)
        put(u2_held, e, t, a * u + b * res)


def step_three(coef, p_ref, u0, u1, u2, r, e, x, out_ref, at):
    a, b = sweep_factors()[2]
    plane = Plane(u2, e)
    for t in range(8):
        rows = slice(8 * t, 8 * t + 8)
        u, more = coupled(coef, u2, plane, t)
        res = (r(e, t) - u) + more
        before = (p_ref[x, rows, :] + u0(e, t)) + (u1(e, t) + u)
        out_ref[at, rows, :] = before + (a * u + b * res)


def near_kernel(p_ref, fx, fym, fyp, fzm, fzp, inv, u_ref, a_ref, y_ref, ca_ref,
                u1_out, r_out, u2_out, done_ref, u1_far, r_far, u2_far):
    par, has_b, mine, v = place()
    inside = jnp.where(has_b, 1.0, 0.0)
    coef = (fx, fym, fyp, fzm, fzp, inv)
    u0 = reader(par, inside, u_ref, a_ref, None, y_ref, ca_ref)
    u1_held = ((u1_out, 4, 6), (u1_far, 6, 9))
    r1_held = ((r_out, 4, 5), (r_far, 5, 8))
    r2_held = ((r_out.at[1:2], 5, 6), (r_far.at[1:2], 6, 7))
    u2_held = ((u2_out, 5, 7), (u2_far, 7, 8))
    for e in (8, 7, 6, 5, 4):
        step_one(coef, u0, e, r1_held, u1_held)
    for e in (7, 6, 5):
        step_two(coef, stored(*u1_held), stored(*r1_held), e, r2_held, u2_held)
    step_three(coef, p_ref, u0, stored(*u1_held), stored(*u2_held), stored(*r2_held), 6, plane_of(par, 3), done_ref, 0)


def far_kernel(p_ref, fx, fym, fyp, fzm, fzp, inv, u_ref, b_ref, y_ref, cb_ref, u1_in, r_in, u2_in, done_ref,
               out_hbm, u1_far, r_far, u2_far, out_ref, sem):
    par, has_b, mine, v = place()
    inside = jnp.where(has_b, 1.0, 0.0)
    coef = (fx, fym, fyp, fzm, fzp, inv)
    u0 = reader(par, inside, u_ref, None, b_ref, y_ref, None, cb_ref)
    u1_new = ((u1_far, 1, 4),)
    u1 = stored(*u1_new, (u1_in, 4, 6))
    r1_new = ((r_far, 2, 4),)
    r1 = stored(*r1_new, (r_in, 4, 5))
    r2_new = ((r_far.at[2:4], 3, 5),)
    r2 = stored(*r2_new, (r_in.at[1:2], 5, 6))
    u2_new = ((u2_far, 2, 5),)
    u2 = stored(*u2_new, (u2_in, 5, 7))
    sends = begin([(done_ref.at[0], out_hbm.at[plane_of(par, 3)])], sem, 3)
    for e in (1, 2, 3):
        step_one(coef, u0, e, r1_new, u1_new)
    for e in (2, 3, 4):
        step_two(coef, u1, r1, e, r2_new, u2_new)
    for e in (3, 4, 5):
        x = plane_of(par, e - 3)
        step_three(coef, p_ref, u0, u1, u2, r2, e, x, out_ref, e - 3)
        sends += begin([(out_ref.at[e - 3], out_hbm.at[x])], sem, e - 3)
    for send in sends:
        send.wait()


def near(*dims, kind=F32):
    return pltpu.VMEM(dims, kind)


def shape(*dims, kind=F32):
    return jax.ShapeDtypeStruct(dims, kind)


def per_device(potential, conductivity, ion_states, rate_scale, rate_slope, type_cond, reversal,
               facet_counts, intra_voxel, extra_voxel, cell_type, gap_partner, gap_cond):
    nv = lax.axis_size("vol")
    swap_a = [pair for i in range(0, nv, 2) for pair in ((i, i + 1), (i + 1, i))]
    swap_b = [pair for i in range(1, nv - 1, 2) for pair in ((i, i + 1), (i + 1, i))] + [(0, 0), (nv - 1, nv - 1)]
    on_mem = lambda x, pairs: lax.ppermute(x, "mem", pairs)
    ring = lambda d: [(i, (i + d) % 4) for i in range(4)]
    to_a = functools.partial(lax.ppermute, axis_name="vol", perm=swap_a)
    to_b = functools.partial(lax.ppermute, axis_name="vol", perm=swap_b)

    intra = intra_voxel.reshape(128, 128)
    extra = extra_voxel.reshape(128, 128)

    states_near, volt, cells, act, part_lane, cond_lane, send_a, send_b, send_up, send_down = pl.pallas_call(
        gather_kernel,
        out_shape=(near(40, 16384), near(128, 128), near(1, 128), near(128, 128),
                   near(8, 128, kind=jnp.int32), near(8, 128),
                   near(4, 64, 1024), near(4, 64, 1024), near(9, 8, 1024), near(9, 8, 1024)),
        in_specs=[SM] + [ANY] * 7,
        out_specs=(ANY,) * 10,
        scratch_shapes=[pltpu.VMEM((4, 64, 1024), F32), pltpu.VMEM((4, 64, 1024), F32),
                        pltpu.VMEM((128, 128), jnp.int32), pltpu.VMEM((128, 128), jnp.int32),
                        pltpu.VMEM((8, 64), jnp.int32), pltpu.VMEM((8, 64), F32), pltpu.VMEM((128, 128), F32),
                        pltpu.VMEM((1, 128), F32), pltpu.VMEM((128, 128), F32), pltpu.VMEM((8, 128), jnp.int32),
                        pltpu.VMEM((8, 128), F32), pltpu.VMEM((8, 1024), F32), pltpu.SemaphoreType.DMA((35,))],
        compiler_params=grant(54),
        cost_estimate=pl.CostEstimate(flops=4000000, bytes_accessed=5000000, transcendentals=0),
        name="voltages",
    )(facet_counts, potential, conductivity, intra, extra, gap_partner.T, gap_cond.T, ion_states)

    below, above, far = on_mem(send_up, ring(1)), on_mem(send_down, ring(3)), on_mem(cells, ring(2))
    early_b, early_a = to_b(send_b), to_a(send_a)

    states_next, ion = pl.pallas_call(
        ionic_kernel,
        out_shape=(shape(40, 16384), near(128, 128)),
        in_specs=[SM, SM] + [VM] * 7,
        out_specs=(ANY, VM),
        scratch_shapes=[pltpu.VMEM((40, 16384), F32), pltpu.VMEM((128, 128), F32),
                        pltpu.VMEM((10, 40, 128), F32), pltpu.SemaphoreType.DMA((CHUNKS,))],
        compiler_params=pltpu.CompilerParams(vmem_limit_bytes=ROOM),
        cost_estimate=pl.CostEstimate(flops=16000000, bytes_accessed=5300000, transcendentals=2600000),
        name="ionic",
    )(facet_counts, cell_type, volt, act, rate_scale, rate_slope, type_cond, reversal.reshape(1, 40), states_near)

    def scatter(first, after):
        return pl.pallas_call(
            functools.partial(scatter_kernel, first),
            out_shape=(near(2, 64, 1024), near(2, 64, 1024)),
            in_specs=[VM] * 4 + [ANY],
            out_specs=(VM, VM),
            compiler_params=grant(12),
            cost_estimate=pl.CostEstimate(flops=400000000, bytes_accessed=1200000, transcendentals=0),
            name="scatter",
        )(ion, act, intra, extra, after)

    half_one = scatter(0, volt)

    y_early, table, more_a, more_b = pl.pallas_call(
        early_edge_kernel,
        out_shape=(shape(8, 8, 1024), shape(8, 128), shape(3, 8, 1024), shape(3, 8, 1024)),
        in_specs=[VM] * 4 + [ANY],
        out_specs=(VM,) * 4,
        compiler_params=grant(6),
        cost_estimate=pl.CostEstimate(flops=300000, bytes_accessed=1000000, transcendentals=0),
        name="early_edges",
    )(below, above, far, cells, half_one[0])
    more_b, more_a = to_b(more_b), to_a(more_a)

    half_two = scatter(2, table)

    w, k = pl.pallas_call(
        prepare_kernel,
        out_shape=(shape(4, 64, 1024), shape(4, 64, 1024)),
        in_specs=[VM] * 9,
        out_specs=(VM, VM),
        compiler_params=grant(20),
        cost_estimate=pl.CostEstimate(flops=16000000, bytes_accessed=8000000, transcendentals=0),
        name="prepare",
    )(potential, conductivity, early_a, early_b, y_early, *half_one, *half_two)

    u, u_a, u_b, u_up, u_down, membrane = pl.pallas_call(
        gap_kernel,
        out_shape=(shape(4, 64, 1024), shape(3, 64, 1024), shape(3, 64, 1024), shape(4, 8, 1024),
                   shape(4, 8, 1024), shape(128, 128)),
        in_specs=[VM] * 9,
        out_specs=(VM,) * 6,
        scratch_shapes=[pltpu.VMEM((256, 128), F32)],
        compiler_params=grant(12),
        cost_estimate=pl.CostEstimate(flops=1000000, bytes_accessed=5000000, transcendentals=0),
        name="gap",
    )(table, more_a, more_b, part_lane, cond_lane, ion, act, w, k)

    late_b = to_b(u_b)
    low_rows, high_rows = on_mem(u_up, ring(1)), on_mem(u_down, ring(3))
    late_a = to_a(u_a)

    big = lambda n: pltpu.VMEM((n, 72, 1024), F32)
    operator = pl.pallas_call(
        operator_kernel,
        out_shape=(shape(9, 72, 1024),) + (shape(8, 72, 1024),) * 5,
        in_specs=[VM] * 6 + [ANY],
        out_specs=(VM,) * 6,
        compiler_params=grant(22),
        cost_estimate=pl.CostEstimate(flops=16000000, bytes_accessed=17000000, transcendentals=0),
        name="operator",
    )(conductivity, early_a, early_b, y_early, more_a, more_b, u_up)

    y_late, corner_a, corner_b = pl.pallas_call(
        late_edge_kernel,
        out_shape=(shape(4, 8, 1024), shape(2, 8, 1024), shape(2, 8, 1024)),
        in_specs=[VM, VM, ANY],
        out_specs=(VM,) * 3,
        compiler_params=grant(4),
        cost_estimate=pl.CostEstimate(flops=100000, bytes_accessed=500000, transcendentals=0),
        name="late_edges",
    )(low_rows, high_rows, operator[-1])
    corner_b, corner_a = to_b(corner_b), to_a(corner_a)

    u1, r, u2, done = pl.pallas_call(
        near_kernel,
        out_shape=(shape(2, 72, 1024), shape(2, 72, 1024), shape(2, 72, 1024), shape(1, 64, 1024)),
        in_specs=[VM] * 11,
        out_specs=(VM,) * 4,
        scratch_shapes=[big(3), big(3), big(1)],
        compiler_params=grant(30),
        cost_estimate=pl.CostEstimate(flops=25000000, bytes_accessed=10000000, transcendentals=0),
        name="near",
    )(potential, *operator, u, late_a, y_late, corner_a)

    potential_next = pl.pallas_call(
        far_kernel,
        out_shape=shape(4, 64, 1024),
        in_specs=[VM] * 15,
        out_specs=ANY,
        scratch_shapes=[big(3), big(4), big(3), pltpu.VMEM((3, 64, 1024), F32), pltpu.SemaphoreType.DMA((4,))],
        compiler_params=grant(30),
        cost_estimate=pl.CostEstimate(flops=25000000, bytes_accessed=10000000, transcendentals=0),
        name="far",
    )(potential, *operator, u, late_b, y_late, corner_b, u1, r, u2, done)
    return potential_next, states_next, membrane.reshape(16384)


def solution(mesh):
    in_specs = (
        P("vol", "mem", None), P("vol", "mem", None), P(None, ("vol", "mem")),
        P(), P(), P(), P(),
        P(("vol", "mem")), P(("vol", "mem")), P(("vol", "mem")), P(("vol", "mem")),
        P(("vol", "mem"), None), P(("vol", "mem"), None),
    )
    out_specs = (P("vol", "mem", None), P(None, ("vol", "mem")), P(("vol", "mem")))
    return jax.shard_map(per_device, mesh=mesh, in_specs=in_specs, out_specs=out_specs, check_vma=False)
```
